32 devices in a mesh: rep: 4 (over y, core), fsdp: 8 (over z, x).
Axes of the slice: x: 2, y: 2, z: 4, core: 2. Of those that a mesh axis runs over, the one named last changes fastest.
Arguments:
- latents: bfloat16 [32, 1024, 1024], P(('rep', 'fsdp')), may hold values from -6 to 6
- conditions: bfloat16 [32, 1024], P('rep'), may hold values from -6 to 6
- modulator: bfloat16 [1024, 6144], P('fsdp'), may hold values from -0.1875 to 0.1875
- modulbias: bfloat16 [6144], P('fsdp'), may hold values from -4 to 4
- projector: bfloat16 [1024, 3072], P('fsdp'), may hold values from -0.1875 to 0.1875
- querybias: bfloat16 [1024], P('fsdp'), may hold values from -6 to 6
- valuebias: bfloat16 [1024], P('fsdp'), may hold values from -0.4375 to 0.4375
- outweight: bfloat16 [1024, 1024], P('fsdp'), may hold values from -3 to 3
- outbiases: bfloat16 [1024], P('fsdp'), may hold values from -4 to 4
- expander: bfloat16 [1024, 4096], P('fsdp'), may hold values from -0.1875 to 0.1875
- expandbias: bfloat16 [4096], P('fsdp'), may hold values from -4 to 4
- shrinker: bfloat16 [4096, 1024], P('fsdp'), may hold values from -0.09375 to 0.09375
- shrinkbias: bfloat16 [1024], P('fsdp'), may hold values from -4 to 4
- upstream: bfloat16 [32, 1024, 1024], P(('rep', 'fsdp')), may hold values from -6 to 6
Outputs:
- layer_out: float32 [32, 1024, 1024], P(('rep', 'fsdp'))
- latents_grad: float32 [32, 1024, 1024], P(('rep', 'fsdp'))
- conditions_grad: float32 [32, 1024], P('rep', 'fsdp')
- modulator_grad: float32 [1024, 6144], P('fsdp')
- modulbias_grad: float32 [6144], P('fsdp')
- projector_grad: float32 [1024, 3072], P('fsdp')
- querybias_grad: float32 [1024], P('fsdp')
- valuebias_grad: float32 [1024], P('fsdp')
- outweight_grad: float32 [1024, 1024], P('fsdp')
- outbiases_grad: float32 [1024], P('fsdp')
- expander_grad: float32 [1024, 4096], P('fsdp')
- expandbias_grad: float32 [4096], P('fsdp')
- shrinker_grad: float32 [4096, 1024], P('fsdp')
- shrinkbias_grad: float32 [1024], P('fsdp')
The draws below stay inside these ranges and needn't reach their ends.
All inputs are finite; a program needn't handle non-finite values.
Results may differ from the reference program's by a relative error of at most 0.015.
The reference program's roundings to bfloat16 on the way count: a program that leaves them out, or rounds other values in their place, can miss the bound.
Values may be sent and summed in bfloat16 or wider, within the bound.
No kernel may reach another device: no remote copies, remote signals or barrier semaphores. Data moves between devices by JAX's collectives and lax.ppermute only.
A program may use at most 256 MiB of HBM per device.

```python
import jax
import jax.numpy as jnp
from jax import lax

D = 1024
HEADS = 16
HEAD_DIM = 64
FF = 4096
LEN = 1024
BATCH = 32


def level_of(own_key, dims, cuts, least, top_value):
    def one(position, parts):
        draws = jax.random.uniform(jax.random.fold_in(jax.random.fold_in(own_key, 6), position), (parts,), jnp.float32, least / len(cuts), top_value / len(cuts))
        return jnp.repeat(jnp.exp(draws), dims[position] // parts).reshape((-1,) + (1,) * (len(dims) - position - 1))

    loudness = one(*cuts[0])
    for cut in cuts[1:]:
        loudness = loudness * one(*cut)
    return loudness


def gaussian(own_key, extent, scale, most, shards=(), kind=jnp.bfloat16):
    values = scale * jax.random.normal(own_key, extent, jnp.float32)
    if shards:
        values = values * level_of(own_key, extent, shards, -0.22, 0.18)
    return jnp.clip(values, -most, most).astype(kind)


def setup_inputs(seed: int = 0) -> dict:
    key_list = jax.random.split(jax.random.key(seed), 15)
    latents = gaussian(key_list[0], (BATCH, LEN, D), 1.0, 6.0, ((0, 32),))
    conditions = gaussian(key_list[1], (BATCH, D), 1.0, 6.0, ((0, 4),))
    modulator = gaussian(key_list[2], (D, 6 * D), D ** -0.5, 0.1875, ((0, 8),))
    modulbias = gaussian(key_list[3], (6 * D,), 0.3, 4.0, ((0, 8),))
    projector = gaussian(key_list[4], (D, 3 * D), D ** -0.5, 0.1875, ((0, 8),))
    querybias = gaussian(key_list[5], (D,), 0.5, 6.0, ((0, 8),))
    valuebias = gaussian(key_list[6], (D,), 0.03, 0.4375, ((0, 8),))
    outweight = gaussian(key_list[7], (D, D), (max(4, D * LEN // 262144)) ** -0.5, 3.0, ((0, 8),))
    outbiases = gaussian(key_list[8], (D,), 0.3, 4.0, ((0, 8),))
    expander = gaussian(key_list[9], (D, FF), D ** -0.5, 0.1875, ((0, 8),))
    expandbias = gaussian(key_list[10], (FF,), 0.3, 4.0, ((0, 8),))
    shrinker = gaussian(key_list[11], (FF, D), FF ** -0.5, 0.09375, ((0, 8),))
    shrinkbias = gaussian(key_list[12], (D,), 0.3, 4.0, ((0, 8),))
    upstream = gaussian(key_list[13], (BATCH, LEN, D), 1.0, 6.0, ((0, 32),))
    return {"latents": latents, "conditions": conditions, "modulator": modulator, "modulbias": modulbias, "projector": projector, "querybias": querybias, "valuebias": valuebias, "outweight": outweight, "outbiases": outbiases, "expander": expander, "expandbias": expandbias, "shrinker": shrinker, "shrinkbias": shrinkbias, "upstream": upstream}


EPS_NORM = 1e-06

@jax.custom_vjp
def low(v):
    return lax.optimization_barrier(v.astype(jnp.bfloat16)).astype(jnp.float32)

@jax.custom_vjp
def low_back(v):
    return v

def low_keep(v):
    return (low(v), None)

def low_pass(kept, grad):
    return (grad,)

def back_keep(v):
    return (v, None)

def back_low(kept, grad):
    return (low(grad),)
low.defvjp(low_keep, low_pass)
low_back.defvjp(back_keep, back_low)

def matmul(left_side, right_side):
    return jnp.dot(left_side, right_side, precision=lax.Precision.HIGHEST, preferred_element_type=jnp.float32)

def normalize(values):
    average = lax.optimization_barrier(jnp.mean(values, axis=-1, keepdims=True))
    centred = values - average
    variance = lax.optimization_barrier(jnp.mean(centred * centred, axis=-1, keepdims=True))
    return centred * lax.rsqrt(variance + EPS_NORM)

def one_latent(params, latent, modrow):
    projector, querybias, valuebias, outweight, outbiases, expander, expandbias, shrinker, shrinkbias = params
    scale_dot = HEAD_DIM ** (-0.5)
    norm_a = low(normalize(latent) * (1.0 + modrow[1]) + modrow[0])
    projected = matmul(norm_a, projector)
    queries = low(low_back(projected[:, :D] + querybias))
    key_rows = low(low_back(projected[:, D:2 * D]))
    values = low(low_back(projected[:, 2 * D:] + valuebias))
    query_heads = queries.reshape(LEN, HEADS, HEAD_DIM)
    key_heads = key_rows.reshape(LEN, HEADS, HEAD_DIM)
    value_heads = values.reshape(LEN, HEADS, HEAD_DIM)
    scores = low_back(jnp.einsum('qhd,khd->hqk', query_heads, key_heads, precision=lax.Precision.HIGHEST) * scale_dot)
    attn_probs = low(jax.nn.softmax(scores, axis=-1))
    attended = jnp.einsum('hqk,khd->qhd', attn_probs, value_heads, precision=lax.Precision.HIGHEST).reshape(LEN, D)
    attended = low(low_back(attended))
    branch_a = low_back(matmul(attended, outweight) + outbiases)
    middle = latent + modrow[2] * branch_a
    norm_m = low(normalize(middle) * (1.0 + modrow[4]) + modrow[3])
    pre_act = low_back(matmul(norm_m, expander) + expandbias)
    hidden = low(jax.nn.gelu(pre_act, approximate=True))
    branch_m = low_back(matmul(hidden, shrinker) + shrinkbias)
    return middle + modrow[5] * branch_m

def forward(latents, conditions, modulator, modulbias, *params):
    cond_act = low(jax.nn.silu(conditions))
    modvals = low_back(matmul(cond_act, modulator) + modulbias).reshape(BATCH, 6, D)
    layer_fn = jax.checkpoint(one_latent)

    def advance(carried, inputs):
        latent, modrow = inputs
        return (carried, layer_fn(params, latent, modrow))
    _, outputs = lax.scan(advance, jnp.zeros((), jnp.float32), (latents, modvals))
    return outputs

def reference(latents, conditions, modulator, modulbias, projector, querybias, valuebias, outweight, outbiases, expander, expandbias, shrinker, shrinkbias, upstream):
    arrays = [member.astype(jnp.float32) for member in (latents, conditions, modulator, modulbias, projector, querybias, valuebias, outweight, outbiases, expander, expandbias, shrinker, shrinkbias)]
    outputs, pullback = jax.vjp(forward, *arrays)
    gradients = pullback(upstream.astype(jnp.float32))
    return (outputs, gradients[0], gradients[1], gradients[2], gradients[3], gradients[4], gradients[5], gradients[6], gradients[7], gradients[8], gradients[9], gradients[10], gradients[11], gradients[12])
```

```python
from functools import partial

import jax
import jax.numpy as jnp
from jax import lax
from jax.sharding import PartitionSpec as P

HEADS = 16
HEAD_DIM = 64


EPS_NORM = 1e-06


def normalize(values):
    average = jnp.mean(values, axis=-1, keepdims=True)
    centred = values - average
    variance = jnp.mean(centred * centred, axis=-1, keepdims=True)
    return centred * lax.rsqrt(variance + EPS_NORM)


def modulate(values, shifts, scales):
    return normalize(values) * (1.0 + scales[:, None, :]) + shifts[:, None, :]


def split_pairs(stacked):
    blocks, length, feature = stacked.shape
    grouped = stacked.reshape(blocks, length, HEADS // 2, 2 * HEAD_DIM).transpose(0, 2, 1, 3)
    return grouped.reshape(blocks * (HEADS // 2), length, 2 * HEAD_DIM)


def join_pairs(paired, blocks):
    length = paired.shape[1]
    grouped = paired.reshape(blocks, HEADS // 2, length, 2 * HEAD_DIM).transpose(0, 2, 1, 3)
    return grouped.reshape(blocks, length, HEADS * HEAD_DIM)


def pair_scores(query_pair, key_pair):
    length = query_pair.shape[0]
    query_heads = query_pair.reshape(length, 2, HEAD_DIM)
    key_heads = key_pair.reshape(length, 2, HEAD_DIM)
    scores = jnp.einsum("qhd,khd->hqk", query_heads, key_heads, preferred_element_type=jnp.float32)
    return (scores * HEAD_DIM ** (-0.5), query_heads, key_heads)


def pair_forward(operands):
    query_pair, key_pair, value_pair = operands
    length = query_pair.shape[0]
    scores, _, _ = pair_scores(query_pair, key_pair)
    value_heads = value_pair.reshape(length, 2, HEAD_DIM)
    top_score = jnp.max(scores, axis=-1, keepdims=True)
    exp_terms = jnp.exp(scores - top_score)
    denominator = jnp.sum(exp_terms, axis=-1, keepdims=True)
    attn_probs = (exp_terms / denominator).astype(jnp.bfloat16)
    attended = jnp.einsum(
        "hqk,khd->qhd", attn_probs, value_heads, preferred_element_type=jnp.float32
    )
    log_total = (top_score + jnp.log(denominator))[:, :, 0]
    return (attended.reshape(length, 2 * HEAD_DIM).astype(jnp.bfloat16), log_total)


def pair_backward(operands):
    query_pair, key_pair, value_pair, grad_pair, log_total = operands
    length = query_pair.shape[0]
    scores, query_heads, key_heads = pair_scores(query_pair, key_pair)
    value_heads = value_pair.reshape(length, 2, HEAD_DIM)
    grad_heads = grad_pair.reshape(length, 2, HEAD_DIM)
    probs_full = jnp.exp(scores - log_total[:, :, None])
    probs_low = probs_full.astype(jnp.bfloat16)
    d_value = jnp.einsum("hqk,qhd->khd", probs_low, grad_heads, preferred_element_type=jnp.float32)
    d_probs = jnp.einsum(
        "qhd,khd->hqk", grad_heads, value_heads, preferred_element_type=jnp.float32
    )
    row_sum = jnp.sum(probs_full * d_probs, axis=-1, keepdims=True)
    d_scores = (probs_full * (d_probs - row_sum)).astype(jnp.bfloat16)
    d_query = jnp.einsum(
        "hqk,khd->qhd", d_scores, key_heads, preferred_element_type=jnp.float32
    ) * HEAD_DIM ** (-0.5)
    d_key = jnp.einsum(
        "hqk,qhd->khd", d_scores, query_heads, preferred_element_type=jnp.float32
    ) * HEAD_DIM ** (-0.5)
    return (
        d_query.reshape(length, 2 * HEAD_DIM).astype(jnp.bfloat16),
        d_key.reshape(length, 2 * HEAD_DIM).astype(jnp.bfloat16),
        d_value.reshape(length, 2 * HEAD_DIM).astype(jnp.bfloat16),
    )


def gather_rows(weight):
    part = weight.shape[0] // lax.axis_size("rep")
    own = lax.dynamic_slice_in_dim(weight, lax.axis_index("rep") * part, part, 0)
    return lax.all_gather(own, ("fsdp", "rep"), axis=0, tiled=True)


def scatter_rows(grad):
    own = lax.psum_scatter(
        grad.astype(jnp.bfloat16), ("fsdp", "rep"), scatter_dimension=0, tiled=True
    )
    return lax.all_gather(own, "rep", axis=0, tiled=True).astype(jnp.float32)


def on_device(
    latents,
    conditions,
    modulator,
    modulbias,
    projector,
    querybias,
    valuebias,
    outweight,
    outbiases,
    expander,
    expandbias,
    shrinker,
    shrinkbias,
    upstream,
):
    seqs_dev, seq_len, feature = latents.shape
    token_count = seqs_dev * seq_len
    shard_id = lax.axis_index("fsdp")
    shards = lax.axis_size("fsdp")
    own_rows = modulator.shape[0]
    own_bias = modulbias.shape[0]
    cond_full = conditions.astype(jnp.float32)
    cond_slice = lax.dynamic_slice_in_dim(cond_full, shard_id * own_rows, own_rows, 1)
    cond_act = jax.nn.silu(cond_slice).astype(jnp.bfloat16)
    mod_term = jnp.dot(cond_act, modulator, preferred_element_type=jnp.float32)
    bias_parts = (modulbias, querybias, valuebias, outbiases, expandbias, shrinkbias)
    own_biases = jnp.concatenate([part.astype(jnp.float32) for part in bias_parts])
    mod_width = seqs_dev * 6 * feature
    sent = jnp.concatenate(
        [
            mod_term.reshape(shards, mod_width),
            jnp.broadcast_to(own_biases[None, :], (shards, own_biases.shape[0])),
        ],
        axis=1,
    )
    got = lax.all_to_all(sent, "fsdp", split_axis=0, concat_axis=0, tiled=True)
    full_biases = []
    start = mod_width
    for part in bias_parts:
        full_biases.append(got[:, start : start + part.shape[0]].reshape(-1))
        start += part.shape[0]
    full_modbias, b_query, b_value, b_out, b_expand, b_shrink = full_biases
    modvals = jnp.sum(got[:, :mod_width], axis=0).reshape(seqs_dev, 6, feature) + full_modbias.reshape(
        1, 6, feature
    )
    shift_a, scale_a, gate_a = (modvals[:, 0], modvals[:, 1], modvals[:, 2])
    shift_m, scale_m, gate_m = (modvals[:, 3], modvals[:, 4], modvals[:, 5])
    w_proj = gather_rows(projector)
    w_out = gather_rows(outweight)
    w_expand = gather_rows(expander)
    w_shrink = gather_rows(shrinker)
    resid_in = latents.astype(jnp.float32)
    norm_a = modulate(resid_in, shift_a, scale_a).astype(jnp.bfloat16).reshape(token_count, feature)
    projected = jnp.dot(norm_a, w_proj, preferred_element_type=jnp.float32)
    queries = (
        (projected[:, :feature] + b_query)
        .astype(jnp.bfloat16)
        .reshape(seqs_dev, seq_len, feature)
    )
    key_rows = (
        projected[:, feature : 2 * feature].astype(jnp.bfloat16).reshape(seqs_dev, seq_len, feature)
    )
    values = (
        (projected[:, 2 * feature :] + b_value)
        .astype(jnp.bfloat16)
        .reshape(seqs_dev, seq_len, feature)
    )
    paired_query = split_pairs(queries)
    paired_key = split_pairs(key_rows)
    paired_value = split_pairs(values)
    attended_pairs, log_totals = lax.map(pair_forward, (paired_query, paired_key, paired_value))
    attended = join_pairs(attended_pairs, seqs_dev).reshape(token_count, feature)
    branch_a = (
        jnp.dot(attended, w_out, preferred_element_type=jnp.float32) + b_out
    ).reshape(seqs_dev, seq_len, feature)
    middle = resid_in + gate_a[:, None, :] * branch_a
    norm_m = modulate(middle, shift_m, scale_m).astype(jnp.bfloat16).reshape(token_count, feature)
    pre_act = jnp.dot(norm_m, w_expand, preferred_element_type=jnp.float32) + b_expand
    gelu_fn = partial(jax.nn.gelu, approximate=True)
    hidden = gelu_fn(pre_act).astype(jnp.bfloat16)
    branch_m = (
        jnp.dot(hidden, w_shrink, preferred_element_type=jnp.float32) + b_shrink
    ).reshape(seqs_dev, seq_len, feature)
    layer_out = middle + gate_m[:, None, :] * branch_m
    grad_out = upstream.astype(jnp.float32)
    d_branch_m = (gate_m[:, None, :] * grad_out).astype(jnp.bfloat16).reshape(token_count, feature)
    d_gate_m = jnp.sum(grad_out * branch_m, axis=1)
    g_shrinkbias = jnp.sum(d_branch_m, axis=0, dtype=jnp.float32)
    g_shrinker = scatter_rows(
        jnp.einsum("nf,nd->fd", hidden, d_branch_m, preferred_element_type=jnp.float32)
    )
    d_hidden = jnp.einsum("nd,fd->nf", d_branch_m, w_shrink, preferred_element_type=jnp.float32)
    _, gelu_pull = jax.vjp(gelu_fn, pre_act)
    d_pre = gelu_pull(d_hidden)[0].astype(jnp.bfloat16)
    g_expandbias = jnp.sum(d_pre, axis=0, dtype=jnp.float32)
    g_expander = scatter_rows(
        jnp.einsum("nd,nf->df", norm_m, d_pre, preferred_element_type=jnp.float32)
    )
    d_norm_m = jnp.einsum(
        "nf,df->nd", d_pre, w_expand, preferred_element_type=jnp.float32
    ).reshape(seqs_dev, seq_len, feature)
    _, norm_pull_m = jax.vjp(modulate, middle, shift_m, scale_m)
    d_mid_norm, d_shift_m, d_scale_m = norm_pull_m(d_norm_m)
    d_middle = grad_out + d_mid_norm
    d_branch_a = (gate_a[:, None, :] * d_middle).astype(jnp.bfloat16).reshape(token_count, feature)
    d_gate_a = jnp.sum(d_middle * branch_a, axis=1)
    g_outbiases = jnp.sum(d_branch_a, axis=0, dtype=jnp.float32)
    g_outweight = scatter_rows(
        jnp.einsum("nd,ne->de", attended, d_branch_a, preferred_element_type=jnp.float32)
    )
    d_attended = (
        jnp.einsum("ne,de->nd", d_branch_a, w_out, preferred_element_type=jnp.float32)
        .astype(jnp.bfloat16)
        .reshape(seqs_dev, seq_len, feature)
    )
    pair_query, pair_key, pair_value = lax.map(
        pair_backward, (paired_query, paired_key, paired_value, split_pairs(d_attended), log_totals)
    )
    d_projected = jnp.concatenate(
        [
            join_pairs(pair_query, seqs_dev).reshape(token_count, feature),
            join_pairs(pair_key, seqs_dev).reshape(token_count, feature),
            join_pairs(pair_value, seqs_dev).reshape(token_count, feature),
        ],
        axis=1,
    )
    g_querybias = jnp.sum(d_projected[:, :feature], axis=0, dtype=jnp.float32)
    g_valuebias = jnp.sum(d_projected[:, 2 * feature :], axis=0, dtype=jnp.float32)
    g_projector = scatter_rows(
        jnp.einsum("nd,ne->de", norm_a, d_projected, preferred_element_type=jnp.float32)
    )
    d_norm_a = jnp.einsum(
        "ne,de->nd", d_projected, w_proj, preferred_element_type=jnp.float32
    ).reshape(seqs_dev, seq_len, feature)
    _, norm_pull_a = jax.vjp(modulate, resid_in, shift_a, scale_a)
    d_in_norm, d_shift_a, d_scale_a = norm_pull_a(d_norm_a)
    latents_grad = d_middle + d_in_norm
    mod_partial = jnp.stack(
        [d_shift_a, d_scale_a, d_gate_a, d_shift_m, d_scale_m, d_gate_m], axis=1
    ).reshape(seqs_dev, 6 * feature)
    bias_sums = (g_querybias, g_valuebias, g_outbiases, g_expandbias, g_shrinkbias)
    small = jnp.concatenate(
        [mod_partial.astype(jnp.bfloat16).reshape(-1), cond_act.reshape(-1)]
        + [part.astype(jnp.bfloat16) for part in bias_sums]
    )
    gathered = lax.all_gather(small, ("rep", "fsdp"), axis=0, tiled=False)
    devices = gathered.shape[0]
    reps = devices // shards
    d_mod = gathered[:, :mod_width].reshape(devices * seqs_dev, 6 * feature)
    group = shards * seqs_dev
    cond_size = cond_act.shape[0] * own_rows
    cond_all = gathered[:, mod_width : mod_width + cond_size].reshape(reps, shards, cond_size)
    cond_all = lax.dynamic_index_in_dim(cond_all, shard_id, 1, keepdims=False)
    cond_all = cond_all.reshape(reps * cond_act.shape[0], own_rows)
    start = mod_width + cond_size
    bias_grads = []
    for part in bias_sums:
        width = part.shape[0] // shards
        own = lax.dynamic_slice_in_dim(gathered, start + shard_id * width, width, 1)
        bias_grads.append(jnp.sum(own, axis=0, dtype=jnp.float32))
        start += part.shape[0]
    g_modbias = jnp.sum(
        lax.dynamic_slice_in_dim(d_mod, shard_id * own_bias, own_bias, 1), axis=0, dtype=jnp.float32
    )
    g_modulator = jnp.einsum("sr,sc->rc", cond_all, d_mod, preferred_element_type=jnp.float32)
    own_mod = lax.dynamic_slice_in_dim(d_mod, lax.axis_index("rep") * group, group, 0)
    d_cond_act = jnp.einsum("sc,rc->sr", own_mod, modulator, preferred_element_type=jnp.float32)
    _, silu_pull = jax.vjp(jax.nn.silu, cond_slice)
    conditions_grad = silu_pull(d_cond_act)[0]
    return (
        layer_out,
        latents_grad,
        conditions_grad,
        g_modulator,
        g_modbias,
        g_projector,
        bias_grads[0],
        bias_grads[1],
        g_outweight,
        bias_grads[2],
        g_expander,
        bias_grads[3],
        g_shrinker,
        bias_grads[4],
    )


def solution(mesh):
    return jax.shard_map(
        on_device,
        mesh=mesh,
        in_specs=(
            P(("rep", "fsdp"), None, None),
            P("rep", None),
            P("fsdp", None),
            P("fsdp"),
            P("fsdp", None),
            P("fsdp"),
            P("fsdp"),
            P("fsdp", None),
            P("fsdp"),
            P("fsdp", None),
            P("fsdp"),
            P("fsdp", None),
            P("fsdp"),
            P(("rep", "fsdp"), None, None),
        ),
        out_specs=(
            P(("rep", "fsdp"), None, None),
            P(("rep", "fsdp"), None, None),
            P("rep", "fsdp"),
            P("fsdp", None),
            P("fsdp"),
            P("fsdp", None),
            P("fsdp"),
            P("fsdp"),
            P("fsdp", None),
            P("fsdp"),
            P("fsdp", None),
            P("fsdp"),
            P("fsdp", None),
            P("fsdp"),
        ),
        check_vma=False,
    )
```

```python
from functools import partial

import jax
import jax.numpy as jnp
from jax import lax
from jax.experimental import pallas as pl
from jax.experimental.pallas import tpu as pltpu
from jax.sharding import PartitionSpec as P

HEADS = 16
HEAD_DIM = 64
PAIR = 2 * HEAD_DIM
CHUNK = 256
EPS_NORM = 1e-06
ROWS = 256
FF_BLOCK = 512
COL_BLOCK = 512
GELU_ROOT = 0.7978845608028654
GELU_CUBE = 0.044715


def dot_nn(left, right):
    return jnp.dot(left, right, preferred_element_type=jnp.float32)


def dot_nt(left, right):
    return lax.dot_general(left, right, (((1,), (1,)), ((), ())), preferred_element_type=jnp.float32)


def dot_tn(left, right):
    return lax.dot_general(left, right, (((0,), (0,)), ((), ())), preferred_element_type=jnp.float32)


def kernel_params(mebibytes):
    return pltpu.CompilerParams(vmem_limit_bytes=mebibytes * 2**20)


def cost(flops, moved, special=0):
    return pl.CostEstimate(flops=flops, bytes_accessed=moved, transcendentals=special)


def weight_spec(weight, first, width, order):
    if weight.ndim == 2:
        offset = first * weight.shape[0] // width
        return pl.BlockSpec((weight.shape[0], width), lambda *at: (0, offset + order(*at)))
    devices, _, rows, columns = weight.shape
    per = columns // width
    return pl.BlockSpec(
        (devices, 1, rows, width),
        lambda *at: (0, first + order(*at) // per, 0, order(*at) % per),
    )


def forward_dot_kernel(x_ref, w_ref, b_ref, out_ref):
    weight = w_ref[...].reshape(x_ref.shape[1], out_ref.shape[1])
    out_ref[...] = (dot_nn(x_ref[...], weight) + b_ref[...]).astype(out_ref.dtype)


def forward_dot(x, weight, first, bias, dtype, name):
    tokens, depth = x.shape
    columns = bias.shape[1]
    return pl.pallas_call(
        forward_dot_kernel,
        grid=(columns // COL_BLOCK,),
        in_specs=[
            pl.BlockSpec((tokens, depth), lambda i: (0, 0)),
            weight_spec(weight, first, COL_BLOCK, lambda i: i),
            pl.BlockSpec((1, COL_BLOCK), lambda i: (0, i)),
        ],
        out_specs=pl.BlockSpec((tokens, COL_BLOCK), lambda i: (0, i)),
        out_shape=jax.ShapeDtypeStruct((tokens, columns), dtype),
        compiler_params=kernel_params(40),
        cost_estimate=cost(2 * tokens * depth * columns, 4 * tokens * columns),
        name=name,
    )(x, weight, bias)


def backward_dot_kernel(dy_ref, w_ref, out_ref, sum_ref):
    step = pl.program_id(0)
    weight = w_ref[...].reshape(out_ref.shape[1], w_ref.shape[-1])
    part = dot_nt(dy_ref[0], weight)

    @pl.when(step == 0)
    def _():
        sum_ref[...] = part

    @pl.when(step > 0)
    def _():
        sum_ref[...] += part

    @pl.when(step == pl.num_programs(0) - 1)
    def _():
        out_ref[...] = sum_ref[...].astype(out_ref.dtype)


def backward_dot(dy, weight, first, dtype, name):
    groups, tokens, columns = dy.shape
    depth = columns
    per = columns // COL_BLOCK
    return pl.pallas_call(
        backward_dot_kernel,
        grid=(groups * per,),
        in_specs=[
            pl.BlockSpec((1, tokens, COL_BLOCK), lambda i: (i // per, 0, i % per)),
            weight_spec(weight, first, COL_BLOCK, lambda i: i),
        ],
        out_specs=pl.BlockSpec((tokens, depth), lambda i: (0, 0)),
        out_shape=jax.ShapeDtypeStruct((tokens, depth), dtype),
        scratch_shapes=[pltpu.VMEM((tokens, depth), jnp.float32)],
        compiler_params=kernel_params(40),
        cost_estimate=cost(2 * groups * tokens * depth * columns, 4 * tokens * columns),
        name=name,
    )(dy, weight)


def store_rows(total, own_core, own_slot, pieces, keep_ref, send_ref):
    rows = total.shape[0] // pieces
    low = total.astype(jnp.bfloat16).reshape(pieces // 2, 2, rows, total.shape[1])
    here = own_core == 0
    for slot in range(pieces // 2):
        first, second = low[slot, 0], low[slot, 1]
        place = pl.ds(pl.multiple_of((own_slot ^ slot) * rows, rows), rows)
        keep_ref[place, :] = jnp.where(here, first, second)
        send_ref[place, :] = jnp.where(here, second, first)


def grad_dot_kernel(pieces, own_ref, x_ref, dy_ref, keep_ref, send_ref):
    total = dot_tn(x_ref[...], dy_ref[0])
    store_rows(total, own_ref[0], own_ref[1], pieces, keep_ref, send_ref)


def grad_dot(own, x, dy, first, groups, pieces, name):
    tokens, depth = x.shape
    columns = dy.shape[2]
    per = columns // COL_BLOCK
    half = jax.ShapeDtypeStruct((depth // 2, groups * columns), jnp.bfloat16)
    block = pl.BlockSpec((depth // 2, COL_BLOCK), lambda i, own: (0, i))
    return pl.pallas_call(
        partial(grad_dot_kernel, pieces),
        grid_spec=pltpu.PrefetchScalarGridSpec(
            num_scalar_prefetch=1,
            grid=(groups * per,),
            in_specs=[
                pl.BlockSpec((tokens, depth), lambda i, own: (0, 0)),
                pl.BlockSpec((1, tokens, COL_BLOCK), lambda i, own: (first + i // per, 0, i % per)),
            ],
            out_specs=[block, block],
        ),
        out_shape=[half, half],
        compiler_params=kernel_params(40),
        cost_estimate=cost(2 * groups * tokens * depth * columns, 4 * tokens * columns),
        name=name,
    )(own, x, dy)


def feed_forward_kernel(
    depth_pieces,
    unit_pieces,
    own_ref,
    norm_ref,
    grad_ref,
    expand_ref,
    bias_ref,
    shrink_ref,
    branch_ref,
    d_norm_ref,
    keep_e_ref,
    send_e_ref,
    keep_s_ref,
    send_s_ref,
    d_bias_ref,
    norm_t,
    hidden,
    d_pre,
):
    tokens, depth = norm_ref.shape
    units = hidden.shape[1]
    step = pl.program_id(0)
    expand = expand_ref[...].reshape(depth, units)
    shrink = shrink_ref[...].reshape(units, depth)

    @pl.when(step == 0)
    def _():
        norm_t[...] = norm_ref[...].T
        branch_ref[...] = jnp.zeros_like(branch_ref)
        d_norm_ref[...] = jnp.zeros_like(d_norm_ref)

    bias_sum = jnp.zeros((1, units), jnp.float32)
    for start in range(0, tokens, ROWS):
        rows = slice(start, start + ROWS)
        pre = dot_nn(norm_ref[rows, :], expand) + bias_ref[...]
        square = pre * pre
        bend = jnp.tanh(GELU_ROOT * pre * (1.0 + GELU_CUBE * square))
        rise = 0.5 + 0.5 * bend
        unit = (pre * rise).astype(jnp.bfloat16)
        hidden[rows, :] = unit
        slope = rise + 0.5 * pre * (1.0 - bend * bend) * (
            GELU_ROOT + (3.0 * GELU_ROOT * GELU_CUBE) * square
        )
        branch_ref[rows, :] += dot_nn(unit, shrink)
        d_unit = dot_nt(grad_ref[rows, :], shrink)
        d_low = (d_unit * slope).astype(jnp.bfloat16)
        d_pre[rows, :] = d_low
        bias_sum = bias_sum + jnp.sum(d_low.astype(jnp.float32), axis=0, keepdims=True)
        d_norm_ref[rows, :] += dot_nt(d_low, expand)
    d_bias_ref[...] = bias_sum
    store_rows(
        dot_tn(hidden[...], grad_ref[...]), own_ref[0], own_ref[3], unit_pieces, keep_s_ref, send_s_ref
    )
    store_rows(
        dot_nn(norm_t[...], d_pre[...]), own_ref[0], own_ref[1], depth_pieces, keep_e_ref, send_e_ref
    )


def feed_forward(own, norm, grad, expand, bias, shrink, depth_pieces, unit_pieces):
    tokens, depth = norm.shape
    total = bias.shape[1]
    steps = total // FF_BLOCK
    whole = pl.BlockSpec((tokens, depth), lambda i, own: (0, 0))
    half_e = pl.BlockSpec((depth // 2, FF_BLOCK), lambda i, own: (0, i))
    half_s = pl.BlockSpec((FF_BLOCK // 2, depth), lambda i, own: (i ^ own[2], 0))
    line = pl.BlockSpec((1, FF_BLOCK), lambda i, own: (0, i))
    if shrink.ndim == 2:
        spec_e = weight_spec(expand, 0, FF_BLOCK, lambda i, own: i)
        spec_s = pl.BlockSpec((FF_BLOCK, depth), lambda i, own: (i, 0))
    else:
        devices, blocks, rows, columns = shrink.shape
        spec_e = weight_spec(expand, 4, FF_BLOCK, lambda i, own: i)
        spec_s = pl.BlockSpec((devices // steps, 4, rows, columns), lambda i, own: (i, 0, 0, 0))
    wide = jax.ShapeDtypeStruct((tokens, depth), jnp.float32)
    out_e = jax.ShapeDtypeStruct((depth // 2, total), jnp.bfloat16)
    out_s = jax.ShapeDtypeStruct((total // 2, depth), jnp.bfloat16)
    return pl.pallas_call(
        partial(feed_forward_kernel, depth_pieces, unit_pieces),
        grid_spec=pltpu.PrefetchScalarGridSpec(
            num_scalar_prefetch=1,
            grid=(steps,),
            in_specs=[whole, whole, spec_e, line, spec_s],
            out_specs=[whole, whole, half_e, half_e, half_s, half_s, line],
            scratch_shapes=[
                pltpu.VMEM((depth, tokens), jnp.bfloat16),
                pltpu.VMEM((tokens, FF_BLOCK), jnp.bfloat16),
                pltpu.VMEM((tokens, FF_BLOCK), jnp.bfloat16),
            ],
        ),
        out_shape=[
            wide,
            wide,
            out_e,
            out_e,
            out_s,
            out_s,
            jax.ShapeDtypeStruct((1, total), jnp.float32),
        ],
        compiler_params=kernel_params(56),
        cost_estimate=cost(12 * tokens * depth * total, 64 * 2**20, tokens * total),
        name="feed_forward",
    )(own, norm, grad, expand, bias, shrink)


def attention_forward_kernel(q_ref, k_ref, v_ref, out_ref, lse_ref):
    length = q_ref.shape[0]
    scaled = q_ref[...] * jnp.bfloat16(HEAD_DIM ** (-0.5))
    keys = k_ref[...]
    values_t = v_ref[...].T
    for start in range(0, length, CHUNK):
        rows = slice(start, start + CHUNK)
        pieces = []
        for head in range(2):
            cols = slice(head * HEAD_DIM, (head + 1) * HEAD_DIM)
            scores = dot_nt(keys[:, cols], scaled[rows, cols])
            top = jnp.max(scores, axis=0, keepdims=True)
            terms = jnp.exp(scores - top)
            total = jnp.sum(terms, axis=0, keepdims=True)
            part = dot_nn(values_t[cols, :], terms.astype(jnp.bfloat16))
            pieces.append(part / total)
            lse_ref[0, head : head + 1, rows] = top + jnp.log(total)
        out_ref[rows, :] = jnp.concatenate(pieces, axis=0).T.astype(jnp.bfloat16)


def attention_forward(projected):
    length = projected.shape[0]
    pairs = HEADS // 2
    return pl.pallas_call(
        attention_forward_kernel,
        grid=(pairs,),
        in_specs=[
            pl.BlockSpec((length, PAIR), lambda i: (0, i)),
            pl.BlockSpec((length, PAIR), lambda i: (0, pairs + i)),
            pl.BlockSpec((length, PAIR), lambda i: (0, 2 * pairs + i)),
        ],
        out_specs=[
            pl.BlockSpec((length, PAIR), lambda i: (0, i)),
            pl.BlockSpec((1, 2, length), lambda i: (i, 0, 0)),
        ],
        out_shape=[
            jax.ShapeDtypeStruct((length, HEADS * HEAD_DIM), jnp.bfloat16),
            jax.ShapeDtypeStruct((pairs, 2, length), jnp.float32),
        ],
        compiler_params=pltpu.CompilerParams(vmem_limit_bytes=48 * 2**20),
        cost_estimate=pl.CostEstimate(flops=16 * 2**30, bytes_accessed=8 * 2**20, transcendentals=16 * 2**20),
        name="attention_forward",
    )(projected, projected, projected)


def attention_backward_kernel(q_ref, k_ref, v_ref, g_ref, lse_ref, out_ref, qb_ref, vb_ref):
    length = q_ref.shape[0]
    root = HEAD_DIM ** (-0.5)
    scaled = q_ref[...] * jnp.bfloat16(root)
    keys = k_ref[...]
    values = v_ref[...]
    grads = g_ref[...]
    keys_t = keys.T
    sums_k = [None, None]
    sums_v = [None, None]
    sum_q = None
    for start in range(0, length, CHUNK):
        rows = slice(start, start + CHUNK)
        pieces = []
        for head in range(2):
            cols = slice(head * HEAD_DIM, (head + 1) * HEAD_DIM)
            query, grad = scaled[rows, cols], grads[rows, cols]
            scores = dot_nt(keys[:, cols], query)
            probs = jnp.exp(scores - lse_ref[0, head : head + 1, rows])
            d_probs = dot_nt(values[:, cols], grad)
            row_sum = jnp.sum(probs * d_probs, axis=0, keepdims=True)
            d_scores = (probs * (d_probs - row_sum)).astype(jnp.bfloat16)
            part_v = dot_nn(probs.astype(jnp.bfloat16), grad)
            part_k = dot_nn(d_scores, query)
            sums_v[head] = part_v if start == 0 else sums_v[head] + part_v
            sums_k[head] = part_k if start == 0 else sums_k[head] + part_k
            pieces.append(dot_nn(keys_t[cols, :], d_scores) * root)
        d_query = jnp.concatenate(pieces, axis=0).T.astype(jnp.bfloat16)
        out_ref[0, rows, :] = d_query
        part_q = jnp.sum(d_query.astype(jnp.float32), axis=0, keepdims=True)
        sum_q = part_q if start == 0 else sum_q + part_q
    out_ref[1] = jnp.concatenate(sums_k, axis=1).astype(jnp.bfloat16)
    d_value = jnp.concatenate(sums_v, axis=1).astype(jnp.bfloat16)
    out_ref[2] = d_value
    qb_ref[...] = sum_q
    vb_ref[...] = jnp.sum(d_value.astype(jnp.float32), axis=0, keepdims=True)


def attention_backward(projected, d_attended, lse):
    length = projected.shape[0]
    width = HEADS * HEAD_DIM
    pairs = HEADS // 2
    block = pl.BlockSpec((length, PAIR), lambda i: (0, i))
    row = pl.BlockSpec((1, PAIR), lambda i: (0, i))
    triple = pl.BlockSpec((3, length, PAIR), lambda i: (0, 0, i))
    whole = jax.ShapeDtypeStruct((3, length, width), jnp.bfloat16)
    line = jax.ShapeDtypeStruct((1, width), jnp.float32)
    return pl.pallas_call(
        attention_backward_kernel,
        grid=(pairs,),
        in_specs=[
            block,
            pl.BlockSpec((length, PAIR), lambda i: (0, pairs + i)),
            pl.BlockSpec((length, PAIR), lambda i: (0, 2 * pairs + i)),
            block,
            pl.BlockSpec((1, 2, length), lambda i: (i, 0, 0)),
        ],
        out_specs=[triple, row, row],
        out_shape=[whole, line, line],
        compiler_params=pltpu.CompilerParams(vmem_limit_bytes=48 * 2**20),
        cost_estimate=pl.CostEstimate(flops=40 * 2**30, bytes_accessed=16 * 2**20, transcendentals=16 * 2**20),
        name="attention_backward",
    )(projected, projected, projected, d_attended, lse)


def normalize(values):
    average = jnp.mean(values, axis=-1, keepdims=True)
    centred = values - average
    variance = jnp.mean(centred * centred, axis=-1, keepdims=True)
    return centred * lax.rsqrt(variance + EPS_NORM)


def modulate(values, shifts, scales):
    return normalize(values) * (1.0 + scales[:, None, :]) + shifts[:, None, :]


def exchange(value, rep_mask, fsdp_mask):
    reps, shards = lax.axis_size("rep"), lax.axis_size("fsdp")
    pairs = [
        (rep * shards + shard, (rep ^ rep_mask) * shards + (shard ^ fsdp_mask))
        for rep in range(reps)
        for shard in range(shards)
    ]
    return lax.ppermute(value, ("rep", "fsdp"), pairs)


def masks_of():
    reps, shards = lax.axis_size("rep"), lax.axis_size("fsdp")
    masks = [(1 << bit, 0) for bit in range(reps.bit_length() - 1)]
    return masks + [(0, 1 << bit) for bit in range(shards.bit_length() - 1)]


def gather_relative(row):
    rows = row[None, :]
    for masks in masks_of():
        rows = jnp.concatenate([rows, exchange(rows, *masks)], axis=0)
    return rows


def to_absolute(parts, own):
    parts = list(parts)
    bit = 1
    while bit < len(parts):
        flipped = (own & bit) != 0
        parts = [jnp.where(flipped, parts[i ^ bit], parts[i]) for i in range(len(parts))]
        bit *= 2
    return parts


def scatter_halves(keep, send, order):
    shards = lax.axis_size("fsdp")
    rows, columns = keep.shape[0] // (2 * shards), keep.shape[1]
    shape = (2, 2, 2, 2, rows, columns)
    masks = {"z2": (0, 4), "z1": (0, 2), "x": (0, 1), "y": (2, 0)}
    axes = ["z2", "z1", "x", "y"]
    arrived = exchange(send, 1, 0)
    total = keep.reshape(shape).astype(jnp.float32) + arrived.reshape(shape).astype(jnp.float32)
    for name in order:
        axis = axes.index(name)
        axes.pop(axis)
        away = lax.index_in_dim(total, 1, axis, keepdims=False).astype(jnp.bfloat16)
        stay = lax.index_in_dim(total, 0, axis, keepdims=False)
        total = stay + exchange(away, *masks[name]).astype(jnp.float32)
    own = total.astype(jnp.bfloat16)
    reps = [own] + [exchange(own, mask, 0) for mask in (1, 2, 3)]
    parts = to_absolute(reps, lax.axis_index("rep"))
    return jnp.concatenate(parts, axis=0).astype(jnp.float32)


def scatter_rows(grad):
    own = lax.psum_scatter(grad, ("fsdp", "rep"), scatter_dimension=0, tiled=True)
    return lax.all_gather(own, "rep", axis=0, tiled=True).astype(jnp.float32)


def own_quarter(weight):
    part = weight.shape[0] // lax.axis_size("rep")
    return lax.dynamic_slice_in_dim(weight, lax.axis_index("rep") * part, part, 0)


def gather_rows(weight):
    return lax.all_gather(own_quarter(weight), ("fsdp", "rep"), axis=0, tiled=True)


def column_blocks(quarter, width):
    rows = quarter.shape[0]
    blocks = quarter.shape[1] // width
    return quarter.reshape(rows, blocks, width).transpose(1, 0, 2).reshape(blocks * rows, width)


def gather_packed(parts, rows):
    packed = jnp.concatenate(parts, axis=0)
    blocks, width = packed.shape[0] // rows, packed.shape[1]
    full = lax.all_gather(packed, ("fsdp", "rep"), axis=0, tiled=True)
    return full.reshape(full.shape[0] // packed.shape[0], blocks, rows, width)


def on_device(
    latents,
    conditions,
    modulator,
    modulbias,
    projector,
    querybias,
    valuebias,
    outweight,
    outbiases,
    expander,
    expandbias,
    shrinker,
    shrinkbias,
    upstream,
):
    seqs_dev, seq_len, feature = latents.shape
    token_count = seqs_dev * seq_len
    shard_id, rep_id = lax.axis_index("fsdp"), lax.axis_index("rep")
    shards, reps = lax.axis_size("fsdp"), lax.axis_size("rep")
    halving = shards == 8 and reps == 4
    own_rows = modulator.shape[0]
    own_bias = modulbias.shape[0]

    if halving:
        quarter = own_rows // reps
        attn_weights = gather_packed(
            [column_blocks(own_quarter(projector), feature), own_quarter(outweight)], quarter
        )
        proj_at, out_at = (attn_weights, 0), (attn_weights, 3)
        ff_weights = gather_packed(
            [own_quarter(shrinker), column_blocks(own_quarter(expander), feature)], quarter
        )
        w_expand, w_shrink = ff_weights, ff_weights
        depth_pieces, unit_pieces = shards * reps, reps
        own = jnp.stack(
            [rep_id & 1, shard_id * 2 + (rep_id >> 1), shard_id, rep_id >> 1]
        ).astype(jnp.int32)
    else:
        proj_at, out_at = (gather_rows(projector), 0), (gather_rows(outweight), 0)
        w_expand, w_shrink = gather_rows(expander), gather_rows(shrinker)
        depth_pieces, unit_pieces = 2, 2
        own = jnp.zeros((4,), jnp.int32)

    def reduce_depth(halves, order):
        if halving:
            return scatter_halves(*halves, order)
        return scatter_rows(jnp.concatenate(halves, axis=0))

    def reduce_units(halves, order):
        if halving:
            return scatter_halves(*halves, order)
        blocks = [half.reshape(-1, 1, FF_BLOCK // 2, feature) for half in halves]
        return scatter_rows(jnp.concatenate(blocks, axis=1).reshape(-1, feature))

    cond_full = conditions.astype(jnp.float32)
    cond_slice = lax.dynamic_slice_in_dim(cond_full, shard_id * own_rows, own_rows, 1)
    cond_act = jax.nn.silu(cond_slice).astype(jnp.bfloat16)
    cond_own = lax.dynamic_slice_in_dim(cond_full, shard_id * seqs_dev, seqs_dev, 0)
    cond_own = jax.nn.silu(cond_own).astype(jnp.bfloat16)
    mod_term = jnp.dot(cond_act, modulator, preferred_element_type=jnp.float32)
    bias_parts = (modulbias, querybias, valuebias, outbiases, expandbias, shrinkbias)
    own_biases = jnp.concatenate([part.astype(jnp.float32) for part in bias_parts])
    mod_width = seqs_dev * 6 * feature
    sent = jnp.concatenate(
        [
            mod_term.reshape(shards, mod_width),
            jnp.broadcast_to(own_biases[None, :], (shards, own_biases.shape[0])),
        ],
        axis=1,
    )
    got = lax.all_to_all(sent, "fsdp", split_axis=0, concat_axis=0, tiled=True)
    full_biases = []
    start = mod_width
    for part in bias_parts:
        full_biases.append(got[:, start : start + part.shape[0]].reshape(1, -1))
        start += part.shape[0]
    full_modbias, b_query, b_value, b_out, b_expand, b_shrink = full_biases
    modvals = jnp.sum(got[:, :mod_width], axis=0).reshape(seqs_dev, 6, feature)
    modvals = modvals + full_modbias.reshape(1, 6, feature)
    shift_a, scale_a, gate_a = (modvals[:, 0], modvals[:, 1], modvals[:, 2])
    shift_m, scale_m, gate_m = (modvals[:, 3], modvals[:, 4], modvals[:, 5])

    resid_in = latents.astype(jnp.float32)
    norm_a = modulate(resid_in, shift_a, scale_a).astype(jnp.bfloat16).reshape(token_count, feature)
    b_proj = jnp.concatenate([b_query, jnp.zeros_like(b_query), b_value], axis=1)
    projected = forward_dot(norm_a, *proj_at, b_proj, jnp.bfloat16, "project")
    attended, log_totals = attention_forward(projected)
    branch_a = forward_dot(attended, *out_at, b_out, jnp.float32, "attention_out")
    branch_a = branch_a.reshape(seqs_dev, seq_len, feature)
    middle = resid_in + gate_a[:, None, :] * branch_a
    norm_m = modulate(middle, shift_m, scale_m).astype(jnp.bfloat16).reshape(token_count, feature)

    grad_out = upstream.astype(jnp.float32)
    d_branch_m = (gate_m[:, None, :] * grad_out).astype(jnp.bfloat16).reshape(token_count, feature)
    g_shrinkbias = jnp.sum(d_branch_m, axis=0, dtype=jnp.float32)
    branch_m, d_norm_m, keep_e, send_e, keep_s, send_s, g_expandbias = feed_forward(
        own, norm_m, d_branch_m, w_expand, b_expand, w_shrink, depth_pieces, unit_pieces
    )
    g_expander = reduce_depth((keep_e, send_e), ("y", "x", "z2", "z1"))
    g_shrinker = reduce_units((keep_s, send_s), ("x", "y", "z2", "z1"))
    branch_m = (branch_m + b_shrink).reshape(seqs_dev, seq_len, feature)
    layer_out = middle + gate_m[:, None, :] * branch_m
    d_gate_m = jnp.sum(grad_out * branch_m, axis=1)
    _, norm_pull_m = jax.vjp(modulate, middle, shift_m, scale_m)
    d_mid_norm, d_shift_m, d_scale_m = norm_pull_m(d_norm_m.reshape(seqs_dev, seq_len, feature))
    d_middle = grad_out + d_mid_norm
    d_branch_a = (gate_a[:, None, :] * d_middle).astype(jnp.bfloat16).reshape(token_count, feature)
    d_gate_a = jnp.sum(d_middle * branch_a, axis=1)
    g_outbiases = jnp.sum(d_branch_a, axis=0, dtype=jnp.float32)
    d_branch_one = d_branch_a[None]
    g_outweight = reduce_depth(
        grad_dot(own, attended, d_branch_one, 0, 1, depth_pieces, "outweight_grad"),
        ("x", "y", "z2", "z1"),
    )
    d_attended = backward_dot(d_branch_one, *out_at, jnp.bfloat16, "attention_out_back")
    early = gather_relative(
        jnp.concatenate(
            [cond_own.reshape(-1)]
            + [
                part.astype(jnp.bfloat16).reshape(-1)
                for part in (
                    d_gate_a, d_shift_m, d_scale_m, d_gate_m, g_outbiases, g_expandbias, g_shrinkbias
                )
            ]
        )
    )
    d_projected, g_querybias, g_valuebias = attention_backward(projected, d_attended, log_totals)
    g_projector = jnp.concatenate(
        [
            reduce_depth(
                grad_dot(own, norm_a, d_projected, 0, 2, depth_pieces, "projector_grad_qk"),
                ("y", "x", "z2", "z1"),
            ),
            reduce_depth(
                grad_dot(own, norm_a, d_projected, 2, 1, depth_pieces, "projector_grad_v"),
                ("x", "y", "z2", "z1"),
            ),
        ],
        axis=1,
    )
    d_norm_a = backward_dot(d_projected, *proj_at, jnp.float32, "project_back")
    _, norm_pull_a = jax.vjp(modulate, resid_in, shift_a, scale_a)
    d_in_norm, d_shift_a, d_scale_a = norm_pull_a(d_norm_a.reshape(seqs_dev, seq_len, feature))
    latents_grad = d_middle + d_in_norm
    late = gather_relative(
        jnp.concatenate(
            [
                part.astype(jnp.bfloat16).reshape(-1)
                for part in (d_shift_a, d_scale_a, g_querybias, g_valuebias)
            ]
        )
    )

    devices = reps * shards
    size = seqs_dev * feature
    cond_all = early[:, :size].reshape(devices * seqs_dev, feature)
    cond_all = lax.dynamic_slice_in_dim(cond_all, shard_id * own_rows, own_rows, 1)
    d_mod = jnp.stack(
        [late[:, i * size : (i + 1) * size] for i in range(2)]
        + [early[:, i * size : (i + 1) * size] for i in range(1, 5)],
        axis=1,
    )
    d_mod = d_mod.reshape(devices, 6, seqs_dev, feature).transpose(0, 2, 1, 3)
    d_mod = d_mod.reshape(devices * seqs_dev, 6 * feature)
    bias_grads = []
    for source, start, width in (
        (late, 2 * size, feature),
        (late, 2 * size + feature, feature),
        (early, 5 * size, feature),
        (early, 5 * size + feature, expandbias.shape[0] * shards),
        (early, 5 * size + feature + expandbias.shape[0] * shards, feature),
    ):
        part = width // shards
        own_part = lax.dynamic_slice_in_dim(source, start + shard_id * part, part, 1)
        bias_grads.append(jnp.sum(own_part, axis=0, dtype=jnp.float32))
    g_modbias = jnp.sum(
        lax.dynamic_slice_in_dim(d_mod, shard_id * own_bias, own_bias, 1), axis=0, dtype=jnp.float32
    )
    g_modulator = jnp.einsum("sr,sc->rc", cond_all, d_mod, preferred_element_type=jnp.float32)
    own_mod = d_mod.reshape(shards, reps, seqs_dev, 6 * feature)[:, 0].reshape(-1, 6 * feature)
    d_cond_act = jnp.einsum("sc,rc->sr", own_mod, modulator, preferred_element_type=jnp.float32)
    d_cond_act = jnp.stack(to_absolute(d_cond_act.reshape(shards, seqs_dev, own_rows), shard_id))
    d_cond_act = d_cond_act.reshape(shards * seqs_dev, own_rows)
    _, silu_pull = jax.vjp(jax.nn.silu, cond_slice)
    conditions_grad = silu_pull(d_cond_act)[0]
    return (
        layer_out,
        latents_grad,
        conditions_grad,
        g_modulator,
        g_modbias,
        g_projector,
        bias_grads[0],
        bias_grads[1],
        g_outweight,
        bias_grads[2],
        g_expander,
        bias_grads[3],
        g_shrinker,
        bias_grads[4],
    )


def solution(mesh):
    return jax.shard_map(
        on_device,
        mesh=mesh,
        in_specs=(
            P(("rep", "fsdp"), None, None),
            P("rep", None),
            P("fsdp", None),
            P("fsdp"),
            P("fsdp", None),
            P("fsdp"),
            P("fsdp"),
            P("fsdp", None),
            P("fsdp"),
            P("fsdp", None),
            P("fsdp"),
            P("fsdp", None),
            P("fsdp"),
            P(("rep", "fsdp"), None, None),
        ),
        out_specs=(
            P(("rep", "fsdp"), None, None),
            P(("rep", "fsdp"), None, None),
            P("rep", "fsdp"),
            P("fsdp", None),
            P("fsdp"),
            P("fsdp", None),
            P("fsdp"),
            P("fsdp"),
            P("fsdp", None),
            P("fsdp"),
            P("fsdp", None),
            P("fsdp"),
            P("fsdp", None),
            P("fsdp"),
        ),
        check_vma=False,
    )
```

```python
from functools import partial

import jax
import jax.numpy as jnp
from jax import lax
from jax.experimental import pallas as pl
from jax.experimental.pallas import tpu as pltpu
from jax.sharding import PartitionSpec as P

HEADS = 16
HEAD_DIM = 64
PAIR = 2 * HEAD_DIM
CHUNK = 256
KEY_BLOCK = 128
EPS_NORM = 1e-06
ROWS = 512
FF_BLOCK = 512
COL_BLOCK = 512
GELU_ROOT = 0.7978845608028654
GELU_CUBE = 0.044715


def dot_nn(left, right):
    return jnp.dot(left, right, preferred_element_type=jnp.float32)


def dot_nt(left, right):
    return lax.dot_general(left, right, (((1,), (1,)), ((), ())), preferred_element_type=jnp.float32)


def dot_tn(left, right):
    return lax.dot_general(left, right, (((0,), (0,)), ((), ())), preferred_element_type=jnp.float32)


def kernel_params(mebibytes):
    return pltpu.CompilerParams(vmem_limit_bytes=mebibytes * 2**20)


def cost(flops, moved, special=0):
    return pl.CostEstimate(flops=flops, bytes_accessed=moved, transcendentals=special)


def weight_spec(weight, first, width, order):
    if weight.ndim == 2:
        offset = first * weight.shape[0] // width
        return pl.BlockSpec((weight.shape[0], width), lambda *at: (0, offset + order(*at)))
    devices, _, rows, columns = weight.shape
    per = columns // width
    return pl.BlockSpec(
        (devices, 1, rows, width),
        lambda *at: (0, first + order(*at) // per, 0, order(*at) % per),
    )


def forward_dot_kernel(x_ref, w_ref, b_ref, out_ref):
    weight = w_ref[...].reshape(x_ref.shape[1], out_ref.shape[1])
    out_ref[...] = (dot_nn(x_ref[...], weight) + b_ref[...]).astype(out_ref.dtype)


def forward_dot(x, weight, first, bias, dtype, name):
    tokens, depth = x.shape
    columns = bias.shape[1]
    return pl.pallas_call(
        forward_dot_kernel,
        grid=(columns // COL_BLOCK,),
        in_specs=[
            pl.BlockSpec((tokens, depth), lambda i: (0, 0)),
            weight_spec(weight, first, COL_BLOCK, lambda i: i),
            pl.BlockSpec((1, COL_BLOCK), lambda i: (0, i)),
        ],
        out_specs=pl.BlockSpec((tokens, COL_BLOCK), lambda i: (0, i)),
        out_shape=jax.ShapeDtypeStruct((tokens, columns), dtype),
        compiler_params=kernel_params(40),
        cost_estimate=cost(tokens * depth * columns, tokens * columns),
        name=name,
    )(x, weight, bias)


def project_kernel(maps, own_ref, x_ref, b_ref, *refs):
    sources, (out_ref, full_ref) = refs[:4], refs[4:]
    step = pl.program_id(0)
    rows = sources[0].shape[1]
    half = pl.num_programs(0) // 2
    for chain in range(2):

        @pl.when((step >= half) == (chain == 1))
        def _():
            for flip in range(2):
                source = sources[2 * chain + flip]
                for index, relative in enumerate(maps[chain]):
                    place = pl.multiple_of((own_ref[0] ^ (relative ^ flip)) * rows, rows)
                    full_ref[pl.ds(place, rows), :] = source[index]

    out_ref[...] = (dot_nn(x_ref[...], full_ref[...]) + b_ref[...]).astype(out_ref.dtype)


def project(flat, x, bias, chains, maps):
    tokens, depth = x.shape
    columns = bias.shape[1]
    steps = columns // COL_BLOCK
    half = steps // 2
    blocks, rows, _ = chains[0][0].shape
    first = pl.BlockSpec((blocks, rows, COL_BLOCK), lambda i, own: (0, 0, jnp.minimum(i, half - 1)))
    second = pl.BlockSpec((blocks, rows, COL_BLOCK), lambda i, own: (0, 0, jnp.maximum(i - half, 0)))
    return pl.pallas_call(
        partial(project_kernel, maps),
        grid_spec=pltpu.PrefetchScalarGridSpec(
            num_scalar_prefetch=1,
            grid=(steps,),
            in_specs=[
                pl.BlockSpec((tokens, depth), lambda i, own: (0, 0)),
                pl.BlockSpec((1, COL_BLOCK), lambda i, own: (0, i)),
                first,
                first,
                second,
                second,
            ],
            out_specs=[
                pl.BlockSpec((tokens, COL_BLOCK), lambda i, own: (0, i)),
                pl.BlockSpec((depth, COL_BLOCK), lambda i, own: (0, i)),
            ],
        ),
        out_shape=[
            jax.ShapeDtypeStruct((tokens, columns), jnp.bfloat16),
            jax.ShapeDtypeStruct((depth, columns), jnp.bfloat16),
        ],
        compiler_params=kernel_params(40),
        cost_estimate=cost(tokens * depth * columns, tokens * columns),
        name="project",
    )(flat, x, bias, *chains[0], *chains[1])


def backward_dot_kernel(dy_ref, w_ref, out_ref, sum_ref):
    step = pl.program_id(0)
    weight = w_ref[...].reshape(out_ref.shape[1], w_ref.shape[-1])
    part = dot_nt(dy_ref[...], weight)

    @pl.when(step == 0)
    def _():
        sum_ref[...] = part

    @pl.when(step > 0)
    def _():
        sum_ref[...] += part

    @pl.when(step == pl.num_programs(0) - 1)
    def _():
        out_ref[...] = sum_ref[...].astype(out_ref.dtype)


def backward_dot(dy, weight, first, dtype, name):
    tokens, columns = dy.shape
    depth = columns
    return pl.pallas_call(
        backward_dot_kernel,
        grid=(columns // COL_BLOCK,),
        in_specs=[
            pl.BlockSpec((tokens, COL_BLOCK), lambda i: (0, i)),
            weight_spec(weight, first, COL_BLOCK, lambda i: i),
        ],
        out_specs=pl.BlockSpec((tokens, depth), lambda i: (0, 0)),
        out_shape=jax.ShapeDtypeStruct((tokens, depth), dtype),
        scratch_shapes=[pltpu.VMEM((tokens, depth), jnp.float32)],
        compiler_params=kernel_params(40),
        cost_estimate=cost(tokens * depth * columns, tokens * columns),
        name=name,
    )(dy, weight)


def project_back_kernel(low_ref, high_ref, w_ref, out_ref):
    step = pl.program_id(0)

    @pl.when(step == 0)
    def _():
        out_ref[...] = dot_nt(low_ref[0], w_ref[...])

    @pl.when((step > 0) & (step % 2 == 0))
    def _():
        out_ref[...] += dot_nt(low_ref[0], w_ref[...])

    @pl.when(step % 2 == 1)
    def _():
        out_ref[...] += dot_nt(high_ref[0], w_ref[...])


def project_back(low, high, weight):
    groups, tokens, width = low.shape
    depth = weight.shape[0]
    block = pl.BlockSpec((1, tokens, width), lambda i: (i // 2, 0, 0))
    return pl.pallas_call(
        project_back_kernel,
        grid=(2 * groups,),
        in_specs=[block, block, pl.BlockSpec((depth, width), lambda i: (0, i))],
        out_specs=pl.BlockSpec((tokens, depth), lambda i: (0, 0)),
        out_shape=jax.ShapeDtypeStruct((tokens, depth), jnp.float32),
        compiler_params=kernel_params(40),
        cost_estimate=cost(groups * tokens * depth * width, tokens * width),
        name="project_back",
    )(low, high, weight)


def store_rows(total, own_core, own_slot, pieces, keep_ref, send_ref):
    rows = total.shape[0] // pieces
    low = total.astype(jnp.bfloat16).reshape(pieces // 2, 2, rows, total.shape[1])
    here = own_core == 0
    for slot in range(pieces // 2):
        first, second = low[slot, 0], low[slot, 1]
        place = pl.ds(pl.multiple_of((own_slot ^ slot) * rows, rows), rows)
        keep_ref[place, :] = jnp.where(here, first, second)
        send_ref[place, :] = jnp.where(here, second, first)


def grad_dot_kernel(pieces, own_ref, x_ref, dy_ref, keep_ref, send_ref):
    total = dot_tn(x_ref[...], dy_ref[0])
    store_rows(total, own_ref[0], own_ref[1], pieces, keep_ref, send_ref)


def grad_dot(own, x, dy, pieces, name):
    tokens, depth = x.shape
    groups, _, columns = dy.shape
    per = columns // COL_BLOCK
    half = jax.ShapeDtypeStruct((depth // 2, groups * columns), jnp.bfloat16)
    block = pl.BlockSpec((depth // 2, COL_BLOCK), lambda i, own: (0, i))
    return pl.pallas_call(
        partial(grad_dot_kernel, pieces),
        grid_spec=pltpu.PrefetchScalarGridSpec(
            num_scalar_prefetch=1,
            grid=(groups * per,),
            in_specs=[
                pl.BlockSpec((tokens, depth), lambda i, own: (0, 0)),
                pl.BlockSpec((1, tokens, COL_BLOCK), lambda i, own: (i // per, 0, i % per)),
            ],
            out_specs=[block, block],
        ),
        out_shape=[half, half],
        compiler_params=kernel_params(40),
        cost_estimate=cost(groups * tokens * depth * columns, tokens * columns),
        name=name,
    )(own, x, dy)


def feed_forward_kernel(
    depth_pieces,
    unit_pieces,
    own_ref,
    norm_ref,
    grad_ref,
    expand_ref,
    bias_ref,
    shrink_ref,
    branch_ref,
    d_norm_ref,
    keep_e_ref,
    send_e_ref,
    keep_s_ref,
    send_s_ref,
    d_bias_ref,
    norm_t,
    hidden,
    d_pre,
):
    tokens, depth = norm_ref.shape
    units = hidden.shape[1]
    step = pl.program_id(0)
    expand = expand_ref[...].reshape(depth, units)
    shrink = shrink_ref[...].reshape(units, depth)

    @pl.when(step == 0)
    def _():
        norm_t[...] = norm_ref[...].T
        branch_ref[...] = jnp.zeros_like(branch_ref)
        d_norm_ref[...] = jnp.zeros_like(d_norm_ref)

    bias_sum = jnp.zeros((1, units), jnp.float32)
    starts = list(range(0, tokens, ROWS))

    def entering(start):
        rows = slice(start, start + ROWS)
        return dot_nn(norm_ref[rows, :], expand), dot_nt(grad_ref[rows, :], shrink)

    upcoming = entering(starts[0])
    for number, start in enumerate(starts):
        rows = slice(start, start + ROWS)
        pre, d_unit = upcoming
        if number + 1 < len(starts):
            upcoming = entering(starts[number + 1])
        pre = pre + bias_ref[...]
        square = pre * pre
        bend = jnp.tanh(GELU_ROOT * pre * (1.0 + GELU_CUBE * square))
        rise = 0.5 + 0.5 * bend
        unit = (pre * rise).astype(jnp.bfloat16)
        hidden[rows, :] = unit
        slope = rise + 0.5 * pre * (1.0 - bend * bend) * (
            GELU_ROOT + (3.0 * GELU_ROOT * GELU_CUBE) * square
        )
        d_low = (d_unit * slope).astype(jnp.bfloat16)
        d_pre[rows, :] = d_low
        bias_sum = bias_sum + jnp.sum(d_low.astype(jnp.float32), axis=0, keepdims=True)
        branch_ref[rows, :] += dot_nn(unit, shrink)
        d_norm_ref[rows, :] += dot_nt(d_low, expand)
    d_bias_ref[...] = bias_sum
    store_rows(
        dot_tn(hidden[...], grad_ref[...]), own_ref[0], own_ref[3], unit_pieces, keep_s_ref, send_s_ref
    )
    store_rows(
        dot_nn(norm_t[...], d_pre[...]), own_ref[0], own_ref[1], depth_pieces, keep_e_ref, send_e_ref
    )


def feed_forward(own, norm, grad, expand, bias, shrink, depth_pieces, unit_pieces):
    tokens, depth = norm.shape
    total = bias.shape[1]
    steps = total // FF_BLOCK
    whole = pl.BlockSpec((tokens, depth), lambda i, own: (0, 0))
    half_e = pl.BlockSpec((depth // 2, FF_BLOCK), lambda i, own: (0, i))
    half_s = pl.BlockSpec((FF_BLOCK // 2, depth), lambda i, own: (i ^ own[2], 0))
    line = pl.BlockSpec((1, FF_BLOCK), lambda i, own: (0, i))
    if shrink.ndim == 2:
        spec_e = weight_spec(expand, 0, FF_BLOCK, lambda i, own: i)
        spec_s = pl.BlockSpec((FF_BLOCK, depth), lambda i, own: (i, 0))
    else:
        devices, blocks, rows, columns = shrink.shape
        spec_e = weight_spec(expand, 4, FF_BLOCK, lambda i, own: i)
        spec_s = pl.BlockSpec((devices // steps, 4, rows, columns), lambda i, own: (i, 0, 0, 0))
    wide = jax.ShapeDtypeStruct((tokens, depth), jnp.float32)
    out_e = jax.ShapeDtypeStruct((depth // 2, total), jnp.bfloat16)
    out_s = jax.ShapeDtypeStruct((total // 2, depth), jnp.bfloat16)
    return pl.pallas_call(
        partial(feed_forward_kernel, depth_pieces, unit_pieces),
        grid_spec=pltpu.PrefetchScalarGridSpec(
            num_scalar_prefetch=1,
            grid=(steps,),
            in_specs=[whole, whole, spec_e, line, spec_s],
            out_specs=[whole, whole, half_e, half_e, half_s, half_s, line],
            scratch_shapes=[
                pltpu.VMEM((depth, tokens), jnp.bfloat16),
                pltpu.VMEM((tokens, FF_BLOCK), jnp.bfloat16),
                pltpu.VMEM((tokens, FF_BLOCK), jnp.bfloat16),
            ],
        ),
        out_shape=[
            wide,
            wide,
            out_e,
            out_e,
            out_s,
            out_s,
            jax.ShapeDtypeStruct((1, total), jnp.float32),
        ],
        compiler_params=kernel_params(56),
        cost_estimate=cost(6 * tokens * depth * total, 16 * 2**20, tokens * total),
        name="feed_forward",
    )(own, norm, grad, expand, bias, shrink)


def attention_forward_kernel(q_ref, k_ref, v_ref, out_ref, out_t_ref, lse_ref):
    length = q_ref.shape[0]
    scaled = q_ref[...] * jnp.bfloat16(HEAD_DIM ** (-0.5))
    keys = k_ref[...]
    values_t = v_ref[...].T
    ones = jnp.ones((16, length), jnp.bfloat16)
    extended = [
        jnp.concatenate([values_t[head * HEAD_DIM : (head + 1) * HEAD_DIM], ones], axis=0)
        for head in range(2)
    ]
    tasks = [(start, head) for start in range(0, length, CHUNK) for head in range(2)]

    def scores_of(task):
        start, head = task
        cols = slice(head * HEAD_DIM, (head + 1) * HEAD_DIM)
        return dot_nt(keys[:, cols], scaled[start : start + CHUNK, cols])

    upcoming = scores_of(tasks[0])
    pieces = []
    for number, (start, head) in enumerate(tasks):
        scores = upcoming
        if number + 1 < len(tasks):
            upcoming = scores_of(tasks[number + 1])
        rows = slice(start, start + CHUNK)
        top = jnp.max(scores, axis=0, keepdims=True)
        terms = jnp.exp(scores - top).astype(jnp.bfloat16)
        part = dot_nn(extended[head], terms)
        total = part[HEAD_DIM : HEAD_DIM + 1]
        piece = part[:HEAD_DIM] / total
        lse_ref[0, head : head + 1, rows] = top + jnp.log(total)
        out_t_ref[head * HEAD_DIM : (head + 1) * HEAD_DIM, rows] = piece
        pieces.append(piece)
        if head == 1:
            out_ref[rows, :] = jnp.concatenate(pieces, axis=0).T.astype(jnp.bfloat16)
            pieces = []


def attention_forward(projected):
    length = projected.shape[0]
    pairs = HEADS // 2
    return pl.pallas_call(
        attention_forward_kernel,
        grid=(pairs,),
        in_specs=[
            pl.BlockSpec((length, PAIR), lambda i: (0, i)),
            pl.BlockSpec((length, PAIR), lambda i: (0, pairs + i)),
            pl.BlockSpec((length, PAIR), lambda i: (0, 2 * pairs + i)),
        ],
        out_specs=[
            pl.BlockSpec((length, PAIR), lambda i: (0, i)),
            pl.BlockSpec((PAIR, length), lambda i: (i, 0)),
            pl.BlockSpec((1, 2, length), lambda i: (i, 0, 0)),
        ],
        out_shape=[
            jax.ShapeDtypeStruct((length, HEADS * HEAD_DIM), jnp.bfloat16),
            jax.ShapeDtypeStruct((HEADS * HEAD_DIM, length), jnp.float32),
            jax.ShapeDtypeStruct((pairs, 2, length), jnp.float32),
        ],
        compiler_params=kernel_params(48),
        cost_estimate=cost(2**32, 8 * 2**20, 2**24),
        name="attention_forward",
    )(projected, projected, projected)


def attention_backward_kernel(
    q_ref, k_ref, v_ref, g_ref, o_ref, lse_ref, out_ref, qb_ref, vb_ref, probs, d_scores
):
    length = q_ref.shape[0]
    root = HEAD_DIM ** (-0.5)
    scaled = q_ref[...] * jnp.bfloat16(root)
    keys = k_ref[...]
    values = v_ref[...]
    grads = g_ref[...]
    keys_t = keys.T
    product = grads.T.astype(jnp.float32) * o_ref[...]
    sums_k = [None, None]
    sums_v = [None, None]
    sum_q = None
    pieces = []
    tasks = [(start, head) for start in range(0, length, CHUNK) for head in range(2)]
    for number, (start, head) in enumerate(tasks):
        rows = slice(start, start + CHUNK)
        slot = number % 2
        cols = slice(head * HEAD_DIM, (head + 1) * HEAD_DIM)
        query, grad = scaled[rows, cols], grads[rows, cols]
        lse = lse_ref[0, head : head + 1, rows]
        row_sum = jnp.sum(product[cols, rows], axis=0, keepdims=True)
        for block in range(0, length, KEY_BLOCK):
            some = slice(block, block + KEY_BLOCK)
            prob = jnp.exp(dot_nt(keys[some, cols], query) - lse)
            d_prob = dot_nt(values[some, cols], grad)
            probs[slot, some, :] = prob.astype(jnp.bfloat16)
            d_scores[slot, some, :] = (prob * (d_prob - row_sum)).astype(jnp.bfloat16)
        part_v = dot_nn(probs[slot], grad)
        part_k = dot_nn(d_scores[slot], query)
        sums_v[head] = part_v if start == 0 else sums_v[head] + part_v
        sums_k[head] = part_k if start == 0 else sums_k[head] + part_k
        pieces.append(dot_nn(keys_t[cols, :], d_scores[slot]) * root)
        if head == 1:
            d_query = jnp.concatenate(pieces, axis=0).T.astype(jnp.bfloat16)
            pieces = []
            out_ref[0, rows, :] = d_query
            part_q = jnp.sum(d_query.astype(jnp.float32), axis=0, keepdims=True)
            sum_q = part_q if start == 0 else sum_q + part_q
    out_ref[1] = jnp.concatenate(sums_k, axis=1).astype(jnp.bfloat16)
    d_value = jnp.concatenate(sums_v, axis=1).astype(jnp.bfloat16)
    out_ref[2] = d_value
    qb_ref[...] = sum_q
    vb_ref[...] = jnp.sum(d_value.astype(jnp.float32), axis=0, keepdims=True)


def attention_backward(projected, d_attended, attended_t, lse, first, count, name):
    length = projected.shape[0]
    width = count * PAIR
    pairs = HEADS // 2
    row = pl.BlockSpec((1, PAIR), lambda i: (0, i))
    line = jax.ShapeDtypeStruct((1, width), jnp.float32)
    return pl.pallas_call(
        attention_backward_kernel,
        grid=(count,),
        in_specs=[
            pl.BlockSpec((length, PAIR), lambda i: (0, first + i)),
            pl.BlockSpec((length, PAIR), lambda i: (0, pairs + first + i)),
            pl.BlockSpec((length, PAIR), lambda i: (0, 2 * pairs + first + i)),
            pl.BlockSpec((length, PAIR), lambda i: (0, first + i)),
            pl.BlockSpec((PAIR, length), lambda i: (first + i, 0)),
            pl.BlockSpec((1, 2, length), lambda i: (first + i, 0, 0)),
        ],
        out_specs=[pl.BlockSpec((3, length, PAIR), lambda i: (0, 0, i)), row, row],
        out_shape=[jax.ShapeDtypeStruct((3, length, width), jnp.bfloat16), line, line],
        scratch_shapes=[
            pltpu.VMEM((2, length, CHUNK), jnp.bfloat16),
            pltpu.VMEM((2, length, CHUNK), jnp.bfloat16),
        ],
        compiler_params=kernel_params(48),
        cost_estimate=cost(count * 2**29, count * 2 * 2**20, count * 2**21),
        name=name,
    )(projected, projected, projected, d_attended, attended_t, lse)


def normalize(values):
    average = jnp.mean(values, axis=-1, keepdims=True)
    centred = values - average
    variance = jnp.mean(centred * centred, axis=-1, keepdims=True)
    return centred * lax.rsqrt(variance + EPS_NORM)


def modulate(values, shifts, scales):
    return normalize(values) * (1.0 + scales[:, None, :]) + shifts[:, None, :]


MASKS = {"core": (1, 0), "y": (2, 0), "x": (0, 1), "z1": (0, 2), "z2": (0, 4)}
GATHER_ORDERS = (("z1", "z2", "x", "y"), ("z1", "z2", "y", "x"))


def exchange(value, rep_mask, fsdp_mask):
    reps, shards = lax.axis_size("rep"), lax.axis_size("fsdp")
    pairs = [
        (rep * shards + shard, (rep ^ rep_mask) * shards + (shard ^ fsdp_mask))
        for rep in range(reps)
        for shard in range(shards)
    ]
    return lax.ppermute(value, ("rep", "fsdp"), pairs)


def gather_relative(row):
    reps, shards = lax.axis_size("rep"), lax.axis_size("fsdp")
    masks = [(0, 1 << bit) for bit in reversed(range(shards.bit_length() - 1))]
    masks += [(1 << bit, 0) for bit in reversed(range(reps.bit_length() - 1))]
    rows = row[None]
    for pair in masks:
        rows = jnp.stack([rows, exchange(rows, *pair)], axis=1).reshape(-1, *row.shape)
    return rows


def gather_chain(quarter, order):
    rows = quarter[None]
    for name in order:
        rows = jnp.concatenate([rows, exchange(rows, *MASKS[name])], axis=0)
    return rows, exchange(rows, *MASKS["core"])


def chain_map(order):
    offsets = [0]
    for name in order:
        rep_mask, fsdp_mask = MASKS[name]
        offsets += [offset ^ (fsdp_mask * 4 + rep_mask) for offset in offsets]
    return tuple(offsets)


def to_absolute(parts, own):
    parts = list(parts)
    bit = 1
    while bit < len(parts):
        flipped = (own & bit) != 0
        parts = [jnp.where(flipped, parts[i ^ bit], parts[i]) for i in range(len(parts))]
        bit *= 2
    return parts


class HalvingSum:
    def __init__(self, keep, send, order):
        rows, columns = keep.shape[0] // 16, keep.shape[1]
        self.shape = (2, 2, 2, 2, rows, columns)
        self.axes = ["z2", "z1", "x", "y"]
        self.order = list(order)
        self.stay = keep.reshape(self.shape)
        self.arrived = exchange(send, *MASKS["core"])

    def half(self, axis, side):
        stay = lax.index_in_dim(self.stay, side, axis, keepdims=False)
        arrived = lax.index_in_dim(self.arrived.reshape(self.stay.shape), side, axis, keepdims=False)
        return (stay.astype(jnp.float32) + arrived.astype(jnp.float32)).astype(jnp.bfloat16)

    def step(self):
        name = self.order.pop(0)
        axis = self.axes.index(name)
        self.axes.pop(axis)
        away, stay = self.half(axis, 1), self.half(axis, 0)
        self.stay, self.arrived = stay, exchange(away, *MASKS[name])

    def finish(self):
        while self.order:
            self.step()
        own = self.stay.astype(jnp.float32) + self.arrived.reshape(self.stay.shape).astype(jnp.float32)
        own = own.astype(jnp.bfloat16)
        pair = [own, exchange(own, *MASKS["core"])]
        both = jnp.stack(pair)
        other = exchange(both, *MASKS["y"])
        parts = to_absolute([*pair, other[0], other[1]], lax.axis_index("rep"))
        return jnp.concatenate(parts, axis=0).astype(jnp.float32)


class PlainSum:
    def __init__(self, grad):
        self.arrived = grad

    def step(self):
        pass

    def finish(self):
        return scatter_rows(self.arrived)


def hold(value, *sums):
    held = lax.optimization_barrier((value, *[total.arrived for total in sums]))
    for total, arrived in zip(sums, held[1:]):
        total.arrived = arrived
    return held[0]


def scatter_rows(grad):
    own = lax.psum_scatter(grad, ("fsdp", "rep"), scatter_dimension=0, tiled=True)
    return lax.all_gather(own, "rep", axis=0, tiled=True).astype(jnp.float32)


def own_quarter(weight):
    part = weight.shape[0] // lax.axis_size("rep")
    return lax.dynamic_slice_in_dim(weight, lax.axis_index("rep") * part, part, 0)


def gather_rows(weight):
    return lax.all_gather(own_quarter(weight), ("fsdp", "rep"), axis=0, tiled=True)


def column_blocks(quarter, width):
    rows = quarter.shape[0]
    blocks = quarter.shape[1] // width
    return quarter.reshape(rows, blocks, width).transpose(1, 0, 2).reshape(blocks * rows, width)


def gather_packed(parts, rows):
    packed = jnp.concatenate(parts, axis=0)
    blocks, width = packed.shape[0] // rows, packed.shape[1]
    full = lax.all_gather(packed, ("fsdp", "rep"), axis=0, tiled=True)
    return full.reshape(full.shape[0] // packed.shape[0], blocks, rows, width)


def on_device(
    latents,
    conditions,
    modulator,
    modulbias,
    projector,
    querybias,
    valuebias,
    outweight,
    outbiases,
    expander,
    expandbias,
    shrinker,
    shrinkbias,
    upstream,
):
    seqs_dev, seq_len, feature = latents.shape
    token_count = seqs_dev * seq_len
    shard_id, rep_id = lax.axis_index("fsdp"), lax.axis_index("rep")
    shards, reps = lax.axis_size("fsdp"), lax.axis_size("rep")
    halving = shards == 8 and reps == 4
    own_rows = modulator.shape[0]
    own_bias = modulbias.shape[0]

    width = projector.shape[1]
    if halving:
        quarter = own_rows // reps
        proj_quarter = own_quarter(projector)
        chains = [
            gather_chain(proj_quarter[:, part * (width // 2) : (part + 1) * (width // 2)], order)
            for part, order in enumerate(GATHER_ORDERS)
        ]
        maps = [chain_map(order) for order in GATHER_ORDERS]
        packed = gather_packed(
            [
                own_quarter(shrinker),
                column_blocks(own_quarter(expander), feature),
                own_quarter(outweight),
            ],
            quarter,
        )
        out_at = (packed, 8)
        w_expand, w_shrink = packed, packed
        depth_pieces, unit_pieces = shards * reps, reps
        own = jnp.stack(
            [rep_id & 1, shard_id * 2 + (rep_id >> 1), shard_id, rep_id >> 1]
        ).astype(jnp.int32)
    else:
        w_proj, out_at = gather_rows(projector), (gather_rows(outweight), 0)
        w_expand, w_shrink = gather_rows(expander), gather_rows(shrinker)
        depth_pieces, unit_pieces = 2, 2
        own = jnp.zeros((4,), jnp.int32)

    def depth_sum(halves, order):
        if halving:
            return HalvingSum(*halves, order)
        return PlainSum(jnp.concatenate(halves, axis=0))

    def unit_sum(halves, order):
        if halving:
            return HalvingSum(*halves, order)
        blocks = [half.reshape(-1, 1, FF_BLOCK // 2, feature) for half in halves]
        return PlainSum(jnp.concatenate(blocks, axis=1).reshape(-1, feature))

    cond_full = conditions.astype(jnp.float32)
    cond_slice = lax.dynamic_slice_in_dim(cond_full, shard_id * own_rows, own_rows, 1)
    cond_act = jax.nn.silu(cond_slice).astype(jnp.bfloat16)
    cond_own = lax.dynamic_slice_in_dim(cond_full, shard_id * seqs_dev, seqs_dev, 0)
    cond_own = jax.nn.silu(cond_own).astype(jnp.bfloat16)
    mod_term = jnp.dot(cond_act, modulator, preferred_element_type=jnp.float32)
    bias_parts = (modulbias, querybias, valuebias, outbiases, expandbias, shrinkbias)
    own_biases = jnp.concatenate([part.astype(jnp.float32) for part in bias_parts])
    mod_width = seqs_dev * 6 * feature
    sent = jnp.concatenate(
        [
            mod_term.reshape(shards, mod_width),
            jnp.broadcast_to(own_biases[None, :], (shards, own_biases.shape[0])),
        ],
        axis=1,
    )
    got = lax.all_to_all(sent, "fsdp", split_axis=0, concat_axis=0, tiled=True)
    full_biases = []
    start = mod_width
    for part in bias_parts:
        full_biases.append(got[:, start : start + part.shape[0]].reshape(1, -1))
        start += part.shape[0]
    full_modbias, b_query, b_value, b_out, b_expand, b_shrink = full_biases
    modvals = jnp.sum(got[:, :mod_width], axis=0).reshape(seqs_dev, 6, feature)
    modvals = modvals + full_modbias.reshape(1, 6, feature)
    shift_a, scale_a, gate_a = (modvals[:, 0], modvals[:, 1], modvals[:, 2])
    shift_m, scale_m, gate_m = (modvals[:, 3], modvals[:, 4], modvals[:, 5])

    resid_in = latents.astype(jnp.float32)
    norm_a = modulate(resid_in, shift_a, scale_a).astype(jnp.bfloat16).reshape(token_count, feature)
    b_proj = jnp.concatenate([b_query, jnp.zeros_like(b_query), b_value], axis=1)
    if halving:
        flat = (shard_id * reps + rep_id).astype(jnp.int32)[None]
        projected, w_proj = project(flat, norm_a, b_proj, chains, maps)
    else:
        projected = forward_dot(norm_a, w_proj, 0, b_proj, jnp.bfloat16, "project")
    attended, attended_t, log_totals = attention_forward(projected)
    branch_a = forward_dot(attended, *out_at, b_out, jnp.float32, "attention_out")
    branch_a = branch_a.reshape(seqs_dev, seq_len, feature)
    middle = resid_in + gate_a[:, None, :] * branch_a
    norm_m = modulate(middle, shift_m, scale_m).astype(jnp.bfloat16).reshape(token_count, feature)

    grad_out = upstream.astype(jnp.float32)
    d_branch_m = (gate_m[:, None, :] * grad_out).astype(jnp.bfloat16).reshape(token_count, feature)
    g_shrinkbias = jnp.sum(d_branch_m, axis=0, dtype=jnp.float32)
    branch_m, d_norm_m, keep_e, send_e, keep_s, send_s, g_expandbias = feed_forward(
        own, norm_m, d_branch_m, w_expand, b_expand, w_shrink, depth_pieces, unit_pieces
    )
    sum_e = depth_sum((keep_e, send_e), ("y", "x", "z2", "z1"))
    sum_s = unit_sum((keep_s, send_s), ("x", "y", "z2", "z1"))
    branch_m = (branch_m + b_shrink).reshape(seqs_dev, seq_len, feature)
    layer_out = middle + gate_m[:, None, :] * branch_m
    d_gate_m = jnp.sum(grad_out * branch_m, axis=1)
    _, norm_pull_m = jax.vjp(modulate, middle, shift_m, scale_m)
    d_mid_norm, d_shift_m, d_scale_m = norm_pull_m(d_norm_m.reshape(seqs_dev, seq_len, feature))
    d_middle = grad_out + d_mid_norm
    d_branch_a = (gate_a[:, None, :] * d_middle).astype(jnp.bfloat16).reshape(token_count, feature)
    d_gate_a = jnp.sum(d_middle * branch_a, axis=1)
    g_outbiases = jnp.sum(d_branch_a, axis=0, dtype=jnp.float32)
    d_attended = backward_dot(d_branch_a, *out_at, jnp.bfloat16, "attention_out_back")
    d_attended = hold(d_attended, sum_e, sum_s)
    sum_e.step()
    sum_s.step()
    half_pairs = HEADS // 4
    d_low, q_low, v_low = attention_backward(
        projected, d_attended, attended_t, log_totals, 0, half_pairs, "attention_backward_low"
    )
    sum_low = depth_sum(
        grad_dot(own, norm_a, d_low, depth_pieces, "projector_grad_low"), ("y", "x", "z2", "z1")
    )
    sum_out = depth_sum(
        grad_dot(own, attended, d_branch_a[None], depth_pieces, "outweight_grad"),
        ("x", "y", "z2", "z1"),
    )
    d_attended = hold(d_attended, sum_e, sum_s, sum_low, sum_out)
    for total in (sum_e, sum_s, sum_low, sum_out):
        total.step()
    d_high, q_high, v_high = attention_backward(
        projected, d_attended, attended_t, log_totals, half_pairs, half_pairs, "attention_backward_high"
    )
    d_high = hold(d_high, sum_e, sum_s, sum_low, sum_out)
    for total in (sum_e, sum_s, sum_low, sum_out):
        total.step()
    sum_high = depth_sum(
        grad_dot(own, norm_a, d_high, depth_pieces, "projector_grad_high"), ("x", "y", "z2", "z1")
    )
    d_norm_a = project_back(d_low, d_high, w_proj)
    d_norm_a = hold(d_norm_a, sum_high)
    sum_high.step()
    g_querybias = jnp.concatenate([q_low, q_high], axis=1)
    g_valuebias = jnp.concatenate([v_low, v_high], axis=1)
    _, norm_pull_a = jax.vjp(modulate, resid_in, shift_a, scale_a)
    d_in_norm, d_shift_a, d_scale_a = norm_pull_a(d_norm_a.reshape(seqs_dev, seq_len, feature))
    latents_grad = d_middle + d_in_norm
    small = jnp.concatenate(
        [
            part.astype(jnp.bfloat16).reshape(-1)
            for part in (
                d_shift_a,
                d_scale_a,
                d_gate_a,
                d_shift_m,
                d_scale_m,
                d_gate_m,
                cond_own,
                g_querybias,
                g_valuebias,
                g_outbiases,
                g_expandbias,
                g_shrinkbias,
            )
        ]
    )
    devices = reps * shards
    size = seqs_dev * feature
    gathered = gather_relative(small.reshape(-1, 128)).reshape(devices, -1)
    g_expander, g_shrinker = sum_e.finish(), sum_s.finish()
    g_outweight = sum_out.finish()
    low, high = sum_low.finish(), sum_high.finish()
    g_projector = jnp.stack(
        [low.reshape(own_rows, 3, feature // 2), high.reshape(own_rows, 3, feature // 2)], axis=2
    ).reshape(own_rows, 3 * feature)

    cond_all = gathered[:, 6 * size : 7 * size].reshape(devices * seqs_dev, feature)
    cond_all = lax.dynamic_slice_in_dim(cond_all, shard_id * own_rows, own_rows, 1)
    d_mod = gathered[:, : 6 * size]
    d_mod = d_mod.reshape(devices, 6, seqs_dev, feature).transpose(0, 2, 1, 3)
    d_mod = d_mod.reshape(devices * seqs_dev, 6 * feature)
    bias_grads = []
    start = 7 * size
    for total in (feature, feature, feature, expandbias.shape[0] * shards, feature):
        part = total // shards
        own_part = lax.dynamic_slice_in_dim(gathered, start + shard_id * part, part, 1)
        bias_grads.append(jnp.sum(own_part, axis=0, dtype=jnp.float32))
        start += total
    g_modbias = jnp.sum(
        lax.dynamic_slice_in_dim(d_mod, shard_id * own_bias, own_bias, 1), axis=0, dtype=jnp.float32
    )
    g_modulator = jnp.einsum("sr,sc->rc", cond_all, d_mod, preferred_element_type=jnp.float32)
    own_mod = d_mod.reshape(shards, reps, seqs_dev, 6 * feature)[:, 0].reshape(-1, 6 * feature)
    d_cond_act = jnp.einsum("sc,rc->sr", own_mod, modulator, preferred_element_type=jnp.float32)
    d_cond_act = jnp.stack(to_absolute(d_cond_act.reshape(shards, seqs_dev, own_rows), shard_id))
    d_cond_act = d_cond_act.reshape(shards * seqs_dev, own_rows)
    _, silu_pull = jax.vjp(jax.nn.silu, cond_slice)
    conditions_grad = silu_pull(d_cond_act)[0]
    return (
        layer_out,
        latents_grad,
        conditions_grad,
        g_modulator,
        g_modbias,
        g_projector,
        bias_grads[0],
        bias_grads[1],
        g_outweight,
        bias_grads[2],
        g_expander,
        bias_grads[3],
        g_shrinker,
        bias_grads[4],
    )


def solution(mesh):
    return jax.shard_map(
        on_device,
        mesh=mesh,
        in_specs=(
            P(("rep", "fsdp"), None, None),
            P("rep", None),
            P("fsdp", None),
            P("fsdp"),
            P("fsdp", None),
            P("fsdp"),
            P("fsdp"),
            P("fsdp", None),
            P("fsdp"),
            P("fsdp", None),
            P("fsdp"),
            P("fsdp", None),
            P("fsdp"),
            P(("rep", "fsdp"), None, None),
        ),
        out_specs=(
            P(("rep", "fsdp"), None, None),
            P(("rep", "fsdp"), None, None),
            P("rep", "fsdp"),
            P("fsdp", None),
            P("fsdp"),
            P("fsdp", None),
            P("fsdp"),
            P("fsdp"),
            P("fsdp", None),
            P("fsdp"),
            P("fsdp", None),
            P("fsdp"),
            P("fsdp", None),
            P("fsdp"),
        ),
        check_vma=False,
    )
```

```python
from functools import partial

import jax
import jax.numpy as jnp
from jax import lax
from jax.experimental import pallas as pl
from jax.experimental.pallas import tpu as pltpu
from jax.sharding import PartitionSpec as P

HEADS = 16
HEAD_DIM = 64
PAIR = 2 * HEAD_DIM
CHUNK = 256
KEY_BLOCK = 128
EPS_NORM = 1e-06
UNIT_SHARDS = 8
ROWS = 256
FF_BLOCK = 512
COL_BLOCK = 512
GELU_ROOT = 0.7978845608028654
GELU_CUBE = 0.044715


def dot_nn(left, right):
    return jnp.dot(left, right, preferred_element_type=jnp.float32)


def dot_nt(left, right):
    return lax.dot_general(left, right, (((1,), (1,)), ((), ())), preferred_element_type=jnp.float32)


def dot_tn(left, right):
    return lax.dot_general(left, right, (((0,), (0,)), ((), ())), preferred_element_type=jnp.float32)


def kernel_params(mebibytes):
    return pltpu.CompilerParams(vmem_limit_bytes=mebibytes * 2**20)


def cost(flops, moved, special=0):
    return pl.CostEstimate(flops=flops, bytes_accessed=moved, transcendentals=special)


def weight_spec(weight, first, width, order):
    if weight.ndim == 2:
        offset = first * weight.shape[0] // width
        return pl.BlockSpec((weight.shape[0], width), lambda *at: (0, offset + order(*at)))
    devices, _, rows, columns = weight.shape
    per = columns // width
    return pl.BlockSpec(
        (devices, 1, rows, width),
        lambda *at: (0, first + order(*at) // per, 0, order(*at) % per),
    )


def forward_dot_kernel(x_ref, w_ref, b_ref, out_ref):
    weight = w_ref[...].reshape(x_ref.shape[1], out_ref.shape[1])
    out_ref[...] = (dot_nn(x_ref[...], weight) + b_ref[...]).astype(out_ref.dtype)


def forward_dot(x, weight, first, bias, dtype, name):
    tokens, depth = x.shape
    columns = bias.shape[1]
    return pl.pallas_call(
        forward_dot_kernel,
        grid=(columns // COL_BLOCK,),
        in_specs=[
            pl.BlockSpec((tokens, depth), lambda i: (0, 0)),
            weight_spec(weight, first, COL_BLOCK, lambda i: i),
            pl.BlockSpec((1, COL_BLOCK), lambda i: (0, i)),
        ],
        out_specs=pl.BlockSpec((tokens, COL_BLOCK), lambda i: (0, i)),
        out_shape=jax.ShapeDtypeStruct((tokens, columns), dtype),
        compiler_params=kernel_params(40),
        cost_estimate=cost(tokens * depth * columns, tokens * columns),
        name=name,
    )(x, weight, bias)


def project_kernel(maps, own_ref, x_ref, b_ref, *refs):
    sources, (out_ref, full_ref) = refs[:4], refs[4:]
    step = pl.program_id(0)
    rows = sources[0].shape[1]
    half = pl.num_programs(0) // 2
    for chain in range(2):

        @pl.when((step >= half) == (chain == 1))
        def _():
            for flip in range(2):
                source = sources[2 * chain + flip]
                for index, relative in enumerate(maps[chain]):
                    place = pl.multiple_of((own_ref[0] ^ (relative ^ flip)) * rows, rows)
                    full_ref[pl.ds(place, rows), :] = source[index]

    out_ref[...] = (dot_nn(x_ref[...], full_ref[...]) + b_ref[...]).astype(out_ref.dtype)


def project(flat, x, bias, chains, maps):
    tokens, depth = x.shape
    columns = bias.shape[1]
    steps = columns // COL_BLOCK
    half = steps // 2
    blocks, rows, _ = chains[0][0].shape
    first = pl.BlockSpec((blocks, rows, COL_BLOCK), lambda i, own: (0, 0, jnp.minimum(i, half - 1)))
    second = pl.BlockSpec((blocks, rows, COL_BLOCK), lambda i, own: (0, 0, jnp.maximum(i - half, 0)))
    return pl.pallas_call(
        partial(project_kernel, maps),
        grid_spec=pltpu.PrefetchScalarGridSpec(
            num_scalar_prefetch=1,
            grid=(steps,),
            in_specs=[
                pl.BlockSpec((tokens, depth), lambda i, own: (0, 0)),
                pl.BlockSpec((1, COL_BLOCK), lambda i, own: (0, i)),
                first,
                first,
                second,
                second,
            ],
            out_specs=[
                pl.BlockSpec((tokens, COL_BLOCK), lambda i, own: (0, i)),
                pl.BlockSpec((depth, COL_BLOCK), lambda i, own: (0, i)),
            ],
        ),
        out_shape=[
            jax.ShapeDtypeStruct((tokens, columns), jnp.bfloat16),
            jax.ShapeDtypeStruct((depth, columns), jnp.bfloat16),
        ],
        compiler_params=kernel_params(40),
        cost_estimate=cost(tokens * depth * columns, tokens * columns),
        name="project",
    )(flat, x, bias, *chains[0], *chains[1])


def backward_dot_kernel(dy_ref, w_ref, out_ref, sum_ref):
    step = pl.program_id(0)
    weight = w_ref[...].reshape(out_ref.shape[1], w_ref.shape[-1])
    part = dot_nt(dy_ref[...], weight)

    @pl.when(step == 0)
    def _():
        sum_ref[...] = part

    @pl.when(step > 0)
    def _():
        sum_ref[...] += part

    @pl.when(step == pl.num_programs(0) - 1)
    def _():
        out_ref[...] = sum_ref[...].astype(out_ref.dtype)


def backward_dot(dy, weight, first, dtype, name):
    tokens, columns = dy.shape
    depth = columns
    return pl.pallas_call(
        backward_dot_kernel,
        grid=(columns // COL_BLOCK,),
        in_specs=[
            pl.BlockSpec((tokens, COL_BLOCK), lambda i: (0, i)),
            weight_spec(weight, first, COL_BLOCK, lambda i: i),
        ],
        out_specs=pl.BlockSpec((tokens, depth), lambda i: (0, 0)),
        out_shape=jax.ShapeDtypeStruct((tokens, depth), dtype),
        scratch_shapes=[pltpu.VMEM((tokens, depth), jnp.float32)],
        compiler_params=kernel_params(40),
        cost_estimate=cost(tokens * depth * columns, tokens * columns),
        name=name,
    )(dy, weight)


def project_back_kernel(low_ref, high_ref, w_ref, out_ref):
    step = pl.program_id(0)

    @pl.when(step == 0)
    def _():
        out_ref[...] = dot_nt(low_ref[0], w_ref[...])

    @pl.when((step > 0) & (step % 2 == 0))
    def _():
        out_ref[...] += dot_nt(low_ref[0], w_ref[...])

    @pl.when(step % 2 == 1)
    def _():
        out_ref[...] += dot_nt(high_ref[0], w_ref[...])


def project_back(low, high, weight):
    groups, tokens, width = low.shape
    depth = weight.shape[0]
    block = pl.BlockSpec((1, tokens, width), lambda i: (i // 2, 0, 0))
    return pl.pallas_call(
        project_back_kernel,
        grid=(2 * groups,),
        in_specs=[block, block, pl.BlockSpec((depth, width), lambda i: (0, i))],
        out_specs=pl.BlockSpec((tokens, depth), lambda i: (0, 0)),
        out_shape=jax.ShapeDtypeStruct((tokens, depth), jnp.float32),
        compiler_params=kernel_params(40),
        cost_estimate=cost(groups * tokens * depth * width, tokens * width),
        name="project_back",
    )(low, high, weight)


def store_rows(total, own_core, own_slot, pieces, keep_ref, send_ref):
    rows = total.shape[0] // pieces
    low = total.astype(jnp.bfloat16).reshape(pieces // 2, 2, rows, total.shape[1])
    here = own_core == 0
    for slot in range(pieces // 2):
        first, second = low[slot, 0], low[slot, 1]
        place = pl.ds(pl.multiple_of((own_slot ^ slot) * rows, rows), rows)
        keep_ref[place, :] = jnp.where(here, first, second)
        send_ref[place, :] = jnp.where(here, second, first)


def grad_dot_kernel(pieces, own_ref, x_ref, dy_ref, keep_ref, send_ref):
    total = dot_tn(x_ref[...], dy_ref[0])
    store_rows(total, own_ref[0], own_ref[1], pieces, keep_ref, send_ref)


def grad_dot(own, x, dy, pieces, name):
    tokens, depth = x.shape
    groups, _, columns = dy.shape
    per = columns // COL_BLOCK
    half = jax.ShapeDtypeStruct((depth // 2, groups * columns), jnp.bfloat16)
    block = pl.BlockSpec((depth // 2, COL_BLOCK), lambda i, own: (0, i))
    return pl.pallas_call(
        partial(grad_dot_kernel, pieces),
        grid_spec=pltpu.PrefetchScalarGridSpec(
            num_scalar_prefetch=1,
            grid=(groups * per,),
            in_specs=[
                pl.BlockSpec((tokens, depth), lambda i, own: (0, 0)),
                pl.BlockSpec((1, tokens, COL_BLOCK), lambda i, own: (i // per, 0, i % per)),
            ],
            out_specs=[block, block],
        ),
        out_shape=[half, half],
        compiler_params=kernel_params(40),
        cost_estimate=cost(groups * tokens * depth * columns, tokens * columns),
        name=name,
    )(own, x, dy)


def feed_forward_kernel(
    depth_pieces,
    unit_pieces,
    own_ref,
    norm_ref,
    grad_ref,
    expand_ref,
    bias_ref,
    shrink_ref,
    branch_ref,
    d_norm_ref,
    keep_e_ref,
    send_e_ref,
    keep_s_ref,
    send_s_ref,
    d_bias_ref,
    norm_t,
    hidden,
    d_pre,
):
    tokens, depth = norm_ref.shape
    units = hidden.shape[1]
    step = pl.program_id(0)
    expand = expand_ref[...].reshape(depth, units)
    shrink = shrink_ref[...].reshape(units, depth)

    @pl.when(step == 0)
    def _():
        norm_t[...] = norm_ref[...].T
        branch_ref[...] = jnp.zeros_like(branch_ref)
        d_norm_ref[...] = jnp.zeros_like(d_norm_ref)

    bias_sum = jnp.zeros((1, units), jnp.float32)
    starts = list(range(0, tokens, ROWS))

    def entering(start):
        rows = slice(start, start + ROWS)
        return dot_nn(norm_ref[rows, :], expand), dot_nt(grad_ref[rows, :], shrink)

    upcoming = entering(starts[0])
    for number, start in enumerate(starts):
        rows = slice(start, start + ROWS)
        pre, d_unit = upcoming
        if number + 1 < len(starts):
            upcoming = entering(starts[number + 1])
        pre = pre + bias_ref[...]
        square = pre * pre
        bend = jnp.tanh(GELU_ROOT * pre * (1.0 + GELU_CUBE * square))
        rise = 0.5 + 0.5 * bend
        unit = (pre * rise).astype(jnp.bfloat16)
        hidden[rows, :] = unit
        slope = rise + 0.5 * pre * (1.0 - bend * bend) * (
            GELU_ROOT + (3.0 * GELU_ROOT * GELU_CUBE) * square
        )
        d_low = (d_unit * slope).astype(jnp.bfloat16)
        d_pre[rows, :] = d_low
        bias_sum = bias_sum + jnp.sum(d_low.astype(jnp.float32), axis=0, keepdims=True)
        branch_ref[rows, :] += dot_nn(unit, shrink)
        d_norm_ref[rows, :] += dot_nt(d_low, expand)
    d_bias_ref[...] = bias_sum
    store_rows(
        dot_tn(hidden[...], grad_ref[...]), own_ref[0], own_ref[3], unit_pieces, keep_s_ref, send_s_ref
    )
    store_rows(
        dot_nn(norm_t[...], d_pre[...]), own_ref[0], own_ref[1], depth_pieces, keep_e_ref, send_e_ref
    )


def feed_forward(own, norm, grad, expand, bias, shrink, half, pieces, name):
    tokens, depth = norm.shape
    depth_pieces, unit_pieces = pieces
    total = bias.shape[1] // 2
    steps = total // FF_BLOCK
    whole = pl.BlockSpec((tokens, depth), lambda i, own: (0, 0))
    half_e = pl.BlockSpec((depth // 2, FF_BLOCK), lambda i, own: (0, i))
    half_s = pl.BlockSpec((FF_BLOCK // 2, depth), lambda i, own: (i, 0))
    if shrink.ndim == 2:
        spec_e = weight_spec(expand, 2 * half, FF_BLOCK, lambda i, own: i)
        spec_s = pl.BlockSpec((FF_BLOCK, depth), lambda i, own: (steps * half + i, 0))
    else:
        devices, blocks, rows, columns = shrink.shape
        shards = devices // 4
        spec_e = weight_spec(expand, 4 + 2 * half, FF_BLOCK, lambda i, own: i)
        shrink = shrink.reshape(shards, 2, 2, blocks, rows, columns)
        spec_s = pl.BlockSpec(
            (shards // steps, 1, 2, 4, rows, columns), lambda i, own: (i, half, 0, 0, 0, 0)
        )
    line = pl.BlockSpec((1, FF_BLOCK), lambda i, own: (0, steps * half + i))
    line_out = pl.BlockSpec((1, FF_BLOCK), lambda i, own: (0, i))
    wide = jax.ShapeDtypeStruct((tokens, depth), jnp.float32)
    out_e = jax.ShapeDtypeStruct((depth // 2, total), jnp.bfloat16)
    out_s = jax.ShapeDtypeStruct((total // 2, depth), jnp.bfloat16)
    return pl.pallas_call(
        partial(feed_forward_kernel, depth_pieces, unit_pieces),
        grid_spec=pltpu.PrefetchScalarGridSpec(
            num_scalar_prefetch=1,
            grid=(steps,),
            in_specs=[whole, whole, spec_e, line, spec_s],
            out_specs=[whole, whole, half_e, half_e, half_s, half_s, line_out],
            scratch_shapes=[
                pltpu.VMEM((depth, tokens), jnp.bfloat16),
                pltpu.VMEM((tokens, FF_BLOCK), jnp.bfloat16),
                pltpu.VMEM((tokens, FF_BLOCK), jnp.bfloat16),
            ],
        ),
        out_shape=[
            wide,
            wide,
            out_e,
            out_e,
            out_s,
            out_s,
            jax.ShapeDtypeStruct((1, total), jnp.float32),
        ],
        compiler_params=kernel_params(56),
        cost_estimate=cost(6 * tokens * depth * total, 16 * 2**20, tokens * total),
        name=name,
    )(own, norm, grad, expand, bias, shrink)


def attention_forward_kernel(q_ref, k_ref, v_ref, out_ref, out_t_ref, lse_ref):
    length = q_ref.shape[0]
    scaled = q_ref[...] * jnp.bfloat16(HEAD_DIM ** (-0.5))
    keys = k_ref[...]
    values_t = v_ref[...].T
    ones = jnp.ones((16, length), jnp.bfloat16)
    extended = [
        jnp.concatenate([values_t[head * HEAD_DIM : (head + 1) * HEAD_DIM], ones], axis=0)
        for head in range(2)
    ]
    tasks = [(start, head) for start in range(0, length, CHUNK) for head in range(2)]

    def scores_of(task):
        start, head = task
        cols = slice(head * HEAD_DIM, (head + 1) * HEAD_DIM)
        return dot_nt(keys[:, cols], scaled[start : start + CHUNK, cols])

    upcoming = scores_of(tasks[0])
    pieces = []
    for number, (start, head) in enumerate(tasks):
        scores = upcoming
        if number + 1 < len(tasks):
            upcoming = scores_of(tasks[number + 1])
        rows = slice(start, start + CHUNK)
        top = jnp.max(scores, axis=0, keepdims=True)
        terms = jnp.exp(scores - top).astype(jnp.bfloat16)
        part = dot_nn(extended[head], terms)
        total = part[HEAD_DIM : HEAD_DIM + 1]
        piece = part[:HEAD_DIM] / total
        lse_ref[0, head : head + 1, rows] = top + jnp.log(total)
        out_t_ref[head * HEAD_DIM : (head + 1) * HEAD_DIM, rows] = piece
        pieces.append(piece)
        if head == 1:
            out_ref[rows, :] = jnp.concatenate(pieces, axis=0).T.astype(jnp.bfloat16)
            pieces = []


def attention_forward(projected):
    length = projected.shape[0]
    pairs = HEADS // 2
    return pl.pallas_call(
        attention_forward_kernel,
        grid=(pairs,),
        in_specs=[
            pl.BlockSpec((length, PAIR), lambda i: (0, i)),
            pl.BlockSpec((length, PAIR), lambda i: (0, pairs + i)),
            pl.BlockSpec((length, PAIR), lambda i: (0, 2 * pairs + i)),
        ],
        out_specs=[
            pl.BlockSpec((length, PAIR), lambda i: (0, i)),
            pl.BlockSpec((PAIR, length), lambda i: (i, 0)),
            pl.BlockSpec((1, 2, length), lambda i: (i, 0, 0)),
        ],
        out_shape=[
            jax.ShapeDtypeStruct((length, HEADS * HEAD_DIM), jnp.bfloat16),
            jax.ShapeDtypeStruct((HEADS * HEAD_DIM, length), jnp.float32),
            jax.ShapeDtypeStruct((pairs, 2, length), jnp.float32),
        ],
        compiler_params=kernel_params(48),
        cost_estimate=cost(2**32, 8 * 2**20, 2**24),
        name="attention_forward",
    )(projected, projected, projected)


def attention_backward_kernel(
    q_ref, k_ref, v_ref, g_ref, o_ref, lse_ref, out_ref, qb_ref, vb_ref, probs, d_scores
):
    length = q_ref.shape[0]
    root = HEAD_DIM ** (-0.5)
    scaled = q_ref[...] * jnp.bfloat16(root)
    keys = k_ref[...]
    values = v_ref[...]
    grads = g_ref[...]
    keys_t = keys.T
    product = grads.T.astype(jnp.float32) * o_ref[...]
    sums_k = [None, None]
    sums_v = [None, None]
    sum_q = None
    pieces = []
    tasks = [(start, head) for start in range(0, length, CHUNK) for head in range(2)]
    for number, (start, head) in enumerate(tasks):
        rows = slice(start, start + CHUNK)
        slot = number % 2
        cols = slice(head * HEAD_DIM, (head + 1) * HEAD_DIM)
        query, grad = scaled[rows, cols], grads[rows, cols]
        lse = lse_ref[0, head : head + 1, rows]
        row_sum = jnp.sum(product[cols, rows], axis=0, keepdims=True)
        for block in range(0, length, KEY_BLOCK):
            some = slice(block, block + KEY_BLOCK)
            prob = jnp.exp(dot_nt(keys[some, cols], query) - lse)
            d_prob = dot_nt(values[some, cols], grad)
            probs[slot, some, :] = prob.astype(jnp.bfloat16)
            d_scores[slot, some, :] = (prob * (d_prob - row_sum)).astype(jnp.bfloat16)
        part_v = dot_nn(probs[slot], grad)
        part_k = dot_nn(d_scores[slot], query)
        sums_v[head] = part_v if start == 0 else sums_v[head] + part_v
        sums_k[head] = part_k if start == 0 else sums_k[head] + part_k
        pieces.append(dot_nn(keys_t[cols, :], d_scores[slot]) * root)
        if head == 1:
            d_query = jnp.concatenate(pieces, axis=0).T.astype(jnp.bfloat16)
            pieces = []
            out_ref[0, rows, :] = d_query
            part_q = jnp.sum(d_query.astype(jnp.float32), axis=0, keepdims=True)
            sum_q = part_q if start == 0 else sum_q + part_q
    out_ref[1] = jnp.concatenate(sums_k, axis=1).astype(jnp.bfloat16)
    d_value = jnp.concatenate(sums_v, axis=1).astype(jnp.bfloat16)
    out_ref[2] = d_value
    qb_ref[...] = sum_q
    vb_ref[...] = jnp.sum(d_value.astype(jnp.float32), axis=0, keepdims=True)


def attention_backward(projected, d_attended, attended_t, lse, first, count, name):
    length = projected.shape[0]
    width = count * PAIR
    pairs = HEADS // 2
    row = pl.BlockSpec((1, PAIR), lambda i: (0, i))
    line = jax.ShapeDtypeStruct((1, width), jnp.float32)
    return pl.pallas_call(
        attention_backward_kernel,
        grid=(count,),
        in_specs=[
            pl.BlockSpec((length, PAIR), lambda i: (0, first + i)),
            pl.BlockSpec((length, PAIR), lambda i: (0, pairs + first + i)),
            pl.BlockSpec((length, PAIR), lambda i: (0, 2 * pairs + first + i)),
            pl.BlockSpec((length, PAIR), lambda i: (0, first + i)),
            pl.BlockSpec((PAIR, length), lambda i: (first + i, 0)),
            pl.BlockSpec((1, 2, length), lambda i: (first + i, 0, 0)),
        ],
        out_specs=[pl.BlockSpec((3, length, PAIR), lambda i: (0, 0, i)), row, row],
        out_shape=[jax.ShapeDtypeStruct((3, length, width), jnp.bfloat16), line, line],
        scratch_shapes=[
            pltpu.VMEM((2, length, CHUNK), jnp.bfloat16),
            pltpu.VMEM((2, length, CHUNK), jnp.bfloat16),
        ],
        compiler_params=kernel_params(48),
        cost_estimate=cost(count * 2**29, count * 2 * 2**20, count * 2**21),
        name=name,
    )(projected, projected, projected, d_attended, attended_t, lse)


def normalize(values):
    average = jnp.mean(values, axis=-1, keepdims=True)
    centred = values - average
    variance = jnp.mean(centred * centred, axis=-1, keepdims=True)
    return centred * lax.rsqrt(variance + EPS_NORM)


def modulate(values, shifts, scales):
    return normalize(values) * (1.0 + scales[:, None, :]) + shifts[:, None, :]


MASKS = {"core": (1, 0), "y": (2, 0), "x": (0, 1), "z1": (0, 2), "z2": (0, 4)}
GATHER_ORDERS = (("z1", "z2", "x", "y"), ("z1", "z2", "y", "x"))


def exchange(value, rep_mask, fsdp_mask):
    reps, shards = lax.axis_size("rep"), lax.axis_size("fsdp")
    pairs = [
        (rep * shards + shard, (rep ^ rep_mask) * shards + (shard ^ fsdp_mask))
        for rep in range(reps)
        for shard in range(shards)
    ]
    return lax.ppermute(value, ("rep", "fsdp"), pairs)


def gather_relative(row):
    reps, shards = lax.axis_size("rep"), lax.axis_size("fsdp")
    masks = [(0, 1 << bit) for bit in reversed(range(shards.bit_length() - 1))]
    masks += [(1 << bit, 0) for bit in reversed(range(reps.bit_length() - 1))]
    rows = row[None]
    for pair in masks:
        rows = jnp.stack([rows, exchange(rows, *pair)], axis=1).reshape(-1, *row.shape)
    return rows


def gather_chain(quarter, order):
    rows = quarter[None]
    for name in order:
        rows = jnp.concatenate([rows, exchange(rows, *MASKS[name])], axis=0)
    return rows, exchange(rows, *MASKS["core"])


def chain_map(order):
    offsets = [0]
    for name in order:
        rep_mask, fsdp_mask = MASKS[name]
        offsets += [offset ^ (fsdp_mask * 4 + rep_mask) for offset in offsets]
    return tuple(offsets)


def to_absolute(parts, own):
    parts = list(parts)
    bit = 1
    while bit < len(parts):
        flipped = (own & bit) != 0
        parts = [jnp.where(flipped, parts[i ^ bit], parts[i]) for i in range(len(parts))]
        bit *= 2
    return parts


class HalvingSum:
    def __init__(self, keep, send, order):
        rows, columns = keep.shape[0] // 16, keep.shape[1]
        self.shape = (2, 2, 2, 2, rows, columns)
        self.axes = ["z2", "z1", "x", "y"]
        self.order = list(order)
        self.stay = keep.reshape(self.shape)
        self.arrived = exchange(send, *MASKS["core"])

    def half(self, axis, side):
        stay = lax.index_in_dim(self.stay, side, axis, keepdims=False)
        arrived = lax.index_in_dim(self.arrived.reshape(self.stay.shape), side, axis, keepdims=False)
        return (stay.astype(jnp.float32) + arrived.astype(jnp.float32)).astype(jnp.bfloat16)

    def step(self):
        name = self.order.pop(0)
        axis = self.axes.index(name)
        self.axes.pop(axis)
        away, stay = self.half(axis, 1), self.half(axis, 0)
        self.stay, self.arrived = stay, exchange(away, *MASKS[name])

    def finish(self):
        while self.order:
            self.step()
        own = self.stay.astype(jnp.float32) + self.arrived.reshape(self.stay.shape).astype(jnp.float32)
        return gather_reps(own.astype(jnp.bfloat16))


def gather_reps(own):
    pair = [own, exchange(own, *MASKS["core"])]
    other = exchange(jnp.stack(pair), *MASKS["y"])
    parts = to_absolute([*pair, other[0], other[1]], lax.axis_index("rep"))
    return jnp.concatenate(parts, axis=0).astype(jnp.float32)


class GroupSum:
    def __init__(self, keep, send):
        self.keep = keep
        self.arrived = exchange(send, *MASKS["core"])

    def step(self):
        total = self.keep.astype(jnp.float32) + self.arrived.astype(jnp.float32)
        self.arrived = total.astype(jnp.bfloat16)

    def launch(self):
        shards = lax.axis_size("fsdp")
        groups = [
            [(2 * y + core) * shards + shard for shard in range(shards) for y in range(2)]
            for core in range(2)
        ]
        self.arrived = lax.psum_scatter(
            self.arrived, ("rep", "fsdp"), scatter_dimension=0, axis_index_groups=groups, tiled=True
        )

    def finish(self):
        return gather_reps(self.arrived)


class PlainSum:
    def __init__(self, grad):
        self.arrived = grad

    def step(self):
        pass

    def launch(self):
        pass

    def finish(self):
        return scatter_rows(self.arrived)


def hold(value, *sums):
    held = lax.optimization_barrier((value, *[total.arrived for total in sums]))
    for total, arrived in zip(sums, held[1:]):
        total.arrived = arrived
    return held[0]


def scatter_rows(grad):
    own = lax.psum_scatter(grad, ("fsdp", "rep"), scatter_dimension=0, tiled=True)
    return lax.all_gather(own, "rep", axis=0, tiled=True).astype(jnp.float32)


def own_quarter(weight):
    part = weight.shape[0] // lax.axis_size("rep")
    return lax.dynamic_slice_in_dim(weight, lax.axis_index("rep") * part, part, 0)


def gather_rows(weight):
    return lax.all_gather(own_quarter(weight), ("fsdp", "rep"), axis=0, tiled=True)


def by_half(columns):
    rows, count = columns.shape
    split = columns.reshape(rows, UNIT_SHARDS, 2, count // (2 * UNIT_SHARDS))
    return split.transpose(0, 2, 1, 3).reshape(rows, count)


def undo_by_half(first, second):
    rows, count = first.shape
    split = [half.reshape(rows, UNIT_SHARDS, count // UNIT_SHARDS) for half in (first, second)]
    return jnp.stack(split, axis=2).reshape(rows, 2 * count)


def column_blocks(quarter, width):
    rows = quarter.shape[0]
    blocks = quarter.shape[1] // width
    return quarter.reshape(rows, blocks, width).transpose(1, 0, 2).reshape(blocks * rows, width)


def gather_packed(parts, rows):
    packed = jnp.concatenate(parts, axis=0)
    blocks, width = packed.shape[0] // rows, packed.shape[1]
    full = lax.all_gather(packed, ("fsdp", "rep"), axis=0, tiled=True)
    return full.reshape(full.shape[0] // packed.shape[0], blocks, rows, width)


def on_device(
    latents,
    conditions,
    modulator,
    modulbias,
    projector,
    querybias,
    valuebias,
    outweight,
    outbiases,
    expander,
    expandbias,
    shrinker,
    shrinkbias,
    upstream,
):
    seqs_dev, seq_len, feature = latents.shape
    token_count = seqs_dev * seq_len
    shard_id, rep_id = lax.axis_index("fsdp"), lax.axis_index("rep")
    shards, reps = lax.axis_size("fsdp"), lax.axis_size("rep")
    halving = shards == 8 and reps == 4
    own_rows = modulator.shape[0]
    own_bias = modulbias.shape[0]

    width = projector.shape[1]
    if halving:
        quarter = own_rows // reps
        proj_quarter = own_quarter(projector)
        chains = [
            gather_chain(proj_quarter[:, part * (width // 2) : (part + 1) * (width // 2)], order)
            for part, order in enumerate(GATHER_ORDERS)
        ]
        maps = [chain_map(order) for order in GATHER_ORDERS]
        packed = gather_packed(
            [
                own_quarter(shrinker),
                column_blocks(by_half(own_quarter(expander)), feature),
                own_quarter(outweight),
            ],
            quarter,
        )
        out_at = (packed, 8)
        w_expand, w_shrink = packed, packed
        depth_pieces, unit_pieces = shards * reps, 2 * reps
        own_core = jnp.stack([rep_id & 1] + [jnp.zeros_like(rep_id)] * 3).astype(jnp.int32)
        own = jnp.stack(
            [rep_id & 1, shard_id * 2 + (rep_id >> 1), shard_id, rep_id >> 1]
        ).astype(jnp.int32)
    else:
        w_proj, out_at = gather_rows(projector), (gather_rows(outweight), 0)
        w_expand = by_half(gather_rows(expander))
        w_shrink = by_half(gather_rows(shrinker).T).T
        depth_pieces, unit_pieces = 2, 2
        own = own_core = jnp.zeros((4,), jnp.int32)

    def depth_sum(halves, order=None):
        if halving:
            return HalvingSum(*halves, order) if order else GroupSum(*halves)
        return PlainSum(jnp.concatenate(halves, axis=0))

    def unit_sum(halves):
        if halving:
            return GroupSum(*halves)
        blocks = [half.reshape(-1, 1, FF_BLOCK // 2, feature) for half in halves]
        return PlainSum(jnp.concatenate(blocks, axis=1).reshape(-1, feature))

    cond_full = conditions.astype(jnp.float32)
    cond_slice = lax.dynamic_slice_in_dim(cond_full, shard_id * own_rows, own_rows, 1)
    cond_act = jax.nn.silu(cond_slice).astype(jnp.bfloat16)
    cond_own = lax.dynamic_slice_in_dim(cond_full, shard_id * seqs_dev, seqs_dev, 0)
    cond_own = jax.nn.silu(cond_own).astype(jnp.bfloat16)
    mod_term = jnp.dot(cond_act, modulator, preferred_element_type=jnp.float32)
    bias_parts = (modulbias, querybias, valuebias, outbiases, expandbias, shrinkbias)
    own_biases = jnp.concatenate([part.astype(jnp.float32) for part in bias_parts])
    mod_width = seqs_dev * 6 * feature
    sent = jnp.concatenate(
        [
            mod_term.reshape(shards, mod_width),
            jnp.broadcast_to(own_biases[None, :], (shards, own_biases.shape[0])),
        ],
        axis=1,
    )
    got = lax.all_to_all(sent, "fsdp", split_axis=0, concat_axis=0, tiled=True)
    full_biases = []
    start = mod_width
    for part in bias_parts:
        full_biases.append(got[:, start : start + part.shape[0]].reshape(1, -1))
        start += part.shape[0]
    full_modbias, b_query, b_value, b_out, b_expand, b_shrink = full_biases
    modvals = jnp.sum(got[:, :mod_width], axis=0).reshape(seqs_dev, 6, feature)
    modvals = modvals + full_modbias.reshape(1, 6, feature)
    shift_a, scale_a, gate_a = (modvals[:, 0], modvals[:, 1], modvals[:, 2])
    shift_m, scale_m, gate_m = (modvals[:, 3], modvals[:, 4], modvals[:, 5])

    resid_in = latents.astype(jnp.float32)
    norm_a = modulate(resid_in, shift_a, scale_a).astype(jnp.bfloat16).reshape(token_count, feature)
    b_proj = jnp.concatenate([b_query, jnp.zeros_like(b_query), b_value], axis=1)
    if halving:
        flat = (shard_id * reps + rep_id).astype(jnp.int32)[None]
        projected, w_proj = project(flat, norm_a, b_proj, chains, maps)
    else:
        projected = forward_dot(norm_a, w_proj, 0, b_proj, jnp.bfloat16, "project")
    attended, attended_t, log_totals = attention_forward(projected)
    branch_a = forward_dot(attended, *out_at, b_out, jnp.float32, "attention_out")
    branch_a = branch_a.reshape(seqs_dev, seq_len, feature)
    middle = resid_in + gate_a[:, None, :] * branch_a
    norm_m = modulate(middle, shift_m, scale_m).astype(jnp.bfloat16).reshape(token_count, feature)

    grad_out = upstream.astype(jnp.float32)
    d_branch_m = (gate_m[:, None, :] * grad_out).astype(jnp.bfloat16).reshape(token_count, feature)
    g_shrinkbias = jnp.sum(d_branch_m, axis=0, dtype=jnp.float32)
    b_units = by_half(b_expand)
    branch_parts, norm_parts, bias_parts, sums_e, sums_s = [], [], [], [], []
    norm_now = norm_m
    for half in range(2):
        branch, d_norm, keep_e, send_e, keep_s, send_s, d_bias = feed_forward(
            own_core,
            norm_now,
            d_branch_m,
            w_expand,
            b_units,
            w_shrink,
            half,
            (depth_pieces, unit_pieces),
            ("feed_forward_low", "feed_forward_high")[half],
        )
        branch_parts.append(branch)
        norm_parts.append(d_norm)
        bias_parts.append(d_bias)
        sum_e, sum_s = depth_sum((keep_e, send_e)), unit_sum((keep_s, send_s))
        sums_e.append(sum_e)
        sums_s.append(sum_s)
        sum_e.step()
        sum_s.step()
        if half == 0:
            norm_now = hold(norm_m, sum_e, sum_s)
            sum_e.launch()
            sum_s.launch()
    g_expandbias = undo_by_half(*bias_parts)
    d_norm_m = norm_parts[0] + norm_parts[1]
    branch_m = branch_parts[0] + branch_parts[1] + b_shrink
    branch_m = branch_m.reshape(seqs_dev, seq_len, feature)
    layer_out = middle + gate_m[:, None, :] * branch_m
    d_gate_m = jnp.sum(grad_out * branch_m, axis=1)
    _, norm_pull_m = jax.vjp(modulate, middle, shift_m, scale_m)
    d_mid_norm, d_shift_m, d_scale_m = norm_pull_m(d_norm_m.reshape(seqs_dev, seq_len, feature))
    d_middle = grad_out + d_mid_norm
    d_branch_a = (gate_a[:, None, :] * d_middle).astype(jnp.bfloat16).reshape(token_count, feature)
    d_gate_a = jnp.sum(d_middle * branch_a, axis=1)
    g_outbiases = jnp.sum(d_branch_a, axis=0, dtype=jnp.float32)
    d_attended = backward_dot(d_branch_a, *out_at, jnp.bfloat16, "attention_out_back")
    sum_e, sum_s = sums_e[1], sums_s[1]
    d_attended = hold(d_attended, sum_e, sum_s)
    sum_e.launch()
    sum_s.launch()
    half_pairs = HEADS // 4
    d_low, q_low, v_low = attention_backward(
        projected, d_attended, attended_t, log_totals, 0, half_pairs, "attention_backward_low"
    )
    sum_out = depth_sum(
        grad_dot(own_core, attended, d_branch_a[None], depth_pieces, "outweight_grad")
    )
    sum_low = depth_sum(grad_dot(own_core, norm_a, d_low, depth_pieces, "projector_grad_low"))
    d_attended = hold(d_attended, sum_low, sum_out)
    d_high, q_high, v_high = attention_backward(
        projected, d_attended, attended_t, log_totals, half_pairs, half_pairs, "attention_backward_high"
    )
    sum_out.step()
    sum_low.step()
    d_high = hold(d_high, sum_low, sum_out)
    sum_out.launch()
    sum_low.launch()
    sum_high = depth_sum(
        grad_dot(own, norm_a, d_high, depth_pieces, "projector_grad_high"), ("y", "x", "z2", "z1")
    )
    d_norm_a = project_back(d_low, d_high, w_proj)
    d_norm_a = hold(d_norm_a, sum_high)
    sum_high.step()
    g_querybias = jnp.concatenate([q_low, q_high], axis=1)
    g_valuebias = jnp.concatenate([v_low, v_high], axis=1)
    _, norm_pull_a = jax.vjp(modulate, resid_in, shift_a, scale_a)
    d_in_norm, d_shift_a, d_scale_a = norm_pull_a(d_norm_a.reshape(seqs_dev, seq_len, feature))
    latents_grad = d_middle + d_in_norm
    small = jnp.concatenate(
        [
            part.astype(jnp.bfloat16).reshape(-1)
            for part in (
                d_shift_a,
                d_scale_a,
                d_gate_a,
                d_shift_m,
                d_scale_m,
                d_gate_m,
                cond_own,
                g_querybias,
                g_valuebias,
                g_outbiases,
                g_expandbias,
                g_shrinkbias,
            )
        ]
    )
    devices = reps * shards
    size = seqs_dev * feature
    gathered = gather_relative(small.reshape(-1, 128)).reshape(devices, -1)
    g_expander = undo_by_half(sums_e[0].finish(), sums_e[1].finish())
    if halving:
        g_shrinker = jnp.concatenate([sums_s[0].finish(), sums_s[1].finish()], axis=0)
    else:
        units = [total.arrived.reshape(UNIT_SHARDS, 1, -1, feature) for total in sums_s]
        g_shrinker = scatter_rows(jnp.concatenate(units, axis=1).reshape(-1, feature))
    g_outweight = sum_out.finish()
    low, high = sum_low.finish(), sum_high.finish()
    g_projector = jnp.stack(
        [low.reshape(own_rows, 3, feature // 2), high.reshape(own_rows, 3, feature // 2)], axis=2
    ).reshape(own_rows, 3 * feature)

    cond_all = gathered[:, 6 * size : 7 * size].reshape(devices * seqs_dev, feature)
    cond_all = lax.dynamic_slice_in_dim(cond_all, shard_id * own_rows, own_rows, 1)
    d_mod = gathered[:, : 6 * size]
    d_mod = d_mod.reshape(devices, 6, seqs_dev, feature).transpose(0, 2, 1, 3)
    d_mod = d_mod.reshape(devices * seqs_dev, 6 * feature)
    bias_grads = []
    start = 7 * size
    for total in (feature, feature, feature, expandbias.shape[0] * shards, feature):
        part = total // shards
        own_part = lax.dynamic_slice_in_dim(gathered, start + shard_id * part, part, 1)
        bias_grads.append(jnp.sum(own_part, axis=0, dtype=jnp.float32))
        start += total
    g_modbias = jnp.sum(
        lax.dynamic_slice_in_dim(d_mod, shard_id * own_bias, own_bias, 1), axis=0, dtype=jnp.float32
    )
    g_modulator = jnp.einsum("sr,sc->rc", cond_all, d_mod, preferred_element_type=jnp.float32)
    own_mod = d_mod.reshape(shards, reps, seqs_dev, 6 * feature)[:, 0].reshape(-1, 6 * feature)
    d_cond_act = jnp.einsum("sc,rc->sr", own_mod, modulator, preferred_element_type=jnp.float32)
    d_cond_act = jnp.stack(to_absolute(d_cond_act.reshape(shards, seqs_dev, own_rows), shard_id))
    d_cond_act = d_cond_act.reshape(shards * seqs_dev, own_rows)
    _, silu_pull = jax.vjp(jax.nn.silu, cond_slice)
    conditions_grad = silu_pull(d_cond_act)[0]
    return (
        layer_out,
        latents_grad,
        conditions_grad,
        g_modulator,
        g_modbias,
        g_projector,
        bias_grads[0],
        bias_grads[1],
        g_outweight,
        bias_grads[2],
        g_expander,
        bias_grads[3],
        g_shrinker,
        bias_grads[4],
    )


def solution(mesh):
    return jax.shard_map(
        on_device,
        mesh=mesh,
        in_specs=(
            P(("rep", "fsdp"), None, None),
            P("rep", None),
            P("fsdp", None),
            P("fsdp"),
            P("fsdp", None),
            P("fsdp"),
            P("fsdp"),
            P("fsdp", None),
            P("fsdp"),
            P("fsdp", None),
            P("fsdp"),
            P("fsdp", None),
            P("fsdp"),
            P(("rep", "fsdp"), None, None),
        ),
        out_specs=(
            P(("rep", "fsdp"), None, None),
            P(("rep", "fsdp"), None, None),
            P("rep", "fsdp"),
            P("fsdp", None),
            P("fsdp"),
            P("fsdp", None),
            P("fsdp"),
            P("fsdp"),
            P("fsdp", None),
            P("fsdp"),
            P("fsdp", None),
            P("fsdp"),
            P("fsdp", None),
            P("fsdp"),
        ),
        check_vma=False,
    )
```

```python
from functools import partial

import jax
import jax.numpy as jnp
from jax import lax
from jax.experimental import pallas as pl
from jax.experimental.pallas import tpu as pltpu
from jax.sharding import PartitionSpec as P

HEADS = 16
HEAD_DIM = 64
PAIR = 2 * HEAD_DIM
CHUNK = 256
KEY_BLOCK = 128
NORM_ROWS = 128
EPS_NORM = 1e-06
ROWS = 512
FF_BLOCK = 512
COL_BLOCK = 512
GELU_ROOT = 0.7978845608028654
GELU_CUBE = 0.044715


def dot_nn(left, right):
    return jnp.dot(left, right, preferred_element_type=jnp.float32)


def dot_nt(left, right):
    return lax.dot_general(left, right, (((1,), (1,)), ((), ())), preferred_element_type=jnp.float32)


def dot_tn(left, right):
    return lax.dot_general(left, right, (((0,), (0,)), ((), ())), preferred_element_type=jnp.float32)


def kernel_params(mebibytes):
    return pltpu.CompilerParams(vmem_limit_bytes=mebibytes * 2**20)


def cost(flops, moved, special=0):
    return pl.CostEstimate(flops=flops, bytes_accessed=moved, transcendentals=special)


def weight_spec(weight, first, width, order):
    if weight.ndim == 2:
        offset = first * weight.shape[0] // width
        return pl.BlockSpec((weight.shape[0], width), lambda *at: (0, offset + order(*at)))
    devices, _, rows, columns = weight.shape
    per = columns // width
    return pl.BlockSpec(
        (devices, 1, rows, width),
        lambda *at: (0, first + order(*at) // per, 0, order(*at) % per),
    )


def forward_dot_kernel(x_ref, w_ref, b_ref, out_ref):
    weight = w_ref[...].reshape(x_ref.shape[1], out_ref.shape[1])
    out_ref[...] = (dot_nn(x_ref[...], weight) + b_ref[...]).astype(out_ref.dtype)


def forward_dot(x, weight, first, bias, dtype, name):
    tokens, depth = x.shape
    columns = bias.shape[1]
    return pl.pallas_call(
        forward_dot_kernel,
        grid=(columns // COL_BLOCK,),
        in_specs=[
            pl.BlockSpec((tokens, depth), lambda i: (0, 0)),
            weight_spec(weight, first, COL_BLOCK, lambda i: i),
            pl.BlockSpec((1, COL_BLOCK), lambda i: (0, i)),
        ],
        out_specs=pl.BlockSpec((tokens, COL_BLOCK), lambda i: (0, i)),
        out_shape=jax.ShapeDtypeStruct((tokens, columns), dtype),
        compiler_params=kernel_params(40),
        cost_estimate=cost(tokens * depth * columns, tokens * columns),
        name=name,
    )(x, weight, bias)


def project_kernel(maps, own_ref, x_ref, b_ref, *refs):
    sources, (out_ref, full_ref) = refs[:4], refs[4:]
    step = pl.program_id(0)
    rows = sources[0].shape[1]
    half = pl.num_programs(0) // 2
    for chain in range(2):

        @pl.when((step >= half) == (chain == 1))
        def _():
            for flip in range(2):
                source = sources[2 * chain + flip]
                for index, relative in enumerate(maps[chain]):
                    place = pl.multiple_of((own_ref[0] ^ (relative ^ flip)) * rows, rows)
                    full_ref[pl.ds(place, rows), :] = source[index]

    out_ref[...] = (dot_nn(x_ref[...], full_ref[...]) + b_ref[...]).astype(out_ref.dtype)


def project(flat, x, bias, chains, maps):
    tokens, depth = x.shape
    columns = bias.shape[1]
    steps = columns // COL_BLOCK
    half = steps // 2
    blocks, rows, _ = chains[0][0].shape
    first = pl.BlockSpec((blocks, rows, COL_BLOCK), lambda i, own: (0, 0, jnp.minimum(i, half - 1)))
    second = pl.BlockSpec((blocks, rows, COL_BLOCK), lambda i, own: (0, 0, jnp.maximum(i - half, 0)))
    return pl.pallas_call(
        partial(project_kernel, maps),
        grid_spec=pltpu.PrefetchScalarGridSpec(
            num_scalar_prefetch=1,
            grid=(steps,),
            in_specs=[
                pl.BlockSpec((tokens, depth), lambda i, own: (0, 0)),
                pl.BlockSpec((1, COL_BLOCK), lambda i, own: (0, i)),
                first,
                first,
                second,
                second,
            ],
            out_specs=[
                pl.BlockSpec((tokens, COL_BLOCK), lambda i, own: (0, i)),
                pl.BlockSpec((depth, COL_BLOCK), lambda i, own: (0, i)),
            ],
        ),
        out_shape=[
            jax.ShapeDtypeStruct((tokens, columns), jnp.bfloat16),
            jax.ShapeDtypeStruct((depth, columns), jnp.bfloat16),
        ],
        compiler_params=kernel_params(40),
        cost_estimate=cost(tokens * depth * columns, tokens * columns),
        name="project",
    )(flat, x, bias, *chains[0], *chains[1])


def backward_dot_kernel(dy_ref, w_ref, out_ref, sum_ref):
    step = pl.program_id(0)
    weight = w_ref[...].reshape(out_ref.shape[1], w_ref.shape[-1])
    part = dot_nt(dy_ref[...], weight)

    @pl.when(step == 0)
    def _():
        sum_ref[...] = part

    @pl.when(step > 0)
    def _():
        sum_ref[...] += part

    @pl.when(step == pl.num_programs(0) - 1)
    def _():
        out_ref[...] = sum_ref[...].astype(out_ref.dtype)


def backward_dot(dy, weight, first, dtype, name):
    tokens, columns = dy.shape
    depth = columns
    return pl.pallas_call(
        backward_dot_kernel,
        grid=(columns // COL_BLOCK,),
        in_specs=[
            pl.BlockSpec((tokens, COL_BLOCK), lambda i: (0, i)),
            weight_spec(weight, first, COL_BLOCK, lambda i: i),
        ],
        out_specs=pl.BlockSpec((tokens, depth), lambda i: (0, 0)),
        out_shape=jax.ShapeDtypeStruct((tokens, depth), dtype),
        scratch_shapes=[pltpu.VMEM((tokens, depth), jnp.float32)],
        compiler_params=kernel_params(40),
        cost_estimate=cost(tokens * depth * columns, tokens * columns),
        name=name,
    )(dy, weight)


def project_back_kernel(
    low_ref, high_ref, w_ref, x_ref, scale_ref, carry_ref, out_ref, shift_sum_ref, scale_sum_ref, total
):
    step = pl.program_id(0)

    @pl.when(step == 0)
    def _():
        total[...] = dot_nt(low_ref[0], w_ref[...])

    @pl.when((step > 0) & (step % 2 == 0))
    def _():
        total[...] += dot_nt(low_ref[0], w_ref[...])

    @pl.when(step % 2 == 1)
    def _():
        total[...] += dot_nt(high_ref[0], w_ref[...])

    @pl.when(step == pl.num_programs(0) - 1)
    def _():
        gain = 1.0 + scale_ref[...]
        shift_sum = jnp.zeros(gain.shape, jnp.float32)
        scale_sum = jnp.zeros(gain.shape, jnp.float32)
        for start in range(0, x_ref.shape[0], NORM_ROWS):
            rows = slice(start, start + NORM_ROWS)
            values = x_ref[rows, :].astype(jnp.float32)
            centred = values - jnp.mean(values, axis=-1, keepdims=True)
            variance = jnp.mean(centred * centred, axis=-1, keepdims=True)
            inverse = lax.rsqrt(variance + EPS_NORM)
            normal = centred * inverse
            grad = total[rows, :]
            shift_sum += jnp.sum(grad, axis=0, keepdims=True)
            scale_sum += jnp.sum(grad * normal, axis=0, keepdims=True)
            inner = grad * gain
            average = jnp.mean(inner, axis=-1, keepdims=True)
            along = jnp.mean(inner * normal, axis=-1, keepdims=True)
            out_ref[rows, :] = carry_ref[rows, :] + inverse * (inner - average - normal * along)
        shift_sum_ref[...] = shift_sum
        scale_sum_ref[...] = scale_sum


def project_back(low, high, weight, x, scale, carry):
    groups, tokens, width = low.shape
    depth = weight.shape[0]
    block = pl.BlockSpec((1, tokens, width), lambda i: (i // 2, 0, 0))
    whole = pl.BlockSpec((tokens, depth), lambda i: (0, 0))
    line = pl.BlockSpec((1, depth), lambda i: (0, 0))
    row = jax.ShapeDtypeStruct((1, depth), jnp.float32)
    return pl.pallas_call(
        project_back_kernel,
        grid=(2 * groups,),
        in_specs=[
            block,
            block,
            pl.BlockSpec((depth, width), lambda i: (0, i)),
            whole,
            line,
            whole,
        ],
        out_specs=[whole, line, line],
        out_shape=[jax.ShapeDtypeStruct((tokens, depth), jnp.float32), row, row],
        scratch_shapes=[pltpu.VMEM((tokens, depth), jnp.float32)],
        compiler_params=kernel_params(48),
        cost_estimate=cost(groups * tokens * depth * width, tokens * width),
        name="project_back",
    )(low, high, weight, x, scale, carry)


def store_rows(total, own_core, own_slot, pieces, keep_ref, send_ref):
    rows = total.shape[0] // pieces
    low = total.astype(jnp.bfloat16).reshape(pieces // 2, 2, rows, total.shape[1])
    here = own_core == 0
    for slot in range(pieces // 2):
        first, second = low[slot, 0], low[slot, 1]
        place = pl.ds(pl.multiple_of((own_slot ^ slot) * rows, rows), rows)
        keep_ref[place, :] = jnp.where(here, first, second)
        send_ref[place, :] = jnp.where(here, second, first)


def grad_dot_kernel(pieces, own_ref, x_ref, dy_ref, keep_ref, send_ref):
    total = dot_tn(x_ref[...], dy_ref[0])
    store_rows(total, own_ref[0], own_ref[1], pieces, keep_ref, send_ref)


def grad_dot(own, x, dy, pieces, name):
    tokens, depth = x.shape
    groups, _, columns = dy.shape
    per = columns // COL_BLOCK
    half = jax.ShapeDtypeStruct((depth // 2, groups * columns), jnp.bfloat16)
    block = pl.BlockSpec((depth // 2, COL_BLOCK), lambda i, own: (0, i))
    return pl.pallas_call(
        partial(grad_dot_kernel, pieces),
        grid_spec=pltpu.PrefetchScalarGridSpec(
            num_scalar_prefetch=1,
            grid=(groups * per,),
            in_specs=[
                pl.BlockSpec((tokens, depth), lambda i, own: (0, 0)),
                pl.BlockSpec((1, tokens, COL_BLOCK), lambda i, own: (i // per, 0, i % per)),
            ],
            out_specs=[block, block],
        ),
        out_shape=[half, half],
        compiler_params=kernel_params(40),
        cost_estimate=cost(groups * tokens * depth * columns, tokens * columns),
        name=name,
    )(own, x, dy)


def grad_pair_kernel(pieces, first, own_ref, x_ref, dx_ref, y_ref, dy_ref, keep_ref, send_ref):
    step = pl.program_id(0)

    @pl.when(step < first)
    def _():
        total = dot_tn(x_ref[...], dx_ref[...])
        store_rows(total, own_ref[0], own_ref[1], pieces, keep_ref, send_ref)

    @pl.when(step >= first)
    def _():
        total = dot_tn(y_ref[...], dy_ref[0])
        store_rows(total, own_ref[0], own_ref[1], pieces, keep_ref, send_ref)


def grad_pair(own, x, dx, y, dy, pieces, name):
    tokens, depth = x.shape
    first = dx.shape[1] // COL_BLOCK
    groups = dy.shape[0]
    columns = dx.shape[1] + groups * COL_BLOCK
    whole = pl.BlockSpec((tokens, depth), lambda i, own: (0, 0))
    block = pl.BlockSpec((depth // 2, COL_BLOCK), lambda i, own: (0, i))
    half = jax.ShapeDtypeStruct((depth // 2, columns), jnp.bfloat16)
    return pl.pallas_call(
        partial(grad_pair_kernel, pieces, first),
        grid_spec=pltpu.PrefetchScalarGridSpec(
            num_scalar_prefetch=1,
            grid=(first + groups,),
            in_specs=[
                whole,
                pl.BlockSpec((tokens, COL_BLOCK), lambda i, own: (0, jnp.minimum(i, first - 1))),
                whole,
                pl.BlockSpec(
                    (1, tokens, COL_BLOCK), lambda i, own: (jnp.maximum(i - first, 0), 0, 0)
                ),
            ],
            out_specs=[block, block],
        ),
        out_shape=[half, half],
        compiler_params=kernel_params(40),
        cost_estimate=cost(tokens * depth * columns, tokens * columns),
        name=name,
    )(own, x, dx, y, dy)


def feed_forward_kernel(
    depth_pieces,
    unit_pieces,
    own_ref,
    norm_ref,
    grad_ref,
    expand_ref,
    bias_ref,
    shrink_ref,
    branch_ref,
    d_norm_ref,
    keep_e_ref,
    send_e_ref,
    keep_s_ref,
    send_s_ref,
    d_bias_ref,
    norm_t,
    hidden,
    d_pre,
):
    tokens, depth = norm_ref.shape
    units = hidden.shape[1]
    step = pl.program_id(0)
    expand = expand_ref[...].reshape(depth, units)
    shrink = shrink_ref[...].reshape(units, depth)

    @pl.when(step == 0)
    def _():
        norm_t[...] = norm_ref[...].T
        branch_ref[...] = jnp.zeros_like(branch_ref)
        d_norm_ref[...] = jnp.zeros_like(d_norm_ref)

    bias_sum = jnp.zeros((1, units), jnp.float32)
    starts = list(range(0, tokens, ROWS))

    def entering(start):
        rows = slice(start, start + ROWS)
        return dot_nn(norm_ref[rows, :], expand), dot_nt(grad_ref[rows, :], shrink)

    upcoming = entering(starts[0])
    for number, start in enumerate(starts):
        rows = slice(start, start + ROWS)
        pre, d_unit = upcoming
        if number + 1 < len(starts):
            upcoming = entering(starts[number + 1])
        pre = pre + bias_ref[...]
        square = pre * pre
        bend = jnp.tanh(GELU_ROOT * pre * (1.0 + GELU_CUBE * square))
        rise = 0.5 + 0.5 * bend
        unit = (pre * rise).astype(jnp.bfloat16)
        hidden[rows, :] = unit
        slope = rise + 0.5 * pre * (1.0 - bend * bend) * (
            GELU_ROOT + (3.0 * GELU_ROOT * GELU_CUBE) * square
        )
        d_low = (d_unit * slope).astype(jnp.bfloat16)
        d_pre[rows, :] = d_low
        bias_sum = bias_sum + jnp.sum(d_low.astype(jnp.float32), axis=0, keepdims=True)
        branch_ref[rows, :] += dot_nn(unit, shrink)
        d_norm_ref[rows, :] += dot_nt(d_low, expand)
    d_bias_ref[...] = bias_sum
    store_rows(
        dot_tn(hidden[...], grad_ref[...]), own_ref[0], own_ref[3], unit_pieces, keep_s_ref, send_s_ref
    )
    store_rows(
        dot_nn(norm_t[...], d_pre[...]), own_ref[0], own_ref[1], depth_pieces, keep_e_ref, send_e_ref
    )


def feed_forward(own, norm, grad, expand, bias, shrink, depth_pieces, unit_pieces):
    tokens, depth = norm.shape
    total = bias.shape[1]
    steps = total // FF_BLOCK
    whole = pl.BlockSpec((tokens, depth), lambda i, own: (0, 0))
    half_e = pl.BlockSpec((depth // 2, FF_BLOCK), lambda i, own: (0, i))
    half_s = pl.BlockSpec((FF_BLOCK // 2, depth), lambda i, own: (i ^ own[2], 0))
    line = pl.BlockSpec((1, FF_BLOCK), lambda i, own: (0, i))
    if shrink.ndim == 2:
        spec_e = weight_spec(expand, 0, FF_BLOCK, lambda i, own: i)
        spec_s = pl.BlockSpec((FF_BLOCK, depth), lambda i, own: (i, 0))
    else:
        devices, blocks, rows, columns = shrink.shape
        spec_e = weight_spec(expand, 4, FF_BLOCK, lambda i, own: i)
        spec_s = pl.BlockSpec((devices // steps, 4, rows, columns), lambda i, own: (i, 0, 0, 0))
    wide = jax.ShapeDtypeStruct((tokens, depth), jnp.float32)
    out_e = jax.ShapeDtypeStruct((depth // 2, total), jnp.bfloat16)
    out_s = jax.ShapeDtypeStruct((total // 2, depth), jnp.bfloat16)
    return pl.pallas_call(
        partial(feed_forward_kernel, depth_pieces, unit_pieces),
        grid_spec=pltpu.PrefetchScalarGridSpec(
            num_scalar_prefetch=1,
            grid=(steps,),
            in_specs=[whole, whole, spec_e, line, spec_s],
            out_specs=[whole, whole, half_e, half_e, half_s, half_s, line],
            scratch_shapes=[
                pltpu.VMEM((depth, tokens), jnp.bfloat16),
                pltpu.VMEM((tokens, FF_BLOCK), jnp.bfloat16),
                pltpu.VMEM((tokens, FF_BLOCK), jnp.bfloat16),
            ],
        ),
        out_shape=[
            wide,
            wide,
            out_e,
            out_e,
            out_s,
            out_s,
            jax.ShapeDtypeStruct((1, total), jnp.float32),
        ],
        compiler_params=kernel_params(56),
        cost_estimate=cost(6 * tokens * depth * total, 16 * 2**20, tokens * total),
        name="feed_forward",
    )(own, norm, grad, expand, bias, shrink)


def attention_forward_kernel(q_ref, k_ref, v_ref, out_ref, out_t_ref, lse_ref):
    length = q_ref.shape[0]
    scaled = q_ref[...] * jnp.bfloat16(HEAD_DIM ** (-0.5))
    keys = k_ref[...]
    values_t = v_ref[...].T
    ones = jnp.ones((16, length), jnp.bfloat16)
    extended = [
        jnp.concatenate([values_t[head * HEAD_DIM : (head + 1) * HEAD_DIM], ones], axis=0)
        for head in range(2)
    ]
    tasks = [(start, head) for start in range(0, length, CHUNK) for head in range(2)]

    def scores_of(task):
        start, head = task
        cols = slice(head * HEAD_DIM, (head + 1) * HEAD_DIM)
        return dot_nt(keys[:, cols], scaled[start : start + CHUNK, cols])

    upcoming = scores_of(tasks[0])
    pieces = []
    for number, (start, head) in enumerate(tasks):
        scores = upcoming
        if number + 1 < len(tasks):
            upcoming = scores_of(tasks[number + 1])
        rows = slice(start, start + CHUNK)
        top = jnp.max(scores, axis=0, keepdims=True)
        terms = jnp.exp(scores - top).astype(jnp.bfloat16)
        part = dot_nn(extended[head], terms)
        total = part[HEAD_DIM : HEAD_DIM + 1]
        piece = part[:HEAD_DIM] / total
        lse_ref[0, head : head + 1, rows] = top + jnp.log(total)
        out_t_ref[head * HEAD_DIM : (head + 1) * HEAD_DIM, rows] = piece
        pieces.append(piece)
        if head == 1:
            out_ref[rows, :] = jnp.concatenate(pieces, axis=0).T.astype(jnp.bfloat16)
            pieces = []


def attention_forward(projected):
    length = projected.shape[0]
    pairs = HEADS // 2
    return pl.pallas_call(
        attention_forward_kernel,
        grid=(pairs,),
        in_specs=[
            pl.BlockSpec((length, PAIR), lambda i: (0, i)),
            pl.BlockSpec((length, PAIR), lambda i: (0, pairs + i)),
            pl.BlockSpec((length, PAIR), lambda i: (0, 2 * pairs + i)),
        ],
        out_specs=[
            pl.BlockSpec((length, PAIR), lambda i: (0, i)),
            pl.BlockSpec((PAIR, length), lambda i: (i, 0)),
            pl.BlockSpec((1, 2, length), lambda i: (i, 0, 0)),
        ],
        out_shape=[
            jax.ShapeDtypeStruct((length, HEADS * HEAD_DIM), jnp.bfloat16),
            jax.ShapeDtypeStruct((HEADS * HEAD_DIM, length), jnp.float32),
            jax.ShapeDtypeStruct((pairs, 2, length), jnp.float32),
        ],
        compiler_params=kernel_params(48),
        cost_estimate=cost(2**32, 8 * 2**20, 2**24),
        name="attention_forward",
    )(projected, projected, projected)


def attention_backward_kernel(
    q_ref, k_ref, v_ref, g_ref, o_ref, lse_ref, out_ref, qb_ref, vb_ref, probs, d_scores
):
    length = q_ref.shape[0]
    root = HEAD_DIM ** (-0.5)
    scaled = q_ref[...] * jnp.bfloat16(root)
    keys = k_ref[...]
    values = v_ref[...]
    grads = g_ref[...]
    keys_t = keys.T
    product = grads.T.astype(jnp.float32) * o_ref[...]
    sums_k = [None, None]
    sums_v = [None, None]
    sum_q = None
    pieces = []
    tasks = [(start, head) for start in range(0, length, CHUNK) for head in range(2)]
    for number, (start, head) in enumerate(tasks):
        rows = slice(start, start + CHUNK)
        slot = number % 2
        cols = slice(head * HEAD_DIM, (head + 1) * HEAD_DIM)
        query, grad = scaled[rows, cols], grads[rows, cols]
        lse = lse_ref[0, head : head + 1, rows]
        row_sum = jnp.sum(product[cols, rows], axis=0, keepdims=True)
        for block in range(0, length, KEY_BLOCK):
            some = slice(block, block + KEY_BLOCK)
            prob = jnp.exp(dot_nt(keys[some, cols], query) - lse)
            d_prob = dot_nt(values[some, cols], grad)
            probs[slot, some, :] = prob.astype(jnp.bfloat16)
            d_scores[slot, some, :] = (prob * (d_prob - row_sum)).astype(jnp.bfloat16)
        part_v = dot_nn(probs[slot], grad)
        part_k = dot_nn(d_scores[slot], query)
        sums_v[head] = part_v if start == 0 else sums_v[head] + part_v
        sums_k[head] = part_k if start == 0 else sums_k[head] + part_k
        pieces.append(dot_nn(keys_t[cols, :], d_scores[slot]) * root)
        if head == 1:
            d_query = jnp.concatenate(pieces, axis=0).T.astype(jnp.bfloat16)
            pieces = []
            out_ref[0, rows, :] = d_query
            part_q = jnp.sum(d_query.astype(jnp.float32), axis=0, keepdims=True)
            sum_q = part_q if start == 0 else sum_q + part_q
    out_ref[1] = jnp.concatenate(sums_k, axis=1).astype(jnp.bfloat16)
    d_value = jnp.concatenate(sums_v, axis=1).astype(jnp.bfloat16)
    out_ref[2] = d_value
    qb_ref[...] = sum_q
    vb_ref[...] = jnp.sum(d_value.astype(jnp.float32), axis=0, keepdims=True)


def attention_backward(projected, d_attended, attended_t, lse, first, count, name):
    length = projected.shape[0]
    width = count * PAIR
    pairs = HEADS // 2
    row = pl.BlockSpec((1, PAIR), lambda i: (0, i))
    line = jax.ShapeDtypeStruct((1, width), jnp.float32)
    return pl.pallas_call(
        attention_backward_kernel,
        grid=(count,),
        in_specs=[
            pl.BlockSpec((length, PAIR), lambda i: (0, first + i)),
            pl.BlockSpec((length, PAIR), lambda i: (0, pairs + first + i)),
            pl.BlockSpec((length, PAIR), lambda i: (0, 2 * pairs + first + i)),
            pl.BlockSpec((length, PAIR), lambda i: (0, first + i)),
            pl.BlockSpec((PAIR, length), lambda i: (first + i, 0)),
            pl.BlockSpec((1, 2, length), lambda i: (first + i, 0, 0)),
        ],
        out_specs=[pl.BlockSpec((3, length, PAIR), lambda i: (0, 0, i)), row, row],
        out_shape=[jax.ShapeDtypeStruct((3, length, width), jnp.bfloat16), line, line],
        scratch_shapes=[
            pltpu.VMEM((2, length, CHUNK), jnp.bfloat16),
            pltpu.VMEM((2, length, CHUNK), jnp.bfloat16),
        ],
        compiler_params=kernel_params(48),
        cost_estimate=cost(count * 2**29, count * 2 * 2**20, count * 2**21),
        name=name,
    )(projected, projected, projected, d_attended, attended_t, lse)


def normalize(values):
    average = jnp.mean(values, axis=-1, keepdims=True)
    centred = values - average
    variance = jnp.mean(centred * centred, axis=-1, keepdims=True)
    return centred * lax.rsqrt(variance + EPS_NORM)


def modulate(values, shifts, scales):
    return normalize(values) * (1.0 + scales[:, None, :]) + shifts[:, None, :]


MASKS = {"core": (1, 0), "y": (2, 0), "x": (0, 1), "z1": (0, 2), "z2": (0, 4)}
GATHER_ORDERS = (("z2", "z1", "x", "y"), ("z2", "z1", "y", "x"))


def exchange(value, rep_mask, fsdp_mask):
    reps, shards = lax.axis_size("rep"), lax.axis_size("fsdp")
    pairs = [
        (rep * shards + shard, (rep ^ rep_mask) * shards + (shard ^ fsdp_mask))
        for rep in range(reps)
        for shard in range(shards)
    ]
    return lax.ppermute(value, ("rep", "fsdp"), pairs)


def gather_relative(row):
    reps, shards = lax.axis_size("rep"), lax.axis_size("fsdp")
    masks = [(0, 1 << bit) for bit in reversed(range(shards.bit_length() - 1))]
    masks += [(1 << bit, 0) for bit in reversed(range(reps.bit_length() - 1))]
    rows = row[None]
    for pair in masks:
        rows = jnp.stack([rows, exchange(rows, *pair)], axis=1).reshape(-1, *row.shape)
    return rows


def gather_chain(quarter, order):
    rows = quarter[None]
    for name in order:
        rows = jnp.concatenate([rows, exchange(rows, *MASKS[name])], axis=0)
    return rows, exchange(rows, *MASKS["core"])


def chain_map(order):
    offsets = [0]
    for name in order:
        rep_mask, fsdp_mask = MASKS[name]
        offsets += [offset ^ (fsdp_mask * 4 + rep_mask) for offset in offsets]
    return tuple(offsets)


def to_absolute(parts, own):
    parts = list(parts)
    bit = 1
    while bit < len(parts):
        flipped = (own & bit) != 0
        parts = [jnp.where(flipped, parts[i ^ bit], parts[i]) for i in range(len(parts))]
        bit *= 2
    return parts


class HalvingSum:
    def __init__(self, keep, send, order):
        rows, columns = keep.shape[0] // 16, keep.shape[1]
        self.shape = (2, 2, 2, 2, rows, columns)
        self.axes = ["z2", "z1", "x", "y"]
        self.order = list(order)
        self.stay = keep.reshape(self.shape)
        self.arrived = exchange(send, *MASKS["core"])

    def half(self, axis, side):
        stay = lax.index_in_dim(self.stay, side, axis, keepdims=False)
        arrived = lax.index_in_dim(self.arrived.reshape(self.stay.shape), side, axis, keepdims=False)
        return (stay.astype(jnp.float32) + arrived.astype(jnp.float32)).astype(jnp.bfloat16)

    def step(self):
        name = self.order.pop(0)
        axis = self.axes.index(name)
        self.axes.pop(axis)
        away, stay = self.half(axis, 1), self.half(axis, 0)
        self.stay, self.arrived = stay, exchange(away, *MASKS[name])

    def finish(self):
        while self.order:
            self.step()
        own = self.stay.astype(jnp.float32) + self.arrived.reshape(self.stay.shape).astype(jnp.float32)
        own = own.astype(jnp.bfloat16)
        pair = [own, exchange(own, *MASKS["core"])]
        both = jnp.stack(pair)
        other = exchange(both, *MASKS["y"])
        parts = to_absolute([*pair, other[0], other[1]], lax.axis_index("rep"))
        return jnp.concatenate(parts, axis=0).astype(jnp.float32)


class PlainSum:
    def __init__(self, grad):
        self.arrived = grad

    def step(self):
        pass

    def finish(self):
        return scatter_rows(self.arrived)


def hold(value, *sums):
    held = lax.optimization_barrier((value, *[total.arrived for total in sums]))
    for total, arrived in zip(sums, held[1:]):
        total.arrived = arrived
    return held[0]


def scatter_rows(grad):
    own = lax.psum_scatter(grad, ("fsdp", "rep"), scatter_dimension=0, tiled=True)
    return lax.all_gather(own, "rep", axis=0, tiled=True).astype(jnp.float32)


def own_quarter(weight):
    part = weight.shape[0] // lax.axis_size("rep")
    return lax.dynamic_slice_in_dim(weight, lax.axis_index("rep") * part, part, 0)


def gather_rows(weight):
    return lax.all_gather(own_quarter(weight), ("fsdp", "rep"), axis=0, tiled=True)


def column_blocks(quarter, width):
    rows = quarter.shape[0]
    blocks = quarter.shape[1] // width
    return quarter.reshape(rows, blocks, width).transpose(1, 0, 2).reshape(blocks * rows, width)


def gather_packed(parts, rows):
    packed = jnp.concatenate(parts, axis=0)
    blocks, width = packed.shape[0] // rows, packed.shape[1]
    full = lax.all_gather(packed, ("fsdp", "rep"), axis=0, tiled=True)
    return full.reshape(full.shape[0] // packed.shape[0], blocks, rows, width)


def on_device(
    latents,
    conditions,
    modulator,
    modulbias,
    projector,
    querybias,
    valuebias,
    outweight,
    outbiases,
    expander,
    expandbias,
    shrinker,
    shrinkbias,
    upstream,
):
    seqs_dev, seq_len, feature = latents.shape
    token_count = seqs_dev * seq_len
    shard_id, rep_id = lax.axis_index("fsdp"), lax.axis_index("rep")
    shards, reps = lax.axis_size("fsdp"), lax.axis_size("rep")
    halving = shards == 8 and reps == 4
    own_rows = modulator.shape[0]
    own_bias = modulbias.shape[0]

    width = projector.shape[1]
    if halving:
        quarter = own_rows // reps
        proj_quarter = own_quarter(projector)
        chains = [
            gather_chain(proj_quarter[:, part * (width // 2) : (part + 1) * (width // 2)], order)
            for part, order in enumerate(GATHER_ORDERS)
        ]
        maps = [chain_map(order) for order in GATHER_ORDERS]
        packed = gather_packed(
            [
                own_quarter(shrinker),
                column_blocks(own_quarter(expander), feature),
                own_quarter(outweight),
            ],
            quarter,
        )
        out_at = (packed, 8)
        w_expand, w_shrink = packed, packed
        depth_pieces, unit_pieces = shards * reps, reps
        own = jnp.stack(
            [rep_id & 1, shard_id * 2 + (rep_id >> 1), shard_id, rep_id >> 1]
        ).astype(jnp.int32)
    else:
        w_proj, out_at = gather_rows(projector), (gather_rows(outweight), 0)
        w_expand, w_shrink = gather_rows(expander), gather_rows(shrinker)
        depth_pieces, unit_pieces = 2, 2
        own = jnp.zeros((4,), jnp.int32)

    def depth_sum(halves, order):
        if halving:
            return HalvingSum(*halves, order)
        return PlainSum(jnp.concatenate(halves, axis=0))

    def unit_sum(halves, order):
        if halving:
            return HalvingSum(*halves, order)
        blocks = [half.reshape(-1, 1, FF_BLOCK // 2, feature) for half in halves]
        return PlainSum(jnp.concatenate(blocks, axis=1).reshape(-1, feature))

    cond_full = conditions.astype(jnp.float32)
    cond_slice = lax.dynamic_slice_in_dim(cond_full, shard_id * own_rows, own_rows, 1)
    cond_act = jax.nn.silu(cond_slice).astype(jnp.bfloat16)
    cond_own = lax.dynamic_slice_in_dim(cond_full, shard_id * seqs_dev, seqs_dev, 0)
    cond_own = jax.nn.silu(cond_own).astype(jnp.bfloat16)
    mod_term = jnp.dot(cond_act, modulator, preferred_element_type=jnp.float32)
    bias_parts = (modulbias, querybias, valuebias, outbiases, expandbias, shrinkbias)
    own_biases = jnp.concatenate([part.astype(jnp.float32) for part in bias_parts])
    mod_width = seqs_dev * 6 * feature
    sent = jnp.concatenate(
        [
            mod_term.reshape(shards, mod_width),
            jnp.broadcast_to(own_biases[None, :], (shards, own_biases.shape[0])),
        ],
        axis=1,
    )
    got = lax.all_to_all(sent, "fsdp", split_axis=0, concat_axis=0, tiled=True)
    full_biases = []
    start = mod_width
    for part in bias_parts:
        full_biases.append(got[:, start : start + part.shape[0]].reshape(1, -1))
        start += part.shape[0]
    full_modbias, b_query, b_value, b_out, b_expand, b_shrink = full_biases
    modvals = jnp.sum(got[:, :mod_width], axis=0).reshape(seqs_dev, 6, feature)
    modvals = modvals + full_modbias.reshape(1, 6, feature)
    shift_a, scale_a, gate_a = (modvals[:, 0], modvals[:, 1], modvals[:, 2])
    shift_m, scale_m, gate_m = (modvals[:, 3], modvals[:, 4], modvals[:, 5])

    resid_in = latents.astype(jnp.float32)
    norm_a = modulate(resid_in, shift_a, scale_a).astype(jnp.bfloat16).reshape(token_count, feature)
    b_proj = jnp.concatenate([b_query, jnp.zeros_like(b_query), b_value], axis=1)
    if halving:
        flat = (shard_id * reps + rep_id).astype(jnp.int32)[None]
        projected, w_proj = project(flat, norm_a, b_proj, chains, maps)
    else:
        projected = forward_dot(norm_a, w_proj, 0, b_proj, jnp.bfloat16, "project")
    attended, attended_t, log_totals = attention_forward(projected)
    branch_a = forward_dot(attended, *out_at, b_out, jnp.float32, "attention_out")
    branch_a = branch_a.reshape(seqs_dev, seq_len, feature)
    middle = resid_in + gate_a[:, None, :] * branch_a
    norm_m = modulate(middle, shift_m, scale_m).astype(jnp.bfloat16).reshape(token_count, feature)

    grad_out = upstream.astype(jnp.float32)
    d_branch_m = (gate_m[:, None, :] * grad_out).astype(jnp.bfloat16).reshape(token_count, feature)
    g_shrinkbias = jnp.sum(d_branch_m, axis=0, dtype=jnp.float32)
    branch_m, d_norm_m, keep_e, send_e, keep_s, send_s, g_expandbias = feed_forward(
        own, norm_m, d_branch_m, w_expand, b_expand, w_shrink, depth_pieces, unit_pieces
    )
    sum_e = depth_sum((keep_e, send_e), ("y", "x", "z1", "z2"))
    sum_s = unit_sum((keep_s, send_s), ("x", "y", "z1", "z2"))
    branch_m = (branch_m + b_shrink).reshape(seqs_dev, seq_len, feature)
    layer_out = middle + gate_m[:, None, :] * branch_m
    d_gate_m = jnp.sum(grad_out * branch_m, axis=1)
    d_norm_m, layer_out, d_gate_m = hold((d_norm_m, layer_out, d_gate_m), sum_e, sum_s)
    sum_e.step()
    sum_s.step()
    _, norm_pull_m = jax.vjp(modulate, middle, shift_m, scale_m)
    d_mid_norm, d_shift_m, d_scale_m = norm_pull_m(d_norm_m.reshape(seqs_dev, seq_len, feature))
    d_middle = grad_out + d_mid_norm
    d_branch_a = (gate_a[:, None, :] * d_middle).astype(jnp.bfloat16).reshape(token_count, feature)
    d_gate_a = jnp.sum(d_middle * branch_a, axis=1)
    g_outbiases = jnp.sum(d_branch_a, axis=0, dtype=jnp.float32)
    d_attended = backward_dot(d_branch_a, *out_at, jnp.bfloat16, "attention_out_back")
    half_pairs = HEADS // 4
    d_low, q_low, v_low = attention_backward(
        projected, d_attended, attended_t, log_totals, 0, half_pairs, "attention_backward_low"
    )
    halves_low = grad_pair(
        own, attended, d_branch_a, norm_a, d_low, depth_pieces, "weight_grad_low"
    )
    d_attended, halves_low = hold((d_attended, halves_low), sum_e, sum_s)
    sum_low = depth_sum(halves_low, ("y", "x", "z1", "z2"))
    for total in (sum_e, sum_s):
        total.step()
    d_high, q_high, v_high = attention_backward(
        projected, d_attended, attended_t, log_totals, half_pairs, half_pairs, "attention_backward_high"
    )
    d_high = hold(d_high, sum_e, sum_s, sum_low)
    for total in (sum_e, sum_s, sum_low):
        total.step()
    sum_high = depth_sum(
        grad_dot(own, norm_a, d_high, depth_pieces, "weight_grad_high"), ("x", "y", "z1", "z2")
    )
    d_high = hold(d_high, sum_high)
    sum_high.step()
    latents_grad, d_shift_a, d_scale_a = project_back(
        d_low,
        d_high,
        w_proj,
        latents.reshape(token_count, feature),
        scale_a,
        d_middle.reshape(token_count, feature),
    )
    latents_grad = latents_grad.reshape(seqs_dev, seq_len, feature)
    latents_grad, d_shift_a, d_scale_a = hold(
        (latents_grad, d_shift_a, d_scale_a), sum_e, sum_s, sum_low, sum_high
    )
    for total in (sum_e, sum_s, sum_low, sum_high):
        total.step()
    g_querybias = jnp.concatenate([q_low, q_high], axis=1)
    g_valuebias = jnp.concatenate([v_low, v_high], axis=1)
    small = jnp.concatenate(
        [
            part.astype(jnp.float32).reshape(-1, 128)
            for part in (
                d_shift_a,
                d_scale_a,
                d_gate_a,
                d_shift_m,
                d_scale_m,
                d_gate_m,
                cond_own,
                g_querybias,
                g_valuebias,
                g_outbiases,
                g_expandbias,
                g_shrinkbias,
            )
        ]
    ).astype(jnp.bfloat16)
    devices = reps * shards
    size = seqs_dev * feature
    gathered = gather_relative(small).reshape(devices, -1)
    g_expander, g_shrinker = sum_e.finish(), sum_s.finish()
    low, high = sum_low.finish(), sum_high.finish()
    g_outweight = low[:, :feature]
    g_projector = jnp.stack(
        [low[:, feature:].reshape(own_rows, 3, -1), high.reshape(own_rows, 3, -1)], axis=2
    ).reshape(own_rows, 3 * feature)

    cond_all = gathered[:, 6 * size : 7 * size].reshape(devices * seqs_dev, feature)
    cond_all = lax.dynamic_slice_in_dim(cond_all, shard_id * own_rows, own_rows, 1)
    d_mod = gathered[:, : 6 * size]
    d_mod = d_mod.reshape(devices, 6, seqs_dev, feature).transpose(0, 2, 1, 3)
    d_mod = d_mod.reshape(devices * seqs_dev, 6 * feature)
    bias_grads = []
    start = 7 * size
    for total in (feature, feature, feature, expandbias.shape[0] * shards, feature):
        part = total // shards
        own_part = lax.dynamic_slice_in_dim(gathered, start + shard_id * part, part, 1)
        bias_grads.append(jnp.sum(own_part, axis=0, dtype=jnp.float32))
        start += total
    g_modbias = jnp.sum(
        lax.dynamic_slice_in_dim(d_mod, shard_id * own_bias, own_bias, 1), axis=0, dtype=jnp.float32
    )
    g_modulator = jnp.einsum("sr,sc->rc", cond_all, d_mod, preferred_element_type=jnp.float32)
    own_mod = d_mod.reshape(shards, reps, seqs_dev, 6 * feature)[:, 0].reshape(-1, 6 * feature)
    d_cond_act = jnp.einsum("sc,rc->sr", own_mod, modulator, preferred_element_type=jnp.float32)
    d_cond_act = jnp.stack(to_absolute(d_cond_act.reshape(shards, seqs_dev, own_rows), shard_id))
    d_cond_act = d_cond_act.reshape(shards * seqs_dev, own_rows)
    _, silu_pull = jax.vjp(jax.nn.silu, cond_slice)
    conditions_grad = silu_pull(d_cond_act)[0]
    return (
        layer_out,
        latents_grad,
        conditions_grad,
        g_modulator,
        g_modbias,
        g_projector,
        bias_grads[0],
        bias_grads[1],
        g_outweight,
        bias_grads[2],
        g_expander,
        bias_grads[3],
        g_shrinker,
        bias_grads[4],
    )


def solution(mesh):
    return jax.shard_map(
        on_device,
        mesh=mesh,
        in_specs=(
            P(("rep", "fsdp"), None, None),
            P("rep", None),
            P("fsdp", None),
            P("fsdp"),
            P("fsdp", None),
            P("fsdp"),
            P("fsdp"),
            P("fsdp", None),
            P("fsdp"),
            P("fsdp", None),
            P("fsdp"),
            P("fsdp", None),
            P("fsdp"),
            P(("rep", "fsdp"), None, None),
        ),
        out_specs=(
            P(("rep", "fsdp"), None, None),
            P(("rep", "fsdp"), None, None),
            P("rep", "fsdp"),
            P("fsdp", None),
            P("fsdp"),
            P("fsdp", None),
            P("fsdp"),
            P("fsdp"),
            P("fsdp", None),
            P("fsdp"),
            P("fsdp", None),
            P("fsdp"),
            P("fsdp", None),
            P("fsdp"),
        ),
        check_vma=False,
    )
```

```python
from functools import partial

import jax
import jax.numpy as jnp
from jax import lax
from jax.experimental import pallas as pl
from jax.experimental.pallas import tpu as pltpu
from jax.sharding import PartitionSpec as P

HEADS = 16
HEAD_DIM = 64
PAIR = 2 * HEAD_DIM
CHUNK = 256
KEY_BLOCK = 128
NORM_ROWS = 128
EPS_NORM = 1e-06
ROWS = 512
FF_BLOCK = 512
COL_BLOCK = 512
GELU_ROOT = 0.7978845608028654
GELU_CUBE = 0.044715


def dot_nn(left, right):
    return jnp.dot(left, right, preferred_element_type=jnp.float32)


def dot_nt(left, right):
    return lax.dot_general(left, right, (((1,), (1,)), ((), ())), preferred_element_type=jnp.float32)


def dot_tn(left, right):
    return lax.dot_general(left, right, (((0,), (0,)), ((), ())), preferred_element_type=jnp.float32)


def kernel_params(mebibytes):
    return pltpu.CompilerParams(vmem_limit_bytes=mebibytes * 2**20)


def cost(flops, moved, special=0):
    return pl.CostEstimate(flops=flops, bytes_accessed=moved, transcendentals=special)


def weight_spec(weight, first, width, order):
    if weight.ndim == 2:
        offset = first * weight.shape[0] // width
        return pl.BlockSpec((weight.shape[0], width), lambda *at: (0, offset + order(*at)))
    devices, _, rows, columns = weight.shape
    per = columns // width
    return pl.BlockSpec(
        (devices, 1, rows, width),
        lambda *at: (0, first + order(*at) // per, 0, order(*at) % per),
    )


def forward_dot_kernel(x_ref, w_ref, b_ref, out_ref):
    weight = w_ref[...].reshape(x_ref.shape[1], out_ref.shape[1])
    out_ref[...] = (dot_nn(x_ref[...], weight) + b_ref[...]).astype(out_ref.dtype)


def forward_dot(x, weight, first, bias, dtype, name):
    tokens, depth = x.shape
    columns = bias.shape[1]
    return pl.pallas_call(
        forward_dot_kernel,
        grid=(columns // COL_BLOCK,),
        in_specs=[
            pl.BlockSpec((tokens, depth), lambda i: (0, 0)),
            weight_spec(weight, first, COL_BLOCK, lambda i: i),
            pl.BlockSpec((1, COL_BLOCK), lambda i: (0, i)),
        ],
        out_specs=pl.BlockSpec((tokens, COL_BLOCK), lambda i: (0, i)),
        out_shape=jax.ShapeDtypeStruct((tokens, columns), dtype),
        compiler_params=kernel_params(40),
        cost_estimate=cost(tokens * depth * columns, tokens * columns),
        name=name,
    )(x, weight, bias)


def project_kernel(maps, own_ref, x_ref, b_ref, *refs):
    sources, (out_ref, full_ref) = refs[:4], refs[4:]
    step = pl.program_id(0)
    rows = sources[0].shape[1]
    half = pl.num_programs(0) // 2
    for chain in range(2):

        @pl.when((step >= half) == (chain == 1))
        def _():
            for flip in range(2):
                source = sources[2 * chain + flip]
                for index, relative in enumerate(maps[chain]):
                    place = pl.multiple_of((own_ref[0] ^ (relative ^ flip)) * rows, rows)
                    full_ref[pl.ds(place, rows), :] = source[index]

    out_ref[...] = (dot_nn(x_ref[...], full_ref[...]) + b_ref[...]).astype(out_ref.dtype)


def project(flat, x, bias, chains, maps):
    tokens, depth = x.shape
    columns = bias.shape[1]
    steps = columns // COL_BLOCK
    half = steps // 2
    blocks, rows, _ = chains[0][0].shape
    first = pl.BlockSpec((blocks, rows, COL_BLOCK), lambda i, own: (0, 0, jnp.minimum(i, half - 1)))
    second = pl.BlockSpec((blocks, rows, COL_BLOCK), lambda i, own: (0, 0, jnp.maximum(i - half, 0)))
    return pl.pallas_call(
        partial(project_kernel, maps),
        grid_spec=pltpu.PrefetchScalarGridSpec(
            num_scalar_prefetch=1,
            grid=(steps,),
            in_specs=[
                pl.BlockSpec((tokens, depth), lambda i, own: (0, 0)),
                pl.BlockSpec((1, COL_BLOCK), lambda i, own: (0, i)),
                first,
                first,
                second,
                second,
            ],
            out_specs=[
                pl.BlockSpec((tokens, COL_BLOCK), lambda i, own: (0, i)),
                pl.BlockSpec((depth, COL_BLOCK), lambda i, own: (0, i)),
            ],
        ),
        out_shape=[
            jax.ShapeDtypeStruct((tokens, columns), jnp.bfloat16),
            jax.ShapeDtypeStruct((depth, columns), jnp.bfloat16),
        ],
        compiler_params=kernel_params(40),
        cost_estimate=cost(tokens * depth * columns, tokens * columns),
        name="project",
    )(flat, x, bias, *chains[0], *chains[1])


def backward_dot_kernel(dy_ref, w_ref, out_ref, sum_ref):
    step = pl.program_id(0)
    weight = w_ref[...].reshape(out_ref.shape[1], w_ref.shape[-1])
    part = dot_nt(dy_ref[...], weight)

    @pl.when(step == 0)
    def _():
        sum_ref[...] = part

    @pl.when(step > 0)
    def _():
        sum_ref[...] += part

    @pl.when(step == pl.num_programs(0) - 1)
    def _():
        out_ref[...] = sum_ref[...].astype(out_ref.dtype)


def backward_dot(dy, weight, first, dtype, name):
    tokens, columns = dy.shape
    depth = columns
    return pl.pallas_call(
        backward_dot_kernel,
        grid=(columns // COL_BLOCK,),
        in_specs=[
            pl.BlockSpec((tokens, COL_BLOCK), lambda i: (0, i)),
            weight_spec(weight, first, COL_BLOCK, lambda i: i),
        ],
        out_specs=pl.BlockSpec((tokens, depth), lambda i: (0, 0)),
        out_shape=jax.ShapeDtypeStruct((tokens, depth), dtype),
        scratch_shapes=[pltpu.VMEM((tokens, depth), jnp.float32)],
        compiler_params=kernel_params(40),
        cost_estimate=cost(tokens * depth * columns, tokens * columns),
        name=name,
    )(dy, weight)


def project_back_kernel(
    low_ref, high_ref, w_ref, x_ref, scale_ref, carry_ref, out_ref, shift_sum_ref, scale_sum_ref, total
):
    step = pl.program_id(0)

    @pl.when(step == 0)
    def _():
        total[...] = dot_nt(low_ref[0], w_ref[...])

    @pl.when((step > 0) & (step % 2 == 0))
    def _():
        total[...] += dot_nt(low_ref[0], w_ref[...])

    @pl.when(step % 2 == 1)
    def _():
        total[...] += dot_nt(high_ref[0], w_ref[...])

    @pl.when(step == pl.num_programs(0) - 1)
    def _():
        gain = 1.0 + scale_ref[...]
        shift_sum = jnp.zeros(gain.shape, jnp.float32)
        scale_sum = jnp.zeros(gain.shape, jnp.float32)
        for start in range(0, x_ref.shape[0], NORM_ROWS):
            rows = slice(start, start + NORM_ROWS)
            values = x_ref[rows, :].astype(jnp.float32)
            centred = values - jnp.mean(values, axis=-1, keepdims=True)
            variance = jnp.mean(centred * centred, axis=-1, keepdims=True)
            inverse = lax.rsqrt(variance + EPS_NORM)
            normal = centred * inverse
            grad = total[rows, :]
            shift_sum += jnp.sum(grad, axis=0, keepdims=True)
            scale_sum += jnp.sum(grad * normal, axis=0, keepdims=True)
            inner = grad * gain
            average = jnp.mean(inner, axis=-1, keepdims=True)
            along = jnp.mean(inner * normal, axis=-1, keepdims=True)
            out_ref[rows, :] = carry_ref[rows, :] + inverse * (inner - average - normal * along)
        shift_sum_ref[...] = shift_sum
        scale_sum_ref[...] = scale_sum


def project_back(low, high, weight, x, scale, carry):
    groups, tokens, width = low.shape
    depth = weight.shape[0]
    block = pl.BlockSpec((1, tokens, width), lambda i: (i // 2, 0, 0))
    whole = pl.BlockSpec((tokens, depth), lambda i: (0, 0))
    line = pl.BlockSpec((1, depth), lambda i: (0, 0))
    row = jax.ShapeDtypeStruct((1, depth), jnp.float32)
    return pl.pallas_call(
        project_back_kernel,
        grid=(2 * groups,),
        in_specs=[
            block,
            block,
            pl.BlockSpec((depth, width), lambda i: (0, i)),
            whole,
            line,
            whole,
        ],
        out_specs=[whole, line, line],
        out_shape=[jax.ShapeDtypeStruct((tokens, depth), jnp.float32), row, row],
        scratch_shapes=[pltpu.VMEM((tokens, depth), jnp.float32)],
        compiler_params=kernel_params(48),
        cost_estimate=cost(groups * tokens * depth * width, tokens * width),
        name="project_back",
    )(low, high, weight, x, scale, carry)


def store_pieces(total, own_core, place_of, keep_ref, send_ref):
    rows = keep_ref.shape[-2]
    pieces = total.shape[0] // rows
    low = total.astype(jnp.bfloat16).reshape(pieces // 2, 2, rows, total.shape[1])
    here = own_core == 0
    for slot in range(pieces // 2):
        first, second = low[slot, 0], low[slot, 1]
        keep_ref[place_of(slot)] = jnp.where(here, first, second)
        send_ref[place_of(slot)] = jnp.where(here, second, first)


def weight_grad_kernel(table, first, own_ref, x_ref, dx_ref, y_ref, dy_ref, keep_ref, send_ref, left):
    step = pl.program_id(0)

    def place_of(slot):
        return own_ref[1] ^ table[slot], 0

    if first:

        @pl.when(step == 0)
        def _():
            left[...] = x_ref[...].T

    @pl.when(step == first)
    def _():
        left[...] = y_ref[...].T

    right = jnp.where(step < first, dx_ref[...], dy_ref[0]) if first else dy_ref[0]
    store_pieces(dot_nn(left[...], right), own_ref[0], place_of, keep_ref, send_ref)


def weight_grad(own, x, dx, y, dy, table, rows, name):
    tokens, depth = y.shape
    first = 0 if dx is None else dx.shape[1] // COL_BLOCK
    groups = dy.shape[0]
    blocks = first + groups
    whole = pl.BlockSpec((tokens, depth), lambda i, own: (0, 0))
    block = pl.BlockSpec((len(table), 1, rows, COL_BLOCK), lambda i, own: (0, i, 0, 0))
    half = jax.ShapeDtypeStruct((len(table), blocks, rows, COL_BLOCK), jnp.bfloat16)
    if dx is None:
        x, dx = y, y
    return pl.pallas_call(
        partial(weight_grad_kernel, table, first),
        grid_spec=pltpu.PrefetchScalarGridSpec(
            num_scalar_prefetch=1,
            grid=(blocks,),
            in_specs=[
                whole,
                pl.BlockSpec(
                    (tokens, COL_BLOCK), lambda i, own: (0, jnp.clip(i, 0, max(first - 1, 0)))
                ),
                whole,
                pl.BlockSpec(
                    (1, tokens, COL_BLOCK), lambda i, own: (jnp.maximum(i - first, 0), 0, 0)
                ),
            ],
            out_specs=[block, block],
            scratch_shapes=[pltpu.VMEM((depth, tokens), jnp.bfloat16)],
        ),
        out_shape=[half, half],
        compiler_params=kernel_params(40),
        cost_estimate=cost(tokens * depth * blocks * COL_BLOCK, tokens * blocks * COL_BLOCK),
        name=name,
    )(own, x, dx, y, dy)


def place_units_kernel(own_ref, *refs):
    sources, (expand_ref, shrink_ref) = refs[:4], refs[4:]
    for flip, source in enumerate(sources):
        at = own_ref[0] ^ flip
        rows = expand_ref.shape[0] // 4
        place = pl.ds(pl.multiple_of(at * rows, rows), rows)
        width = source.shape[2]
        for block in range(expand_ref.shape[1] // width):
            piece = source[0, block * rows : (block + 1) * rows, :]
            expand_ref[place, block * width : (block + 1) * width] = piece.astype(jnp.float32)
        rows = source.shape[1]
        place = pl.ds(pl.multiple_of(at * rows, rows), rows)
        shrink_ref[place, :] = source[1].astype(jnp.float32)


def place_attention_kernel(own_ref, *refs):
    sources, (out_ref, proj_ref) = refs[:4], refs[4:]
    for flip, source in enumerate(sources):
        blocks, rows, width = source.shape
        place = pl.ds(pl.multiple_of((own_ref[0] ^ flip) * rows, rows), rows)
        for block in range(blocks):
            piece = source[block].astype(jnp.float32)
            if block < 2:
                out_ref[place, block * width : (block + 1) * width] = piece
            else:
                group, half = (block - 2) % 3, (block - 2) // 3
                start = (2 * group + half) * width
                proj_ref[place, start : start + width] = piece


def place_reps(kernel, rep_id, own, shapes, name):
    parts = [own] + [exchange(own, mask, 0) for mask in (1, 2, 3)]
    return pl.pallas_call(
        kernel,
        grid_spec=pltpu.PrefetchScalarGridSpec(num_scalar_prefetch=1, grid=()),
        out_shape=[jax.ShapeDtypeStruct(shape, jnp.float32) for shape in shapes],
        compiler_params=kernel_params(32),
        cost_estimate=cost(2**20, 2**20),
        name=name,
    )(rep_id.astype(jnp.int32)[None], *parts)


def feed_forward_kernel(
    table,
    own_ref,
    norm_ref,
    grad_ref,
    expand_ref,
    bias_ref,
    shrink_ref,
    branch_ref,
    d_norm_ref,
    keep_e_ref,
    send_e_ref,
    keep_s_ref,
    send_s_ref,
    d_bias_ref,
    norm_t,
    hidden,
    d_pre,
):
    tokens, depth = norm_ref.shape
    units = hidden.shape[1]
    step = pl.program_id(0)
    expand = expand_ref[...].reshape(depth, units)
    shrink = shrink_ref[...].reshape(units, depth)

    @pl.when(step == 0)
    def _():
        norm_t[...] = norm_ref[...].T
        branch_ref[...] = jnp.zeros_like(branch_ref)
        d_norm_ref[...] = jnp.zeros_like(d_norm_ref)

    bias_sum = jnp.zeros((1, units), jnp.float32)
    starts = list(range(0, tokens, ROWS))

    def entering(start):
        rows = slice(start, start + ROWS)
        return dot_nn(norm_ref[rows, :], expand), dot_nt(grad_ref[rows, :], shrink)

    upcoming = entering(starts[0])
    for number, start in enumerate(starts):
        rows = slice(start, start + ROWS)
        pre, d_unit = upcoming
        if number + 1 < len(starts):
            upcoming = entering(starts[number + 1])
        pre = pre + bias_ref[...]
        square = pre * pre
        bend = jnp.tanh(GELU_ROOT * pre * (1.0 + GELU_CUBE * square))
        rise = 0.5 + 0.5 * bend
        unit = (pre * rise).astype(jnp.bfloat16)
        hidden[rows, :] = unit
        slope = rise + 0.5 * pre * (1.0 - bend * bend) * (
            GELU_ROOT + (3.0 * GELU_ROOT * GELU_CUBE) * square
        )
        d_low = (d_unit * slope).astype(jnp.bfloat16)
        d_pre[rows, :] = d_low
        bias_sum = bias_sum + jnp.sum(d_low.astype(jnp.float32), axis=0, keepdims=True)
        branch_ref[rows, :] += dot_nn(unit, shrink)
        d_norm_ref[rows, :] += dot_nt(d_low, expand)
    d_bias_ref[...] = bias_sum
    store_pieces(
        dot_tn(hidden[...], grad_ref[...]),
        own_ref[0],
        lambda slot: (0, own_ref[3] ^ slot, 0),
        keep_s_ref,
        send_s_ref,
    )
    store_pieces(
        dot_nn(norm_t[...], d_pre[...]),
        own_ref[0],
        lambda slot: (own_ref[1] ^ table[slot], 0),
        keep_e_ref,
        send_e_ref,
    )


def feed_forward(own, norm, grad, expand, bias, shrink, table):
    tokens, depth = norm.shape
    total = bias.shape[1]
    steps = total // FF_BLOCK
    slots = len(table)
    rows_e = depth // (2 * slots)
    per = depth // FF_BLOCK
    whole = pl.BlockSpec((tokens, depth), lambda i, own: (0, 0))
    half_e = pl.BlockSpec(
        (slots, 1, rows_e, FF_BLOCK), lambda i, own: (0, i // per, 0, i % per)
    )
    if slots > 1:
        spec_e = weight_spec(expand, 4, FF_BLOCK, lambda i, own: i)
        spec_s = pl.BlockSpec(
            (shrink.shape[0] // steps, 4) + shrink.shape[2:], lambda i, own: (i, 0, 0, 0)
        )
        shape_s = (2, 2, steps // 2, FF_BLOCK // 4, depth)
        half_s = pl.BlockSpec(
            (1, 2, 1, FF_BLOCK // 4, depth),
            lambda i, own: ((i & 1) ^ own[2], 0, ((i & 2) | (i >> 2)) ^ own[4], 0, 0),
        )
    else:
        spec_e = weight_spec(expand, 0, FF_BLOCK, lambda i, own: i)
        spec_s = pl.BlockSpec((FF_BLOCK, depth), lambda i, own: (i, 0))
        shape_s = (1, 1, steps, FF_BLOCK // 2, depth)
        half_s = pl.BlockSpec((1, 1, 1, FF_BLOCK // 2, depth), lambda i, own: (0, 0, i, 0, 0))
    line = pl.BlockSpec((1, FF_BLOCK), lambda i, own: (0, i))
    wide = jax.ShapeDtypeStruct((tokens, depth), jnp.float32)
    out_e = jax.ShapeDtypeStruct((slots, total // depth, rows_e, depth), jnp.bfloat16)
    out_s = jax.ShapeDtypeStruct(shape_s, jnp.bfloat16)
    return pl.pallas_call(
        partial(feed_forward_kernel, table),
        grid_spec=pltpu.PrefetchScalarGridSpec(
            num_scalar_prefetch=1,
            grid=(steps,),
            in_specs=[whole, whole, spec_e, line, spec_s],
            out_specs=[whole, whole, half_e, half_e, half_s, half_s, line],
            scratch_shapes=[
                pltpu.VMEM((depth, tokens), jnp.bfloat16),
                pltpu.VMEM((tokens, FF_BLOCK), jnp.bfloat16),
                pltpu.VMEM((tokens, FF_BLOCK), jnp.bfloat16),
            ],
        ),
        out_shape=[
            wide,
            wide,
            out_e,
            out_e,
            out_s,
            out_s,
            jax.ShapeDtypeStruct((1, total), jnp.float32),
        ],
        compiler_params=kernel_params(56),
        cost_estimate=cost(6 * tokens * depth * total, 16 * 2**20, tokens * total),
        name="feed_forward",
    )(own, norm, grad, expand, bias, shrink)


def attention_forward_kernel(q_ref, k_ref, v_ref, out_ref, out_t_ref, lse_ref):
    length = q_ref.shape[0]
    scaled = q_ref[...] * jnp.bfloat16(HEAD_DIM ** (-0.5))
    keys = k_ref[...]
    values_t = v_ref[...].T
    ones = jnp.ones((16, length), jnp.bfloat16)
    extended = [
        jnp.concatenate([values_t[head * HEAD_DIM : (head + 1) * HEAD_DIM], ones], axis=0)
        for head in range(2)
    ]
    tasks = [(start, head) for start in range(0, length, CHUNK) for head in range(2)]

    def scores_of(task):
        start, head = task
        cols = slice(head * HEAD_DIM, (head + 1) * HEAD_DIM)
        return dot_nt(keys[:, cols], scaled[start : start + CHUNK, cols])

    upcoming = scores_of(tasks[0])
    pieces = []
    for number, (start, head) in enumerate(tasks):
        scores = upcoming
        if number + 1 < len(tasks):
            upcoming = scores_of(tasks[number + 1])
        rows = slice(start, start + CHUNK)
        top = jnp.max(scores, axis=0, keepdims=True)
        terms = jnp.exp(scores - top).astype(jnp.bfloat16)
        part = dot_nn(extended[head], terms)
        total = part[HEAD_DIM : HEAD_DIM + 1]
        piece = part[:HEAD_DIM] / total
        lse_ref[0, head : head + 1, rows] = top + jnp.log(total)
        out_t_ref[head * HEAD_DIM : (head + 1) * HEAD_DIM, rows] = piece
        pieces.append(piece)
        if head == 1:
            out_ref[rows, :] = jnp.concatenate(pieces, axis=0).T.astype(jnp.bfloat16)
            pieces = []


def attention_forward(projected):
    length = projected.shape[0]
    pairs = HEADS // 2
    return pl.pallas_call(
        attention_forward_kernel,
        grid=(pairs,),
        in_specs=[
            pl.BlockSpec((length, PAIR), lambda i: (0, i)),
            pl.BlockSpec((length, PAIR), lambda i: (0, pairs + i)),
            pl.BlockSpec((length, PAIR), lambda i: (0, 2 * pairs + i)),
        ],
        out_specs=[
            pl.BlockSpec((length, PAIR), lambda i: (0, i)),
            pl.BlockSpec((PAIR, length), lambda i: (i, 0)),
            pl.BlockSpec((1, 2, length), lambda i: (i, 0, 0)),
        ],
        out_shape=[
            jax.ShapeDtypeStruct((length, HEADS * HEAD_DIM), jnp.bfloat16),
            jax.ShapeDtypeStruct((HEADS * HEAD_DIM, length), jnp.float32),
            jax.ShapeDtypeStruct((pairs, 2, length), jnp.float32),
        ],
        compiler_params=kernel_params(48),
        cost_estimate=cost(2**32, 8 * 2**20, 2**24),
        name="attention_forward",
    )(projected, projected, projected)


def attention_backward_kernel(
    q_ref, k_ref, v_ref, g_ref, o_ref, lse_ref, out_ref, qb_ref, vb_ref, probs, d_scores
):
    length = q_ref.shape[0]
    root = HEAD_DIM ** (-0.5)
    scaled = q_ref[...] * jnp.bfloat16(root)
    keys = k_ref[...]
    values = v_ref[...]
    grads = g_ref[...]
    keys_t = keys.T
    product = grads.T.astype(jnp.float32) * o_ref[...]
    sums_k = [None, None]
    sums_v = [None, None]
    sum_q = None
    pieces = []
    tasks = [(start, head) for start in range(0, length, CHUNK) for head in range(2)]
    for number, (start, head) in enumerate(tasks):
        rows = slice(start, start + CHUNK)
        slot = number % 2
        cols = slice(head * HEAD_DIM, (head + 1) * HEAD_DIM)
        query, grad = scaled[rows, cols], grads[rows, cols]
        lse = lse_ref[0, head : head + 1, rows]
        row_sum = jnp.sum(product[cols, rows], axis=0, keepdims=True)
        for block in range(0, length, KEY_BLOCK):
            some = slice(block, block + KEY_BLOCK)
            prob = jnp.exp(dot_nt(keys[some, cols], query) - lse)
            d_prob = dot_nt(values[some, cols], grad)
            probs[slot, some, :] = prob.astype(jnp.bfloat16)
            d_scores[slot, some, :] = (prob * (d_prob - row_sum)).astype(jnp.bfloat16)
        part_v = dot_nn(probs[slot], grad)
        part_k = dot_nn(d_scores[slot], query)
        sums_v[head] = part_v if start == 0 else sums_v[head] + part_v
        sums_k[head] = part_k if start == 0 else sums_k[head] + part_k
        pieces.append(dot_nn(keys_t[cols, :], d_scores[slot]) * root)
        if head == 1:
            d_query = jnp.concatenate(pieces, axis=0).T.astype(jnp.bfloat16)
            pieces = []
            out_ref[0, rows, :] = d_query
            part_q = jnp.sum(d_query.astype(jnp.float32), axis=0, keepdims=True)
            sum_q = part_q if start == 0 else sum_q + part_q
    out_ref[1] = jnp.concatenate(sums_k, axis=1).astype(jnp.bfloat16)
    d_value = jnp.concatenate(sums_v, axis=1).astype(jnp.bfloat16)
    out_ref[2] = d_value
    qb_ref[...] = sum_q
    vb_ref[...] = jnp.sum(d_value.astype(jnp.float32), axis=0, keepdims=True)


def attention_backward(projected, d_attended, attended_t, lse, first, count, name):
    length = projected.shape[0]
    width = count * PAIR
    pairs = HEADS // 2
    row = pl.BlockSpec((1, PAIR), lambda i: (0, i))
    line = jax.ShapeDtypeStruct((1, width), jnp.float32)
    return pl.pallas_call(
        attention_backward_kernel,
        grid=(count,),
        in_specs=[
            pl.BlockSpec((length, PAIR), lambda i: (0, first + i)),
            pl.BlockSpec((length, PAIR), lambda i: (0, pairs + first + i)),
            pl.BlockSpec((length, PAIR), lambda i: (0, 2 * pairs + first + i)),
            pl.BlockSpec((length, PAIR), lambda i: (0, first + i)),
            pl.BlockSpec((PAIR, length), lambda i: (first + i, 0)),
            pl.BlockSpec((1, 2, length), lambda i: (first + i, 0, 0)),
        ],
        out_specs=[pl.BlockSpec((3, length, PAIR), lambda i: (0, 0, i)), row, row],
        out_shape=[jax.ShapeDtypeStruct((3, length, width), jnp.bfloat16), line, line],
        scratch_shapes=[
            pltpu.VMEM((2, length, CHUNK), jnp.bfloat16),
            pltpu.VMEM((2, length, CHUNK), jnp.bfloat16),
        ],
        compiler_params=kernel_params(48),
        cost_estimate=cost(count * 2**29, count * 2 * 2**20, count * 2**21),
        name=name,
    )(projected, projected, projected, d_attended, attended_t, lse)


def normalize(values):
    average = jnp.mean(values, axis=-1, keepdims=True)
    centred = values - average
    variance = jnp.mean(centred * centred, axis=-1, keepdims=True)
    return centred * lax.rsqrt(variance + EPS_NORM)


def modulate(values, shifts, scales):
    return normalize(values) * (1.0 + scales[:, None, :]) + shifts[:, None, :]


MASKS = {"core": (1, 0), "y": (2, 0), "x": (0, 1), "z1": (0, 2), "z2": (0, 4)}
GATHER_ORDERS = (("z2", "z1", "x", "y"), ("z2", "z1", "y", "x"))


def exchange(value, rep_mask, fsdp_mask):
    reps, shards = lax.axis_size("rep"), lax.axis_size("fsdp")
    pairs = [
        (rep * shards + shard, (rep ^ rep_mask) * shards + (shard ^ fsdp_mask))
        for rep in range(reps)
        for shard in range(shards)
    ]
    return lax.ppermute(value, ("rep", "fsdp"), pairs)


def gather_relative(row):
    reps, shards = lax.axis_size("rep"), lax.axis_size("fsdp")
    masks = [(0, 1 << bit) for bit in reversed(range(shards.bit_length() - 1))]
    masks += [(1 << bit, 0) for bit in reversed(range(reps.bit_length() - 1))]
    rows = row[None]
    for pair in masks:
        rows = jnp.concatenate([rows, exchange(rows, *pair)], axis=0)
    return rows


def gather_chain(quarter, order):
    rows = quarter[None]
    for name in order:
        rows = jnp.concatenate([rows, exchange(rows, *MASKS[name])], axis=0)
    return rows, exchange(rows, *MASKS["core"])


def chain_map(order):
    offsets = [0]
    for name in order:
        rep_mask, fsdp_mask = MASKS[name]
        offsets += [offset ^ (fsdp_mask * 4 + rep_mask) for offset in offsets]
    return tuple(offsets)


def to_absolute(parts, own):
    parts = list(parts)
    bit = 1
    while bit < len(parts):
        flipped = (own & bit) != 0
        parts = [jnp.where(flipped, parts[i ^ bit], parts[i]) for i in range(len(parts))]
        bit *= 2
    return parts


ORDERS = (("y", "x", "z1", "z2"), ("x", "y", "z1", "z2"))


def place_in(order, shard, y):
    bits = {"z2": (shard >> 2) & 1, "z1": (shard >> 1) & 1, "x": shard & 1, "y": y}
    place = 0
    for name in order:
        place = place * 2 + bits[name]
    return place


class HalvingSum:
    def __init__(self, halves, order):
        keep, send = halves
        self.masks = [MASKS[name] for name in order]
        self.stay = keep
        self.arrived = exchange(send, *MASKS["core"])

    def added(self, start, stop):
        stay, arrived = self.stay[start:stop], self.arrived[start:stop]
        return (stay.astype(jnp.float32) + arrived.astype(jnp.float32)).astype(jnp.bfloat16)

    def step(self):
        count = self.stay.shape[0]
        away = self.added(count // 2, count)
        self.stay = self.added(0, count // 2)
        self.arrived = exchange(away, *self.masks.pop(0))

    def finish(self):
        while self.masks:
            self.step()
        return self.added(0, 1)[0]


class PlainSum:
    def __init__(self, grad):
        self.arrived = grad

    def step(self):
        pass

    def finish(self):
        return scatter_rows(self.arrived)


def hold(value, *sums):
    held = lax.optimization_barrier((value, *[total.arrived for total in sums]))
    for total, arrived in zip(sums, held[1:]):
        total.arrived = arrived
    return held[0]


def scatter_rows(grad):
    own = lax.psum_scatter(grad, ("fsdp", "rep"), scatter_dimension=0, tiled=True)
    return lax.all_gather(own, "rep", axis=0, tiled=True).astype(jnp.float32)


def own_quarter(weight):
    part = weight.shape[0] // lax.axis_size("rep")
    return lax.dynamic_slice_in_dim(weight, lax.axis_index("rep") * part, part, 0)


def gather_rows(weight):
    return lax.all_gather(own_quarter(weight), ("fsdp", "rep"), axis=0, tiled=True)


def column_blocks(quarter, width):
    rows = quarter.shape[0]
    blocks = quarter.shape[1] // width
    return quarter.reshape(rows, blocks, width).transpose(1, 0, 2).reshape(blocks * rows, width)


def gather_packed(parts, rows):
    packed = jnp.concatenate(parts, axis=0)
    blocks, width = packed.shape[0] // rows, packed.shape[1]
    full = lax.all_gather(packed, ("fsdp", "rep"), axis=0, tiled=True)
    return full.reshape(full.shape[0] // packed.shape[0], blocks, rows, width)


def on_device(
    latents,
    conditions,
    modulator,
    modulbias,
    projector,
    querybias,
    valuebias,
    outweight,
    outbiases,
    expander,
    expandbias,
    shrinker,
    shrinkbias,
    upstream,
):
    seqs_dev, seq_len, feature = latents.shape
    token_count = seqs_dev * seq_len
    shard_id, rep_id = lax.axis_index("fsdp"), lax.axis_index("rep")
    shards, reps = lax.axis_size("fsdp"), lax.axis_size("rep")
    halving = shards == 8 and reps == 4
    own_rows = modulator.shape[0]
    own_bias = modulbias.shape[0]

    width = projector.shape[1]
    if halving:
        quarter = own_rows // reps
        proj_quarter = own_quarter(projector)
        chains = [
            gather_chain(proj_quarter[:, part * (width // 2) : (part + 1) * (width // 2)], order)
            for part, order in enumerate(GATHER_ORDERS)
        ]
        maps = [chain_map(order) for order in GATHER_ORDERS]
        packed = gather_packed(
            [
                own_quarter(shrinker),
                column_blocks(own_quarter(expander), feature),
                own_quarter(outweight),
            ],
            quarter,
        )
        out_at = (packed, 8)
        w_expand, w_shrink = packed, packed
        y_id = rep_id >> 1
        own, own_high = [
            jnp.stack(
                [
                    rep_id & 1,
                    place_in(order, shard_id, y_id),
                    shard_id & 1,
                    y_id,
                    (shard_id & 2) | (shard_id >> 2),
                ]
            ).astype(jnp.int32)
            for order in ORDERS
        ]
        tables = [
            tuple(place_in(order, slot >> 1, slot & 1) for slot in range(2 * shards))
            for order in ORDERS
        ]
        piece = quarter
    else:
        w_proj, out_at = gather_rows(projector), (gather_rows(outweight), 0)
        w_expand, w_shrink = gather_rows(expander), gather_rows(shrinker)
        own = own_high = jnp.zeros((5,), jnp.int32)
        tables = [(0,), (0,)]
        piece = feature // 2

    def depth_sum(halves, order):
        if halving:
            return HalvingSum(halves, order)
        columns = [half[0].transpose(1, 0, 2).reshape(feature // 2, -1) for half in halves]
        return PlainSum(jnp.concatenate(columns, axis=0))

    def unit_sum(halves, order):
        if halving:
            return HalvingSum([half.reshape(16, -1, feature) for half in halves], order)
        blocks = [half.reshape(-1, 1, FF_BLOCK // 2, feature) for half in halves]
        return PlainSum(jnp.concatenate(blocks, axis=1).reshape(-1, feature))

    cond_full = conditions.astype(jnp.float32)
    cond_slice = lax.dynamic_slice_in_dim(cond_full, shard_id * own_rows, own_rows, 1)
    cond_act = jax.nn.silu(cond_slice).astype(jnp.bfloat16)
    cond_own = lax.dynamic_slice_in_dim(cond_full, shard_id * seqs_dev, seqs_dev, 0)
    cond_own = jax.nn.silu(cond_own).astype(jnp.bfloat16)
    mod_term = jnp.dot(cond_act, modulator, preferred_element_type=jnp.float32)
    bias_parts = (modulbias, querybias, valuebias, outbiases, expandbias, shrinkbias)
    own_biases = jnp.concatenate([part.astype(jnp.float32) for part in bias_parts])
    mod_width = seqs_dev * 6 * feature
    sent = jnp.concatenate(
        [
            mod_term.reshape(shards, mod_width),
            jnp.broadcast_to(own_biases[None, :], (shards, own_biases.shape[0])),
        ],
        axis=1,
    )
    got = lax.all_to_all(sent, "fsdp", split_axis=0, concat_axis=0, tiled=True)
    full_biases = []
    start = mod_width
    for part in bias_parts:
        full_biases.append(got[:, start : start + part.shape[0]].reshape(1, -1))
        start += part.shape[0]
    full_modbias, b_query, b_value, b_out, b_expand, b_shrink = full_biases
    modvals = jnp.sum(got[:, :mod_width], axis=0).reshape(seqs_dev, 6, feature)
    modvals = modvals + full_modbias.reshape(1, 6, feature)
    shift_a, scale_a, gate_a = (modvals[:, 0], modvals[:, 1], modvals[:, 2])
    shift_m, scale_m, gate_m = (modvals[:, 3], modvals[:, 4], modvals[:, 5])

    resid_in = latents.astype(jnp.float32)
    norm_a = modulate(resid_in, shift_a, scale_a).astype(jnp.bfloat16).reshape(token_count, feature)
    b_proj = jnp.concatenate([b_query, jnp.zeros_like(b_query), b_value], axis=1)
    if halving:
        flat = (shard_id * reps + rep_id).astype(jnp.int32)[None]
        projected, w_proj = project(flat, norm_a, b_proj, chains, maps)
    else:
        projected = forward_dot(norm_a, w_proj, 0, b_proj, jnp.bfloat16, "project")
    attended, attended_t, log_totals = attention_forward(projected)
    branch_a = forward_dot(attended, *out_at, b_out, jnp.float32, "attention_out")
    branch_a = branch_a.reshape(seqs_dev, seq_len, feature)
    middle = resid_in + gate_a[:, None, :] * branch_a
    norm_m = modulate(middle, shift_m, scale_m).astype(jnp.bfloat16).reshape(token_count, feature)

    grad_out = upstream.astype(jnp.float32)
    d_branch_m = (gate_m[:, None, :] * grad_out).astype(jnp.bfloat16).reshape(token_count, feature)
    g_shrinkbias = jnp.sum(d_branch_m, axis=0, dtype=jnp.float32)
    branch_m, d_norm_m, keep_e, send_e, keep_s, send_s, g_expandbias = feed_forward(
        own, norm_m, d_branch_m, w_expand, b_expand, w_shrink, tables[0]
    )
    sum_e = depth_sum((keep_e, send_e), ORDERS[0])
    sum_s = unit_sum((keep_s, send_s), ORDERS[1])
    branch_m = (branch_m + b_shrink).reshape(seqs_dev, seq_len, feature)
    layer_out = middle + gate_m[:, None, :] * branch_m
    d_gate_m = jnp.sum(grad_out * branch_m, axis=1)
    d_norm_m, layer_out, d_gate_m = hold((d_norm_m, layer_out, d_gate_m), sum_e, sum_s)
    sum_e.step()
    sum_s.step()
    _, norm_pull_m = jax.vjp(modulate, middle, shift_m, scale_m)
    d_mid_norm, d_shift_m, d_scale_m = norm_pull_m(d_norm_m.reshape(seqs_dev, seq_len, feature))
    d_middle = grad_out + d_mid_norm
    d_branch_a = (gate_a[:, None, :] * d_middle).astype(jnp.bfloat16).reshape(token_count, feature)
    d_gate_a = jnp.sum(d_middle * branch_a, axis=1)
    g_outbiases = jnp.sum(d_branch_a, axis=0, dtype=jnp.float32)
    d_attended = backward_dot(d_branch_a, *out_at, jnp.bfloat16, "attention_out_back")
    half_pairs = HEADS // 4
    d_low, q_low, v_low = attention_backward(
        projected, d_attended, attended_t, log_totals, 0, half_pairs, "attention_backward_low"
    )
    halves_low = weight_grad(
        own, attended, d_branch_a, norm_a, d_low, tables[0], piece, "weight_grad_low"
    )
    d_attended, halves_low = hold((d_attended, halves_low), sum_e, sum_s)
    sum_low = depth_sum(halves_low, ORDERS[0])
    for total in (sum_e, sum_s):
        total.step()
    d_high, q_high, v_high = attention_backward(
        projected, d_attended, attended_t, log_totals, half_pairs, half_pairs, "attention_backward_high"
    )
    d_high = hold(d_high, sum_e, sum_s, sum_low)
    for total in (sum_e, sum_s, sum_low):
        total.step()
    halves_high = weight_grad(
        own_high, None, None, norm_a, d_high, tables[1], piece, "weight_grad_high"
    )
    sum_high = depth_sum(halves_high, ORDERS[1])
    d_high = hold(d_high, sum_high)
    sum_high.step()
    latents_grad, d_shift_a, d_scale_a = project_back(
        d_low,
        d_high,
        w_proj,
        latents.reshape(token_count, feature),
        scale_a,
        d_middle.reshape(token_count, feature),
    )
    latents_grad = latents_grad.reshape(seqs_dev, seq_len, feature)
    latents_grad, d_shift_a, d_scale_a = hold(
        (latents_grad, d_shift_a, d_scale_a), sum_e, sum_s, sum_low, sum_high
    )
    for total in (sum_e, sum_s, sum_low, sum_high):
        total.step()
    g_querybias = jnp.concatenate([q_low, q_high], axis=1)
    g_valuebias = jnp.concatenate([v_low, v_high], axis=1)
    small = jnp.concatenate(
        [
            part.astype(jnp.float32).reshape(-1, 128)
            for part in (
                d_shift_a,
                d_scale_a,
                d_gate_a,
                d_shift_m,
                d_scale_m,
                d_gate_m,
                cond_own,
                g_querybias,
                g_valuebias,
                g_outbiases,
                g_expandbias,
                g_shrinkbias,
                jnp.zeros((feature,)),
            )
        ]
    ).astype(jnp.bfloat16)
    devices = reps * shards
    size = seqs_dev * feature
    gathered = gather_relative(small)
    if halving:
        done = jnp.stack([total.finish().reshape(-1, feature) for total in (sum_e, sum_s)])
        g_expander, g_shrinker = place_reps(
            place_units_kernel, rep_id, done, (expander.shape, shrinker.shape), "place_units"
        )
        done = jnp.concatenate([sum_low.finish(), sum_high.finish()], axis=0)
        g_outweight, g_projector = place_reps(
            place_attention_kernel, rep_id, done, (outweight.shape, projector.shape), "place_attention"
        )
    else:
        g_expander, g_shrinker = sum_e.finish(), sum_s.finish()
        low, high = sum_low.finish(), sum_high.finish()
        g_outweight = low[:, :feature]
        g_projector = jnp.stack(
            [low[:, feature:].reshape(own_rows, 3, -1), high.reshape(own_rows, 3, -1)], axis=2
        ).reshape(own_rows, 3 * feature)

    lines = size // 128
    cond_all = gathered[:, 6 * lines : 7 * lines].reshape(devices * seqs_dev, feature)
    cond_all = lax.dynamic_slice_in_dim(cond_all, shard_id * own_rows, own_rows, 1)
    d_mod = gathered[:, : 6 * lines].reshape(devices, 6, seqs_dev, feature).transpose(0, 2, 1, 3)
    d_mod = d_mod.reshape(devices * seqs_dev, 6 * feature)
    bias_sums = jnp.sum(gathered[:, 7 * lines :], axis=0, dtype=jnp.float32).reshape(-1)
    bias_grads = []
    start = 0
    for total in (feature, feature, feature, expandbias.shape[0] * shards, feature):
        part = total // shards
        bias_grads.append(lax.dynamic_slice_in_dim(bias_sums, start + shard_id * part, part, 0))
        start += total
    g_modbias = jnp.sum(
        lax.dynamic_slice_in_dim(d_mod, shard_id * own_bias, own_bias, 1), axis=0, dtype=jnp.float32
    )
    g_modulator = jnp.einsum("sr,sc->rc", cond_all, d_mod, preferred_element_type=jnp.float32)
    own_mod = d_mod[: shards * seqs_dev]
    d_cond_act = jnp.einsum("sc,rc->sr", own_mod, modulator, preferred_element_type=jnp.float32)
    d_cond_act = d_cond_act.reshape(shards, seqs_dev, own_rows)
    bits = shards.bit_length() - 1
    turned = [sum(((i >> bit) & 1) << (bits - 1 - bit) for bit in range(bits)) for i in range(shards)]
    d_cond_act = jnp.stack(to_absolute([d_cond_act[i] for i in turned], shard_id))
    d_cond_act = d_cond_act.reshape(shards * seqs_dev, own_rows)
    _, silu_pull = jax.vjp(jax.nn.silu, cond_slice)
    conditions_grad = silu_pull(d_cond_act)[0]
    return (
        layer_out,
        latents_grad,
        conditions_grad,
        g_modulator,
        g_modbias,
        g_projector,
        bias_grads[0],
        bias_grads[1],
        g_outweight,
        bias_grads[2],
        g_expander,
        bias_grads[3],
        g_shrinker,
        bias_grads[4],
    )


def solution(mesh):
    return jax.shard_map(
        on_device,
        mesh=mesh,
        in_specs=(
            P(("rep", "fsdp"), None, None),
            P("rep", None),
            P("fsdp", None),
            P("fsdp"),
            P("fsdp", None),
            P("fsdp"),
            P("fsdp"),
            P("fsdp", None),
            P("fsdp"),
            P("fsdp", None),
            P("fsdp"),
            P("fsdp", None),
            P("fsdp"),
            P(("rep", "fsdp"), None, None),
        ),
        out_specs=(
            P(("rep", "fsdp"), None, None),
            P(("rep", "fsdp"), None, None),
            P("rep", "fsdp"),
            P("fsdp", None),
            P("fsdp"),
            P("fsdp", None),
            P("fsdp"),
            P("fsdp"),
            P("fsdp", None),
            P("fsdp"),
            P("fsdp", None),
            P("fsdp"),
            P("fsdp", None),
            P("fsdp"),
        ),
        check_vma=False,
    )
```

```python
from functools import partial

import jax
import jax.numpy as jnp
from jax import lax
from jax.experimental import pallas as pl
from jax.experimental.pallas import tpu as pltpu
from jax.sharding import PartitionSpec as P

HEADS = 16
HEAD_DIM = 64
PAIR = 2 * HEAD_DIM
CHUNK = 256
KEY_BLOCK = 128
NORM_ROWS = 128
EPS_NORM = 1e-06
ROWS = 512
FF_BLOCK = 512
COL_BLOCK = 512
GELU_ROOT = 0.7978845608028654
GELU_CUBE = 0.044715


def dot_nn(left, right):
    return jnp.dot(left, right, preferred_element_type=jnp.float32)


def dot_nt(left, right):
    return lax.dot_general(left, right, (((1,), (1,)), ((), ())), preferred_element_type=jnp.float32)


def dot_tn(left, right):
    return lax.dot_general(left, right, (((0,), (0,)), ((), ())), preferred_element_type=jnp.float32)


def kernel_params(mebibytes):
    return pltpu.CompilerParams(vmem_limit_bytes=mebibytes * 2**20)


def cost(flops, moved, special=0):
    return pl.CostEstimate(flops=flops, bytes_accessed=moved, transcendentals=special)


def weight_spec(weight, first, width, order):
    if weight.ndim == 2:
        offset = first * weight.shape[0] // width
        return pl.BlockSpec((weight.shape[0], width), lambda *at: (0, offset + order(*at)))
    devices, _, rows, columns = weight.shape
    per = columns // width
    return pl.BlockSpec(
        (devices, 1, rows, width),
        lambda *at: (0, first + order(*at) // per, 0, order(*at) % per),
    )


def forward_dot_kernel(x_ref, w_ref, b_ref, out_ref):
    weight = w_ref[...].reshape(x_ref.shape[1], out_ref.shape[1])
    out_ref[...] = (dot_nn(x_ref[...], weight) + b_ref[...]).astype(out_ref.dtype)


def forward_dot(x, weight, first, bias, dtype, name):
    tokens, depth = x.shape
    columns = bias.shape[1]
    return pl.pallas_call(
        forward_dot_kernel,
        grid=(columns // COL_BLOCK,),
        in_specs=[
            pl.BlockSpec((tokens, depth), lambda i: (0, 0)),
            weight_spec(weight, first, COL_BLOCK, lambda i: i),
            pl.BlockSpec((1, COL_BLOCK), lambda i: (0, i)),
        ],
        out_specs=pl.BlockSpec((tokens, COL_BLOCK), lambda i: (0, i)),
        out_shape=jax.ShapeDtypeStruct((tokens, columns), dtype),
        compiler_params=kernel_params(40),
        cost_estimate=cost(tokens * depth * columns, tokens * columns),
        name=name,
    )(x, weight, bias)


def project_kernel(maps, own_ref, x_ref, b_ref, *refs):
    sources, (out_ref, full_ref) = refs[:4], refs[4:]
    step = pl.program_id(0)
    rows = sources[0].shape[1]
    half = pl.num_programs(0) // 2
    for chain in range(2):

        @pl.when((step >= half) == (chain == 1))
        def _():
            for flip in range(2):
                source = sources[2 * chain + flip]
                for index, relative in enumerate(maps[chain]):
                    place = pl.multiple_of((own_ref[0] ^ (relative ^ flip)) * rows, rows)
                    full_ref[pl.ds(place, rows), :] = source[index]

    out_ref[...] = (dot_nn(x_ref[...], full_ref[...]) + b_ref[...]).astype(out_ref.dtype)


def project(flat, x, bias, chains, maps):
    tokens, depth = x.shape
    columns = bias.shape[1]
    steps = columns // COL_BLOCK
    half = steps // 2
    blocks, rows, _ = chains[0][0].shape
    first = pl.BlockSpec((blocks, rows, COL_BLOCK), lambda i, own: (0, 0, jnp.minimum(i, half - 1)))
    second = pl.BlockSpec((blocks, rows, COL_BLOCK), lambda i, own: (0, 0, jnp.maximum(i - half, 0)))
    return pl.pallas_call(
        partial(project_kernel, maps),
        grid_spec=pltpu.PrefetchScalarGridSpec(
            num_scalar_prefetch=1,
            grid=(steps,),
            in_specs=[
                pl.BlockSpec((tokens, depth), lambda i, own: (0, 0)),
                pl.BlockSpec((1, COL_BLOCK), lambda i, own: (0, i)),
                first,
                first,
                second,
                second,
            ],
            out_specs=[
                pl.BlockSpec((tokens, COL_BLOCK), lambda i, own: (0, i)),
                pl.BlockSpec((depth, COL_BLOCK), lambda i, own: (0, i)),
            ],
        ),
        out_shape=[
            jax.ShapeDtypeStruct((tokens, columns), jnp.bfloat16),
            jax.ShapeDtypeStruct((depth, columns), jnp.bfloat16),
        ],
        compiler_params=kernel_params(40),
        cost_estimate=cost(tokens * depth * columns, tokens * columns),
        name="project",
    )(flat, x, bias, *chains[0], *chains[1])


def backward_dot_kernel(dy_ref, w_ref, out_ref, sum_ref):
    step = pl.program_id(0)
    weight = w_ref[...].reshape(out_ref.shape[1], w_ref.shape[-1])
    part = dot_nt(dy_ref[...], weight)

    @pl.when(step == 0)
    def _():
        sum_ref[...] = part

    @pl.when(step > 0)
    def _():
        sum_ref[...] += part

    @pl.when(step == pl.num_programs(0) - 1)
    def _():
        out_ref[...] = sum_ref[...].astype(out_ref.dtype)


def backward_dot(dy, weight, first, dtype, name):
    tokens, columns = dy.shape
    depth = columns
    return pl.pallas_call(
        backward_dot_kernel,
        grid=(columns // COL_BLOCK,),
        in_specs=[
            pl.BlockSpec((tokens, COL_BLOCK), lambda i: (0, i)),
            weight_spec(weight, first, COL_BLOCK, lambda i: i),
        ],
        out_specs=pl.BlockSpec((tokens, depth), lambda i: (0, 0)),
        out_shape=jax.ShapeDtypeStruct((tokens, depth), dtype),
        scratch_shapes=[pltpu.VMEM((tokens, depth), jnp.float32)],
        compiler_params=kernel_params(40),
        cost_estimate=cost(tokens * depth * columns, tokens * columns),
        name=name,
    )(dy, weight)


def project_back_kernel(
    low_ref, high_ref, w_ref, x_ref, scale_ref, carry_ref, out_ref, shift_sum_ref, scale_sum_ref, total
):
    step = pl.program_id(0)

    @pl.when(step == 0)
    def _():
        total[...] = dot_nt(low_ref[0], w_ref[...])

    @pl.when((step > 0) & (step % 2 == 0))
    def _():
        total[...] += dot_nt(low_ref[0], w_ref[...])

    @pl.when(step % 2 == 1)
    def _():
        total[...] += dot_nt(high_ref[0], w_ref[...])

    @pl.when(step == pl.num_programs(0) - 1)
    def _():
        gain = 1.0 + scale_ref[...]
        shift_sum = jnp.zeros(gain.shape, jnp.float32)
        scale_sum = jnp.zeros(gain.shape, jnp.float32)
        for start in range(0, x_ref.shape[0], NORM_ROWS):
            rows = slice(start, start + NORM_ROWS)
            values = x_ref[rows, :].astype(jnp.float32)
            centred = values - jnp.mean(values, axis=-1, keepdims=True)
            variance = jnp.mean(centred * centred, axis=-1, keepdims=True)
            inverse = lax.rsqrt(variance + EPS_NORM)
            normal = centred * inverse
            grad = total[rows, :]
            shift_sum += jnp.sum(grad, axis=0, keepdims=True)
            scale_sum += jnp.sum(grad * normal, axis=0, keepdims=True)
            inner = grad * gain
            average = jnp.mean(inner, axis=-1, keepdims=True)
            along = jnp.mean(inner * normal, axis=-1, keepdims=True)
            out_ref[rows, :] = carry_ref[rows, :] + inverse * (inner - average - normal * along)
        shift_sum_ref[...] = shift_sum
        scale_sum_ref[...] = scale_sum


def project_back(low, high, weight, x, scale, carry):
    groups, tokens, width = low.shape
    depth = weight.shape[0]
    block = pl.BlockSpec((1, tokens, width), lambda i: (i // 2, 0, 0))
    whole = pl.BlockSpec((tokens, depth), lambda i: (0, 0))
    line = pl.BlockSpec((1, depth), lambda i: (0, 0))
    row = jax.ShapeDtypeStruct((1, depth), jnp.float32)
    return pl.pallas_call(
        project_back_kernel,
        grid=(2 * groups,),
        in_specs=[
            block,
            block,
            pl.BlockSpec((depth, width), lambda i: (0, i)),
            whole,
            line,
            whole,
        ],
        out_specs=[whole, line, line],
        out_shape=[jax.ShapeDtypeStruct((tokens, depth), jnp.float32), row, row],
        scratch_shapes=[pltpu.VMEM((tokens, depth), jnp.float32)],
        compiler_params=kernel_params(48),
        cost_estimate=cost(groups * tokens * depth * width, tokens * width),
        name="project_back",
    )(low, high, weight, x, scale, carry)


def store_pieces(total, own_core, place_of, keep_ref, send_ref):
    rows = keep_ref.shape[-2]
    pieces = total.shape[0] // rows
    low = total.astype(jnp.bfloat16).reshape(pieces // 2, 2, rows, total.shape[1])
    here = own_core == 0
    for slot in range(pieces // 2):
        first, second = low[slot, 0], low[slot, 1]
        keep_ref[place_of(slot)] = jnp.where(here, first, second)
        send_ref[place_of(slot)] = jnp.where(here, second, first)


def weight_grad_kernel(table, first, own_ref, x_ref, dx_ref, y_ref, dy_ref, keep_ref, send_ref, left):
    step = pl.program_id(0)

    def place_of(slot):
        return own_ref[1] ^ table[slot], 0

    if first:

        @pl.when(step == 0)
        def _():
            left[...] = x_ref[...].T

    @pl.when(step == first)
    def _():
        left[...] = y_ref[...].T

    right = jnp.where(step < first, dx_ref[...], dy_ref[0]) if first else dy_ref[0]
    store_pieces(dot_nn(left[...], right), own_ref[0], place_of, keep_ref, send_ref)


def weight_grad(own, x, dx, y, dy, table, rows, name):
    tokens, depth = y.shape
    first = 0 if dx is None else dx.shape[1] // COL_BLOCK
    groups = dy.shape[0]
    blocks = first + groups
    whole = pl.BlockSpec((tokens, depth), lambda i, own: (0, 0))
    block = pl.BlockSpec((len(table), 1, rows, COL_BLOCK), lambda i, own: (0, i, 0, 0))
    half = jax.ShapeDtypeStruct((len(table), blocks, rows, COL_BLOCK), jnp.bfloat16)
    if dx is None:
        x, dx = y, y
    return pl.pallas_call(
        partial(weight_grad_kernel, table, first),
        grid_spec=pltpu.PrefetchScalarGridSpec(
            num_scalar_prefetch=1,
            grid=(blocks,),
            in_specs=[
                whole,
                pl.BlockSpec(
                    (tokens, COL_BLOCK), lambda i, own: (0, jnp.clip(i, 0, max(first - 1, 0)))
                ),
                whole,
                pl.BlockSpec(
                    (1, tokens, COL_BLOCK), lambda i, own: (jnp.maximum(i - first, 0), 0, 0)
                ),
            ],
            out_specs=[block, block],
            scratch_shapes=[pltpu.VMEM((depth, tokens), jnp.bfloat16)],
        ),
        out_shape=[half, half],
        compiler_params=kernel_params(40),
        cost_estimate=cost(tokens * depth * blocks * COL_BLOCK, tokens * blocks * COL_BLOCK),
        name=name,
    )(own, x, dx, y, dy)


def place_units_kernel(own_ref, *refs):
    sources, (expand_ref, shrink_ref) = refs[:4], refs[4:]
    for flip, source in enumerate(sources):
        at = own_ref[0] ^ flip
        rows = expand_ref.shape[0] // 4
        place = pl.ds(pl.multiple_of(at * rows, rows), rows)
        width = source.shape[2]
        for block in range(expand_ref.shape[1] // width):
            piece = source[0, block * rows : (block + 1) * rows, :]
            expand_ref[place, block * width : (block + 1) * width] = piece.astype(jnp.float32)
        rows = source.shape[1]
        place = pl.ds(pl.multiple_of(at * rows, rows), rows)
        shrink_ref[place, :] = source[1].astype(jnp.float32)


def place_attention_kernel(own_ref, *refs):
    sources, (out_ref, proj_ref) = refs[:4], refs[4:]
    for flip, source in enumerate(sources):
        blocks, rows, width = source.shape
        place = pl.ds(pl.multiple_of((own_ref[0] ^ flip) * rows, rows), rows)
        for block in range(blocks):
            piece = source[block].astype(jnp.float32)
            if block < 2:
                out_ref[place, block * width : (block + 1) * width] = piece
            else:
                group, half = (block - 2) % 3, (block - 2) // 3
                start = (2 * group + half) * width
                proj_ref[place, start : start + width] = piece


def place_reps(kernel, rep_id, own, shapes, name):
    across = exchange(own, *MASKS["y"])
    parts = [own, exchange(own, *MASKS["core"]), across, exchange(across, *MASKS["core"])]
    return pl.pallas_call(
        kernel,
        grid_spec=pltpu.PrefetchScalarGridSpec(num_scalar_prefetch=1, grid=()),
        out_shape=[jax.ShapeDtypeStruct(shape, jnp.float32) for shape in shapes],
        compiler_params=kernel_params(32),
        cost_estimate=cost(2**20, 2**20),
        name=name,
    )(rep_id.astype(jnp.int32)[None], *parts)


def feed_forward_kernel(
    table,
    own_ref,
    norm_ref,
    grad_ref,
    expand_ref,
    bias_ref,
    shrink_ref,
    branch_ref,
    d_norm_ref,
    keep_e_ref,
    send_e_ref,
    keep_s_ref,
    send_s_ref,
    d_bias_ref,
    norm_t,
    hidden,
    d_pre,
):
    tokens, depth = norm_ref.shape
    units = hidden.shape[1]
    step = pl.program_id(0)
    expand = expand_ref[...].reshape(depth, units)
    shrink = shrink_ref[...].reshape(units, depth)

    @pl.when(step == 0)
    def _():
        norm_t[...] = norm_ref[...].T
        branch_ref[...] = jnp.zeros_like(branch_ref)
        d_norm_ref[...] = jnp.zeros_like(d_norm_ref)

    bias_sum = jnp.zeros((1, units), jnp.float32)
    starts = list(range(0, tokens, ROWS))

    def entering(start):
        rows = slice(start, start + ROWS)
        return dot_nn(norm_ref[rows, :], expand), dot_nt(grad_ref[rows, :], shrink)

    upcoming = entering(starts[0])
    for number, start in enumerate(starts):
        rows = slice(start, start + ROWS)
        pre, d_unit = upcoming
        if number + 1 < len(starts):
            upcoming = entering(starts[number + 1])
        pre = pre + bias_ref[...]
        square = pre * pre
        bend = jnp.tanh(GELU_ROOT * pre * (1.0 + GELU_CUBE * square))
        rise = 0.5 + 0.5 * bend
        unit = (pre * rise).astype(jnp.bfloat16)
        hidden[rows, :] = unit
        slope = rise + 0.5 * pre * (1.0 - bend * bend) * (
            GELU_ROOT + (3.0 * GELU_ROOT * GELU_CUBE) * square
        )
        d_low = (d_unit * slope).astype(jnp.bfloat16)
        d_pre[rows, :] = d_low
        bias_sum = bias_sum + jnp.sum(d_low.astype(jnp.float32), axis=0, keepdims=True)
        branch_ref[rows, :] += dot_nn(unit, shrink)
        d_norm_ref[rows, :] += dot_nt(d_low, expand)
    d_bias_ref[...] = bias_sum
    store_pieces(
        dot_tn(hidden[...], grad_ref[...]),
        own_ref[0],
        lambda slot: (0, own_ref[3] ^ slot, 0),
        keep_s_ref,
        send_s_ref,
    )
    store_pieces(
        dot_nn(norm_t[...], d_pre[...]),
        own_ref[0],
        lambda slot: (own_ref[1] ^ table[slot], 0),
        keep_e_ref,
        send_e_ref,
    )


def feed_forward(own, norm, grad, expand, bias, shrink, table):
    tokens, depth = norm.shape
    total = bias.shape[1]
    steps = total // FF_BLOCK
    slots = len(table)
    rows_e = depth // (2 * slots)
    per = depth // FF_BLOCK
    whole = pl.BlockSpec((tokens, depth), lambda i, own: (0, 0))
    half_e = pl.BlockSpec(
        (slots, 1, rows_e, FF_BLOCK), lambda i, own: (0, i // per, 0, i % per)
    )
    if slots > 1:
        spec_e = weight_spec(expand, 4, FF_BLOCK, lambda i, own: i)
        spec_s = pl.BlockSpec(
            (shrink.shape[0] // steps, 4) + shrink.shape[2:], lambda i, own: (i, 0, 0, 0)
        )
        shape_s = (2, 2, steps // 2, FF_BLOCK // 4, depth)
        half_s = pl.BlockSpec(
            (1, 2, 1, FF_BLOCK // 4, depth),
            lambda i, own: ((i & 1) ^ own[2], 0, ((i & 2) | (i >> 2)) ^ own[4], 0, 0),
        )
    else:
        spec_e = weight_spec(expand, 0, FF_BLOCK, lambda i, own: i)
        spec_s = pl.BlockSpec((FF_BLOCK, depth), lambda i, own: (i, 0))
        shape_s = (1, 1, steps, FF_BLOCK // 2, depth)
        half_s = pl.BlockSpec((1, 1, 1, FF_BLOCK // 2, depth), lambda i, own: (0, 0, i, 0, 0))
    line = pl.BlockSpec((1, FF_BLOCK), lambda i, own: (0, i))
    wide = jax.ShapeDtypeStruct((tokens, depth), jnp.float32)
    out_e = jax.ShapeDtypeStruct((slots, total // depth, rows_e, depth), jnp.bfloat16)
    out_s = jax.ShapeDtypeStruct(shape_s, jnp.bfloat16)
    return pl.pallas_call(
        partial(feed_forward_kernel, table),
        grid_spec=pltpu.PrefetchScalarGridSpec(
            num_scalar_prefetch=1,
            grid=(steps,),
            in_specs=[whole, whole, spec_e, line, spec_s],
            out_specs=[whole, whole, half_e, half_e, half_s, half_s, line],
            scratch_shapes=[
                pltpu.VMEM((depth, tokens), jnp.bfloat16),
                pltpu.VMEM((tokens, FF_BLOCK), jnp.bfloat16),
                pltpu.VMEM((tokens, FF_BLOCK), jnp.bfloat16),
            ],
        ),
        out_shape=[
            wide,
            wide,
            out_e,
            out_e,
            out_s,
            out_s,
            jax.ShapeDtypeStruct((1, total), jnp.float32),
        ],
        compiler_params=kernel_params(56),
        cost_estimate=cost(6 * tokens * depth * total, 16 * 2**20, tokens * total),
        name="feed_forward",
    )(own, norm, grad, expand, bias, shrink)


def attention_forward_kernel(q_ref, k_ref, v_ref, out_ref, out_t_ref, lse_ref):
    length = q_ref.shape[0]
    scaled = q_ref[...] * jnp.bfloat16(HEAD_DIM ** (-0.5))
    keys = k_ref[...]
    values_t = v_ref[...].T
    ones = jnp.ones((16, length), jnp.bfloat16)
    extended = [
        jnp.concatenate([values_t[head * HEAD_DIM : (head + 1) * HEAD_DIM], ones], axis=0)
        for head in range(2)
    ]
    tasks = [(start, head) for start in range(0, length, CHUNK) for head in range(2)]

    def scores_of(task):
        start, head = task
        cols = slice(head * HEAD_DIM, (head + 1) * HEAD_DIM)
        return dot_nt(keys[:, cols], scaled[start : start + CHUNK, cols])

    upcoming = scores_of(tasks[0])
    pieces = []
    for number, (start, head) in enumerate(tasks):
        scores = upcoming
        if number + 1 < len(tasks):
            upcoming = scores_of(tasks[number + 1])
        rows = slice(start, start + CHUNK)
        top = jnp.max(scores, axis=0, keepdims=True)
        terms = jnp.exp(scores - top).astype(jnp.bfloat16)
        part = dot_nn(extended[head], terms)
        total = part[HEAD_DIM : HEAD_DIM + 1]
        piece = part[:HEAD_DIM] / total
        lse_ref[0, head : head + 1, rows] = top + jnp.log(total)
        out_t_ref[head * HEAD_DIM : (head + 1) * HEAD_DIM, rows] = piece
        pieces.append(piece)
        if head == 1:
            out_ref[rows, :] = jnp.concatenate(pieces, axis=0).T.astype(jnp.bfloat16)
            pieces = []


def attention_forward(projected):
    length = projected.shape[0]
    pairs = HEADS // 2
    return pl.pallas_call(
        attention_forward_kernel,
        grid=(pairs,),
        in_specs=[
            pl.BlockSpec((length, PAIR), lambda i: (0, i)),
            pl.BlockSpec((length, PAIR), lambda i: (0, pairs + i)),
            pl.BlockSpec((length, PAIR), lambda i: (0, 2 * pairs + i)),
        ],
        out_specs=[
            pl.BlockSpec((length, PAIR), lambda i: (0, i)),
            pl.BlockSpec((PAIR, length), lambda i: (i, 0)),
            pl.BlockSpec((1, 2, length), lambda i: (i, 0, 0)),
        ],
        out_shape=[
            jax.ShapeDtypeStruct((length, HEADS * HEAD_DIM), jnp.bfloat16),
            jax.ShapeDtypeStruct((HEADS * HEAD_DIM, length), jnp.float32),
            jax.ShapeDtypeStruct((pairs, 2, length), jnp.float32),
        ],
        compiler_params=kernel_params(48),
        cost_estimate=cost(2**32, 8 * 2**20, 2**24),
        name="attention_forward",
    )(projected, projected, projected)


def attention_backward_kernel(q_ref, k_ref, v_ref, g_ref, o_ref, lse_ref, *refs):
    out_ref, qb_ref, vb_ref, probs, d_scores = refs[-5:]
    length = q_ref.shape[0]
    root = HEAD_DIM ** (-0.5)
    scaled = q_ref[...] * jnp.bfloat16(root)
    keys = k_ref[...]
    values = v_ref[...]
    grads = g_ref[...]
    keys_t = keys.T
    product = grads.T.astype(jnp.float32) * o_ref[...]
    sums_k = [None, None]
    sums_v = [None, None]
    sum_q = None
    pieces = []
    tasks = [(start, head) for start in range(0, length, CHUNK) for head in range(2)]
    for number, (start, head) in enumerate(tasks):
        rows = slice(start, start + CHUNK)
        slot = number % 2
        cols = slice(head * HEAD_DIM, (head + 1) * HEAD_DIM)
        query, grad = scaled[rows, cols], grads[rows, cols]
        lse = lse_ref[0, head : head + 1, rows]
        row_sum = jnp.sum(product[cols, rows], axis=0, keepdims=True)
        for block in range(0, length, KEY_BLOCK):
            some = slice(block, block + KEY_BLOCK)
            prob = jnp.exp(dot_nt(keys[some, cols], query) - lse)
            d_prob = dot_nt(values[some, cols], grad)
            probs[slot, some, :] = prob.astype(jnp.bfloat16)
            d_scores[slot, some, :] = (prob * (d_prob - row_sum)).astype(jnp.bfloat16)
        part_v = dot_nn(probs[slot], grad)
        part_k = dot_nn(d_scores[slot], query)
        sums_v[head] = part_v if start == 0 else sums_v[head] + part_v
        sums_k[head] = part_k if start == 0 else sums_k[head] + part_k
        pieces.append(dot_nn(keys_t[cols, :], d_scores[slot]) * root)
        if head == 1:
            d_query = jnp.concatenate(pieces, axis=0).T.astype(jnp.bfloat16)
            pieces = []
            out_ref[0, rows, :] = d_query
            part_q = jnp.sum(d_query.astype(jnp.float32), axis=0, keepdims=True)
            sum_q = part_q if start == 0 else sum_q + part_q
    out_ref[1] = jnp.concatenate(sums_k, axis=1).astype(jnp.bfloat16)
    d_value = jnp.concatenate(sums_v, axis=1).astype(jnp.bfloat16)
    out_ref[2] = d_value
    qb_ref[...] = sum_q
    vb_ref[...] = jnp.sum(d_value.astype(jnp.float32), axis=0, keepdims=True)


def attention_backward(operands, first, count, total, at, into, name):
    projected, d_attended, attended_t, lse = operands
    length = projected.shape[0]
    pairs = HEADS // 2
    row = pl.BlockSpec((1, PAIR), lambda i: (0, i))
    line = jax.ShapeDtypeStruct((1, count * PAIR), jnp.float32)
    in_specs = [
        pl.BlockSpec((length, PAIR), lambda i: (0, first + i)),
        pl.BlockSpec((length, PAIR), lambda i: (0, pairs + first + i)),
        pl.BlockSpec((length, PAIR), lambda i: (0, 2 * pairs + first + i)),
        pl.BlockSpec((length, PAIR), lambda i: (0, first + i)),
        pl.BlockSpec((PAIR, length), lambda i: (first + i, 0)),
        pl.BlockSpec((1, 2, length), lambda i: (first + i, 0, 0)),
    ]
    arrays = [projected, projected, projected, d_attended, attended_t, lse]
    aliases = {}
    if into is not None:
        in_specs.append(pl.BlockSpec(memory_space=pl.ANY))
        aliases = {len(arrays): 0}
        arrays.append(into)
    return pl.pallas_call(
        attention_backward_kernel,
        grid=(count,),
        in_specs=in_specs,
        out_specs=[pl.BlockSpec((3, length, PAIR), lambda i: (0, 0, at + i)), row, row],
        out_shape=[jax.ShapeDtypeStruct((3, length, total * PAIR), jnp.bfloat16), line, line],
        input_output_aliases=aliases,
        scratch_shapes=[
            pltpu.VMEM((2, length, CHUNK), jnp.bfloat16),
            pltpu.VMEM((2, length, CHUNK), jnp.bfloat16),
        ],
        compiler_params=kernel_params(48),
        cost_estimate=cost(count * 2**29, count * 2 * 2**20, count * 2**21),
        name=name,
    )(*arrays)


def normalize(values):
    average = jnp.mean(values, axis=-1, keepdims=True)
    centred = values - average
    variance = jnp.mean(centred * centred, axis=-1, keepdims=True)
    return centred * lax.rsqrt(variance + EPS_NORM)


def modulate(values, shifts, scales):
    return normalize(values) * (1.0 + scales[:, None, :]) + shifts[:, None, :]


MASKS = {"core": (1, 0), "y": (2, 0), "x": (0, 1), "z1": (0, 2), "z2": (0, 4)}
GATHER_ORDERS = (("z2", "z1", "x", "y"), ("z2", "z1", "y", "x"))


def exchange(value, rep_mask, fsdp_mask):
    reps, shards = lax.axis_size("rep"), lax.axis_size("fsdp")
    pairs = [
        (rep * shards + shard, (rep ^ rep_mask) * shards + (shard ^ fsdp_mask))
        for rep in range(reps)
        for shard in range(shards)
    ]
    return lax.ppermute(value, ("rep", "fsdp"), pairs)


def gather_relative(row, after_first):
    reps, shards = lax.axis_size("rep"), lax.axis_size("fsdp")
    masks = [(0, 1 << bit) for bit in reversed(range(shards.bit_length() - 1))]
    masks += [(1 << bit, 0) for bit in reversed(range(reps.bit_length() - 1))]
    rows = row[None]
    for number, pair in enumerate(masks):
        rows = jnp.concatenate([rows, exchange(rows, *pair)], axis=0)
        if number == 0:
            rows = after_first(rows)
    return rows


def gather_chain(quarter, order):
    rows = quarter[None]
    for name in order:
        rows = jnp.concatenate([rows, exchange(rows, *MASKS[name])], axis=0)
    return rows, exchange(rows, *MASKS["core"])


def chain_map(order):
    offsets = [0]
    for name in order:
        rep_mask, fsdp_mask = MASKS[name]
        offsets += [offset ^ (fsdp_mask * 4 + rep_mask) for offset in offsets]
    return tuple(offsets)


def to_absolute(parts, own):
    parts = list(parts)
    bit = 1
    while bit < len(parts):
        flipped = (own & bit) != 0
        parts = [jnp.where(flipped, parts[i ^ bit], parts[i]) for i in range(len(parts))]
        bit *= 2
    return parts


ORDERS = (("y", "x", "z1", "z2"), ("x", "y", "z1", "z2"))


def place_in(order, shard, y):
    bits = {"z2": (shard >> 2) & 1, "z1": (shard >> 1) & 1, "x": shard & 1, "y": y}
    place = 0
    for name in order:
        place = place * 2 + bits[name]
    return place


class HalvingSum:
    def __init__(self, halves, order):
        keep, send = halves
        self.masks = [MASKS[name] for name in order]
        self.stay = keep
        self.arrived = exchange(send, *MASKS["core"])

    def added(self, start, stop):
        stay, arrived = self.stay[start:stop], self.arrived[start:stop]
        return (stay.astype(jnp.float32) + arrived.astype(jnp.float32)).astype(jnp.bfloat16)

    def step(self):
        count = self.stay.shape[0]
        away = self.added(count // 2, count)
        self.stay = self.added(0, count // 2)
        self.arrived = exchange(away, *self.masks.pop(0))

    def finish(self):
        while self.masks:
            self.step()
        return self.added(0, 1)[0]


class PlainSum:
    def __init__(self, grad):
        self.arrived = grad

    def step(self):
        pass

    def finish(self):
        return scatter_rows(self.arrived)


def hold(value, *sums):
    held = lax.optimization_barrier((value, *[total.arrived for total in sums]))
    for total, arrived in zip(sums, held[1:]):
        total.arrived = arrived
    return held[0]


def scatter_rows(grad):
    own = lax.psum_scatter(grad, ("fsdp", "rep"), scatter_dimension=0, tiled=True)
    return lax.all_gather(own, "rep", axis=0, tiled=True).astype(jnp.float32)


def own_quarter(weight):
    part = weight.shape[0] // lax.axis_size("rep")
    return lax.dynamic_slice_in_dim(weight, lax.axis_index("rep") * part, part, 0)


def gather_rows(weight):
    return lax.all_gather(own_quarter(weight), ("fsdp", "rep"), axis=0, tiled=True)


def column_blocks(quarter, width):
    rows = quarter.shape[0]
    blocks = quarter.shape[1] // width
    return quarter.reshape(rows, blocks, width).transpose(1, 0, 2).reshape(blocks * rows, width)


def gather_packed(parts, rows):
    packed = jnp.concatenate(parts, axis=0)
    blocks, width = packed.shape[0] // rows, packed.shape[1]
    full = lax.all_gather(packed, ("fsdp", "rep"), axis=0, tiled=True)
    return full.reshape(full.shape[0] // packed.shape[0], blocks, rows, width)


def on_device(
    latents,
    conditions,
    modulator,
    modulbias,
    projector,
    querybias,
    valuebias,
    outweight,
    outbiases,
    expander,
    expandbias,
    shrinker,
    shrinkbias,
    upstream,
):
    seqs_dev, seq_len, feature = latents.shape
    token_count = seqs_dev * seq_len
    shard_id, rep_id = lax.axis_index("fsdp"), lax.axis_index("rep")
    shards, reps = lax.axis_size("fsdp"), lax.axis_size("rep")
    halving = shards == 8 and reps == 4
    own_rows = modulator.shape[0]
    own_bias = modulbias.shape[0]

    width = projector.shape[1]
    if halving:
        quarter = own_rows // reps
        proj_quarter = own_quarter(projector)
        chains = [
            gather_chain(proj_quarter[:, part * (width // 2) : (part + 1) * (width // 2)], order)
            for part, order in enumerate(GATHER_ORDERS)
        ]
        maps = [chain_map(order) for order in GATHER_ORDERS]
        packed = gather_packed(
            [
                own_quarter(shrinker),
                column_blocks(own_quarter(expander), feature),
                own_quarter(outweight),
            ],
            quarter,
        )
        out_at = (packed, 8)
        w_expand, w_shrink = packed, packed
        y_id = rep_id >> 1
        own = jnp.stack(
            [
                rep_id & 1,
                place_in(ORDERS[0], shard_id, y_id),
                shard_id & 1,
                y_id,
                (shard_id & 2) | (shard_id >> 2),
            ]
        ).astype(jnp.int32)
        table = tuple(place_in(ORDERS[0], slot >> 1, slot & 1) for slot in range(2 * shards))
        piece = quarter
    else:
        w_proj, out_at = gather_rows(projector), (gather_rows(outweight), 0)
        w_expand, w_shrink = gather_rows(expander), gather_rows(shrinker)
        own = jnp.zeros((5,), jnp.int32)
        table = (0,)
        piece = feature // 2

    def depth_sum(halves, order):
        if halving:
            return HalvingSum(halves, order)
        columns = [half[0].transpose(1, 0, 2).reshape(feature // 2, -1) for half in halves]
        return PlainSum(jnp.concatenate(columns, axis=0))

    def unit_sum(halves, order):
        if halving:
            return HalvingSum([half.reshape(16, -1, feature) for half in halves], order)
        blocks = [half.reshape(-1, 1, FF_BLOCK // 2, feature) for half in halves]
        return PlainSum(jnp.concatenate(blocks, axis=1).reshape(-1, feature))

    cond_full = conditions.astype(jnp.float32)
    cond_slice = lax.dynamic_slice_in_dim(cond_full, shard_id * own_rows, own_rows, 1)
    cond_act = jax.nn.silu(cond_slice).astype(jnp.bfloat16)
    cond_own = lax.dynamic_slice_in_dim(cond_full, shard_id * seqs_dev, seqs_dev, 0)
    cond_own = jax.nn.silu(cond_own).astype(jnp.bfloat16)
    mod_term = jnp.dot(cond_act, modulator, preferred_element_type=jnp.float32)
    bias_parts = (modulbias, querybias, valuebias, outbiases, expandbias, shrinkbias)
    own_biases = jnp.concatenate([part.astype(jnp.float32) for part in bias_parts])
    mod_width = seqs_dev * 6 * feature
    sent = jnp.concatenate(
        [
            mod_term.reshape(shards, mod_width),
            jnp.broadcast_to(own_biases[None, :], (shards, own_biases.shape[0])),
        ],
        axis=1,
    )
    got = lax.all_to_all(sent, "fsdp", split_axis=0, concat_axis=0, tiled=True)
    full_biases = []
    start = mod_width
    for part in bias_parts:
        full_biases.append(got[:, start : start + part.shape[0]].reshape(1, -1))
        start += part.shape[0]
    full_modbias, b_query, b_value, b_out, b_expand, b_shrink = full_biases
    modvals = jnp.sum(got[:, :mod_width], axis=0).reshape(seqs_dev, 6, feature)
    modvals = modvals + full_modbias.reshape(1, 6, feature)
    shift_a, scale_a, gate_a = (modvals[:, 0], modvals[:, 1], modvals[:, 2])
    shift_m, scale_m, gate_m = (modvals[:, 3], modvals[:, 4], modvals[:, 5])

    resid_in = latents.astype(jnp.float32)
    norm_a = modulate(resid_in, shift_a, scale_a).astype(jnp.bfloat16).reshape(token_count, feature)
    b_proj = jnp.concatenate([b_query, jnp.zeros_like(b_query), b_value], axis=1)
    if halving:
        flat = (shard_id * reps + rep_id).astype(jnp.int32)[None]
        projected, w_proj = project(flat, norm_a, b_proj, chains, maps)
    else:
        projected = forward_dot(norm_a, w_proj, 0, b_proj, jnp.bfloat16, "project")
    attended, attended_t, log_totals = attention_forward(projected)
    branch_a = forward_dot(attended, *out_at, b_out, jnp.float32, "attention_out")
    branch_a = branch_a.reshape(seqs_dev, seq_len, feature)
    middle = resid_in + gate_a[:, None, :] * branch_a
    norm_m = modulate(middle, shift_m, scale_m).astype(jnp.bfloat16).reshape(token_count, feature)

    grad_out = upstream.astype(jnp.float32)
    d_branch_m = (gate_m[:, None, :] * grad_out).astype(jnp.bfloat16).reshape(token_count, feature)
    g_shrinkbias = jnp.sum(d_branch_m, axis=0, dtype=jnp.float32)
    branch_m, d_norm_m, keep_e, send_e, keep_s, send_s, g_expandbias = feed_forward(
        own, norm_m, d_branch_m, w_expand, b_expand, w_shrink, table
    )
    sum_e = depth_sum((keep_e, send_e), ORDERS[0])
    sum_s = unit_sum((keep_s, send_s), ORDERS[1])
    branch_m = (branch_m + b_shrink).reshape(seqs_dev, seq_len, feature)
    layer_out = middle + gate_m[:, None, :] * branch_m
    d_gate_m = jnp.sum(grad_out * branch_m, axis=1)
    d_norm_m, layer_out, d_gate_m = hold((d_norm_m, layer_out, d_gate_m), sum_e, sum_s)
    sum_e.step()
    sum_s.step()
    _, norm_pull_m = jax.vjp(modulate, middle, shift_m, scale_m)
    d_mid_norm, d_shift_m, d_scale_m = norm_pull_m(d_norm_m.reshape(seqs_dev, seq_len, feature))
    d_middle = grad_out + d_mid_norm
    d_branch_a = (gate_a[:, None, :] * d_middle).astype(jnp.bfloat16).reshape(token_count, feature)
    d_gate_a = jnp.sum(d_middle * branch_a, axis=1)
    g_outbiases = jnp.sum(d_branch_a, axis=0, dtype=jnp.float32)
    d_attended = backward_dot(d_branch_a, *out_at, jnp.bfloat16, "attention_out_back")
    half_pairs = HEADS // 4
    part_pairs = half_pairs // 2
    d_low, q_low, v_low = attention_backward(
        (projected, d_attended, attended_t, log_totals),
        0,
        half_pairs,
        half_pairs,
        0,
        None,
        "attention_backward_low",
    )
    halves_low = weight_grad(
        own, attended, d_branch_a, norm_a, d_low, table, piece, "weight_grad_low"
    )
    d_attended, halves_low = hold((d_attended, halves_low), sum_e, sum_s)
    sum_low = depth_sum(halves_low, ORDERS[0])
    for total in (sum_e, sum_s):
        total.step()
    d_high, *sums_mid = attention_backward(
        (projected, d_attended, attended_t, log_totals),
        half_pairs,
        part_pairs,
        half_pairs,
        0,
        None,
        "attention_backward_mid",
    )
    d_high = hold(d_high, sum_e, sum_s, sum_low)
    for total in (sum_e, sum_s, sum_low):
        total.step()
    d_high, *sums_high = attention_backward(
        (projected, d_attended, attended_t, log_totals),
        half_pairs + part_pairs,
        part_pairs,
        half_pairs,
        part_pairs,
        d_high,
        "attention_backward_high",
    )
    q_high, v_high = [jnp.concatenate(parts, axis=1) for parts in zip(sums_mid, sums_high)]
    halves_high = weight_grad(
        own, None, None, norm_a, d_high, table, piece, "weight_grad_high"
    )
    d_high, halves_high = hold((d_high, halves_high), sum_e, sum_s, sum_low)
    sum_high = depth_sum(halves_high, ORDERS[0])
    for total in (sum_e, sum_s, sum_low):
        total.step()
    d_high = hold(d_high, sum_high)
    sum_high.step()
    latents_grad, d_shift_a, d_scale_a = project_back(
        d_low,
        d_high,
        w_proj,
        latents.reshape(token_count, feature),
        scale_a,
        d_middle.reshape(token_count, feature),
    )
    latents_grad = latents_grad.reshape(seqs_dev, seq_len, feature)
    g_querybias = jnp.concatenate([q_low, q_high], axis=1)
    g_valuebias = jnp.concatenate([v_low, v_high], axis=1)
    small = jnp.concatenate(
        [
            part.astype(jnp.float32).reshape(-1, 128)
            for part in (
                d_shift_a,
                d_scale_a,
                d_gate_a,
                d_shift_m,
                d_scale_m,
                d_gate_m,
                cond_own,
                g_querybias,
                g_valuebias,
                g_outbiases,
                g_expandbias,
                g_shrinkbias,
                jnp.zeros((feature,)),
            )
        ]
    ).astype(jnp.bfloat16)
    devices = reps * shards
    size = seqs_dev * feature

    def advance(rows):
        rows = hold(rows, sum_e, sum_s, sum_low, sum_high)
        for total in (sum_low, sum_high):
            total.step()
        return rows

    gathered = gather_relative(small, advance)
    if halving:
        done = jnp.stack([total.finish().reshape(-1, feature) for total in (sum_e, sum_s)])
        g_expander, g_shrinker = place_reps(
            place_units_kernel, rep_id, done, (expander.shape, shrinker.shape), "place_units"
        )
        done = jnp.concatenate([sum_low.finish(), sum_high.finish()], axis=0)
        g_outweight, g_projector = place_reps(
            place_attention_kernel, rep_id, done, (outweight.shape, projector.shape), "place_attention"
        )
    else:
        g_expander, g_shrinker = sum_e.finish(), sum_s.finish()
        low, high = sum_low.finish(), sum_high.finish()
        g_outweight = low[:, :feature]
        g_projector = jnp.stack(
            [low[:, feature:].reshape(own_rows, 3, -1), high.reshape(own_rows, 3, -1)], axis=2
        ).reshape(own_rows, 3 * feature)

    lines = size // 128
    cond_all = gathered[:, 6 * lines : 7 * lines].reshape(devices * seqs_dev, feature)
    cond_all = lax.dynamic_slice_in_dim(cond_all, shard_id * own_rows, own_rows, 1)
    d_mod = gathered[:, : 6 * lines].reshape(devices, 6, seqs_dev, feature).transpose(0, 2, 1, 3)
    d_mod = d_mod.reshape(devices * seqs_dev, 6 * feature)
    bias_sums = jnp.sum(gathered[:, 7 * lines :], axis=0, dtype=jnp.float32).reshape(-1)
    bias_grads = []
    start = 0
    for total in (feature, feature, feature, expandbias.shape[0] * shards, feature):
        part = total // shards
        bias_grads.append(lax.dynamic_slice_in_dim(bias_sums, start + shard_id * part, part, 0))
        start += total
    g_modbias = jnp.sum(
        lax.dynamic_slice_in_dim(d_mod, shard_id * own_bias, own_bias, 1), axis=0, dtype=jnp.float32
    )
    g_modulator = jnp.einsum("sr,sc->rc", cond_all, d_mod, preferred_element_type=jnp.float32)
    own_mod = d_mod[: shards * seqs_dev]
    d_cond_act = jnp.einsum("sc,rc->sr", own_mod, modulator, preferred_element_type=jnp.float32)
    d_cond_act = d_cond_act.reshape(shards, seqs_dev, own_rows)
    bits = shards.bit_length() - 1
    turned = [sum(((i >> bit) & 1) << (bits - 1 - bit) for bit in range(bits)) for i in range(shards)]
    d_cond_act = jnp.stack(to_absolute([d_cond_act[i] for i in turned], shard_id))
    d_cond_act = d_cond_act.reshape(shards * seqs_dev, own_rows)
    _, silu_pull = jax.vjp(jax.nn.silu, cond_slice)
    conditions_grad = silu_pull(d_cond_act)[0]
    return (
        layer_out,
        latents_grad,
        conditions_grad,
        g_modulator,
        g_modbias,
        g_projector,
        bias_grads[0],
        bias_grads[1],
        g_outweight,
        bias_grads[2],
        g_expander,
        bias_grads[3],
        g_shrinker,
        bias_grads[4],
    )


def solution(mesh):
    return jax.shard_map(
        on_device,
        mesh=mesh,
        in_specs=(
            P(("rep", "fsdp"), None, None),
            P("rep", None),
            P("fsdp", None),
            P("fsdp"),
            P("fsdp", None),
            P("fsdp"),
            P("fsdp"),
            P("fsdp", None),
            P("fsdp"),
            P("fsdp", None),
            P("fsdp"),
            P("fsdp", None),
            P("fsdp"),
            P(("rep", "fsdp"), None, None),
        ),
        out_specs=(
            P(("rep", "fsdp"), None, None),
            P(("rep", "fsdp"), None, None),
            P("rep", "fsdp"),
            P("fsdp", None),
            P("fsdp"),
            P("fsdp", None),
            P("fsdp"),
            P("fsdp"),
            P("fsdp", None),
            P("fsdp"),
            P("fsdp", None),
            P("fsdp"),
            P("fsdp", None),
            P("fsdp"),
        ),
        check_vma=False,
    )
```

```python
from functools import partial

import jax
import jax.numpy as jnp
from jax import lax
from jax.experimental import pallas as pl
from jax.experimental.pallas import tpu as pltpu
from jax.sharding import PartitionSpec as P

HEADS = 16
HEAD_DIM = 64
PAIR = 2 * HEAD_DIM
CHUNK = 256
KEY_BLOCK = 128
NORM_ROWS = 128
MIDDLE_ROWS = 256
EPS_NORM = 1e-06
ROWS = 512
FF_BLOCK = 512
COL_BLOCK = 512
GELU_ROOT = 0.7978845608028654
GELU_CUBE = 0.044715


def dot_nn(left, right):
    return jnp.dot(left, right, preferred_element_type=jnp.float32)


def dot_nt(left, right):
    return lax.dot_general(left, right, (((1,), (1,)), ((), ())), preferred_element_type=jnp.float32)


def dot_tn(left, right):
    return lax.dot_general(left, right, (((0,), (0,)), ((), ())), preferred_element_type=jnp.float32)


def kernel_params(mebibytes):
    return pltpu.CompilerParams(vmem_limit_bytes=mebibytes * 2**20)


def cost(flops, moved, special=0):
    return pl.CostEstimate(flops=flops, bytes_accessed=moved, transcendentals=special)


def weight_spec(weight, first, width, order):
    if weight.ndim == 2:
        offset = first * weight.shape[0] // width
        return pl.BlockSpec((weight.shape[0], width), lambda *at: (0, offset + order(*at)))
    devices, _, rows, columns = weight.shape
    per = columns // width
    return pl.BlockSpec(
        (devices, 1, rows, width),
        lambda *at: (0, first + order(*at) // per, 0, order(*at) % per),
    )


def forward_dot_kernel(x_ref, w_ref, b_ref, out_ref):
    weight = w_ref[...].reshape(x_ref.shape[1], out_ref.shape[1])
    out_ref[...] = (dot_nn(x_ref[...], weight) + b_ref[...]).astype(out_ref.dtype)


def forward_dot(x, weight, first, bias, dtype, name):
    tokens, depth = x.shape
    columns = bias.shape[1]
    return pl.pallas_call(
        forward_dot_kernel,
        grid=(columns // COL_BLOCK,),
        in_specs=[
            pl.BlockSpec((tokens, depth), lambda i: (0, 0)),
            weight_spec(weight, first, COL_BLOCK, lambda i: i),
            pl.BlockSpec((1, COL_BLOCK), lambda i: (0, i)),
        ],
        out_specs=pl.BlockSpec((tokens, COL_BLOCK), lambda i: (0, i)),
        out_shape=jax.ShapeDtypeStruct((tokens, columns), dtype),
        compiler_params=kernel_params(40),
        cost_estimate=cost(tokens * depth * columns, tokens * columns),
        name=name,
    )(x, weight, bias)


def project_kernel(maps, own_ref, x_ref, b_ref, *refs):
    sources, (out_ref, full_ref) = refs[:4], refs[4:]
    step = pl.program_id(0)
    rows = sources[0].shape[1]
    half = pl.num_programs(0) // 2
    for chain in range(2):

        @pl.when((step >= half) == (chain == 1))
        def _():
            for flip in range(2):
                source = sources[2 * chain + flip]
                for index, relative in enumerate(maps[chain]):
                    place = pl.multiple_of((own_ref[0] ^ (relative ^ flip)) * rows, rows)
                    full_ref[pl.ds(place, rows), :] = source[index]

    out_ref[...] = (dot_nn(x_ref[...], full_ref[...]) + b_ref[...]).astype(out_ref.dtype)


def project(flat, x, bias, chains, maps):
    tokens, depth = x.shape
    columns = bias.shape[1]
    steps = columns // COL_BLOCK
    half = steps // 2
    blocks, rows, _ = chains[0][0].shape
    first = pl.BlockSpec((blocks, rows, COL_BLOCK), lambda i, own: (0, 0, jnp.minimum(i, half - 1)))
    second = pl.BlockSpec((blocks, rows, COL_BLOCK), lambda i, own: (0, 0, jnp.maximum(i - half, 0)))
    return pl.pallas_call(
        partial(project_kernel, maps),
        grid_spec=pltpu.PrefetchScalarGridSpec(
            num_scalar_prefetch=1,
            grid=(steps,),
            in_specs=[
                pl.BlockSpec((tokens, depth), lambda i, own: (0, 0)),
                pl.BlockSpec((1, COL_BLOCK), lambda i, own: (0, i)),
                first,
                first,
                second,
                second,
            ],
            out_specs=[
                pl.BlockSpec((tokens, COL_BLOCK), lambda i, own: (0, i)),
                pl.BlockSpec((depth, COL_BLOCK), lambda i, own: (0, i)),
            ],
        ),
        out_shape=[
            jax.ShapeDtypeStruct((tokens, columns), jnp.bfloat16),
            jax.ShapeDtypeStruct((depth, columns), jnp.bfloat16),
        ],
        compiler_params=kernel_params(40),
        cost_estimate=cost(tokens * depth * columns, tokens * columns),
        name="project",
    )(flat, x, bias, *chains[0], *chains[1])


def middle_back_kernel(
    branch_ref,
    grad_ref,
    middle_ref,
    up_ref,
    branch_a_ref,
    lines_ref,
    w_ref,
    layer_ref,
    d_middle_ref,
    d_branch_ref,
    d_attended_ref,
    sums_ref,
):
    bias, gate_m, scale, gate_a = [lines_ref[i : i + 1, :] for i in range(4)]
    values = middle_ref[...]
    above = up_ref[...].astype(jnp.float32)
    branch = branch_ref[...] + bias
    layer_ref[...] = values + gate_m * branch
    centred = values - jnp.mean(values, axis=-1, keepdims=True)
    inverse = lax.rsqrt(jnp.mean(centred * centred, axis=-1, keepdims=True) + EPS_NORM)
    normal = centred * inverse
    grad = grad_ref[...]
    inner = grad * (1.0 + scale)
    average = jnp.mean(inner, axis=-1, keepdims=True)
    along = jnp.mean(inner * normal, axis=-1, keepdims=True)
    d_middle = above + inverse * (inner - average - normal * along)
    d_middle_ref[...] = d_middle
    d_branch = (gate_a * d_middle).astype(jnp.bfloat16)
    d_branch_ref[...] = d_branch
    weight = w_ref[...].reshape(d_attended_ref.shape[1], d_branch.shape[1])
    d_attended_ref[...] = dot_nt(d_branch, weight).astype(jnp.bfloat16)
    parts = (
        above * branch,
        grad,
        grad * normal,
        d_middle * branch_a_ref[...],
        d_branch.astype(jnp.float32),
    )
    sums = [jnp.sum(part, axis=0, keepdims=True) for part in parts]
    sums = jnp.concatenate(sums + [jnp.zeros((3, bias.shape[1]), jnp.float32)], axis=0)
    step = pl.program_id(0)

    @pl.when(step == 0)
    def _():
        sums_ref[...] = sums

    @pl.when(step > 0)
    def _():
        sums_ref[...] += sums


def middle_back(branch, grad, middle, above, branch_a, lines, weight, first):
    tokens, depth = middle.shape
    block = pl.BlockSpec((MIDDLE_ROWS, depth), lambda i: (i, 0))
    fixed = pl.BlockSpec((8, depth), lambda i: (0, 0))
    wide = jax.ShapeDtypeStruct((tokens, depth), jnp.float32)
    low = jax.ShapeDtypeStruct((tokens, depth), jnp.bfloat16)
    return pl.pallas_call(
        middle_back_kernel,
        grid=(tokens // MIDDLE_ROWS,),
        in_specs=[block] * 5 + [fixed, weight_spec(weight, first, depth, lambda i: 0)],
        out_specs=[block] * 4 + [fixed],
        out_shape=[wide, wide, low, low, jax.ShapeDtypeStruct((8, depth), jnp.float32)],
        compiler_params=kernel_params(48),
        cost_estimate=cost(tokens * depth * depth, 8 * tokens * depth),
        name="middle_back",
    )(branch, grad, middle, above, branch_a, lines, weight)


def project_back_kernel(
    low_ref, high_ref, w_ref, x_ref, scale_ref, carry_ref, out_ref, shift_sum_ref, scale_sum_ref, total
):
    step = pl.program_id(0)

    @pl.when(step == 0)
    def _():
        total[...] = dot_nt(low_ref[0], w_ref[...])

    @pl.when((step > 0) & (step % 2 == 0))
    def _():
        total[...] += dot_nt(low_ref[0], w_ref[...])

    @pl.when(step % 2 == 1)
    def _():
        total[...] += dot_nt(high_ref[0], w_ref[...])

    @pl.when(step == pl.num_programs(0) - 1)
    def _():
        gain = 1.0 + scale_ref[...]
        shift_sum = jnp.zeros(gain.shape, jnp.float32)
        scale_sum = jnp.zeros(gain.shape, jnp.float32)
        for start in range(0, x_ref.shape[0], NORM_ROWS):
            rows = slice(start, start + NORM_ROWS)
            values = x_ref[rows, :].astype(jnp.float32)
            centred = values - jnp.mean(values, axis=-1, keepdims=True)
            variance = jnp.mean(centred * centred, axis=-1, keepdims=True)
            inverse = lax.rsqrt(variance + EPS_NORM)
            normal = centred * inverse
            grad = total[rows, :]
            shift_sum += jnp.sum(grad, axis=0, keepdims=True)
            scale_sum += jnp.sum(grad * normal, axis=0, keepdims=True)
            inner = grad * gain
            average = jnp.mean(inner, axis=-1, keepdims=True)
            along = jnp.mean(inner * normal, axis=-1, keepdims=True)
            out_ref[rows, :] = carry_ref[rows, :] + inverse * (inner - average - normal * along)
        shift_sum_ref[...] = shift_sum
        scale_sum_ref[...] = scale_sum


def project_back(low, high, weight, x, scale, carry):
    groups, tokens, width = low.shape
    depth = weight.shape[0]
    block = pl.BlockSpec((1, tokens, width), lambda i: (i // 2, 0, 0))
    whole = pl.BlockSpec((tokens, depth), lambda i: (0, 0))
    line = pl.BlockSpec((1, depth), lambda i: (0, 0))
    row = jax.ShapeDtypeStruct((1, depth), jnp.float32)
    return pl.pallas_call(
        project_back_kernel,
        grid=(2 * groups,),
        in_specs=[
            block,
            block,
            pl.BlockSpec((depth, width), lambda i: (0, i)),
            whole,
            line,
            whole,
        ],
        out_specs=[whole, line, line],
        out_shape=[jax.ShapeDtypeStruct((tokens, depth), jnp.float32), row, row],
        scratch_shapes=[pltpu.VMEM((tokens, depth), jnp.float32)],
        compiler_params=kernel_params(48),
        cost_estimate=cost(groups * tokens * depth * width, tokens * width),
        name="project_back",
    )(low, high, weight, x, scale, carry)


def store_pieces(total, own_core, place_of, keep_ref, send_ref):
    rows = keep_ref.shape[-2]
    pieces = total.shape[0] // rows
    low = total.astype(jnp.bfloat16).reshape(pieces // 2, 2, rows, total.shape[1])
    here = own_core == 0
    for slot in range(pieces // 2):
        first, second = low[slot, 0], low[slot, 1]
        keep_ref[place_of(slot)] = jnp.where(here, first, second)
        send_ref[place_of(slot)] = jnp.where(here, second, first)


def weight_grad_kernel(table, first, own_ref, x_ref, dx_ref, y_ref, dy_ref, keep_ref, send_ref, left):
    step = pl.program_id(0)

    def place_of(slot):
        return own_ref[1] ^ table[slot], 0

    if first:

        @pl.when(step == 0)
        def _():
            left[...] = x_ref[...].T

    @pl.when(step == first)
    def _():
        left[...] = y_ref[...].T

    right = jnp.where(step < first, dx_ref[...], dy_ref[0]) if first else dy_ref[0]
    store_pieces(dot_nn(left[...], right), own_ref[0], place_of, keep_ref, send_ref)


def weight_grad(own, x, dx, y, dy, table, rows, name):
    tokens, depth = y.shape
    first = 0 if dx is None else dx.shape[1] // COL_BLOCK
    groups = dy.shape[0]
    blocks = first + groups
    whole = pl.BlockSpec((tokens, depth), lambda i, own: (0, 0))
    block = pl.BlockSpec((len(table), 1, rows, COL_BLOCK), lambda i, own: (0, i, 0, 0))
    half = jax.ShapeDtypeStruct((len(table), blocks, rows, COL_BLOCK), jnp.bfloat16)
    if dx is None:
        x, dx = y, y
    return pl.pallas_call(
        partial(weight_grad_kernel, table, first),
        grid_spec=pltpu.PrefetchScalarGridSpec(
            num_scalar_prefetch=1,
            grid=(blocks,),
            in_specs=[
                whole,
                pl.BlockSpec(
                    (tokens, COL_BLOCK), lambda i, own: (0, jnp.clip(i, 0, max(first - 1, 0)))
                ),
                whole,
                pl.BlockSpec(
                    (1, tokens, COL_BLOCK), lambda i, own: (jnp.maximum(i - first, 0), 0, 0)
                ),
            ],
            out_specs=[block, block],
            scratch_shapes=[pltpu.VMEM((depth, tokens), jnp.bfloat16)],
        ),
        out_shape=[half, half],
        compiler_params=kernel_params(40),
        cost_estimate=cost(tokens * depth * blocks * COL_BLOCK, tokens * blocks * COL_BLOCK),
        name=name,
    )(own, x, dx, y, dy)


def place_units_kernel(own_ref, *refs):
    sources, (expand_ref, shrink_ref) = refs[:4], refs[4:]
    for flip, source in enumerate(sources):
        at = own_ref[0] ^ flip
        rows = expand_ref.shape[0] // 4
        place = pl.ds(pl.multiple_of(at * rows, rows), rows)
        width = source.shape[2]
        for block in range(expand_ref.shape[1] // width):
            piece = source[0, block * rows : (block + 1) * rows, :]
            expand_ref[place, block * width : (block + 1) * width] = piece.astype(jnp.float32)
        rows = source.shape[1]
        place = pl.ds(pl.multiple_of(at * rows, rows), rows)
        shrink_ref[place, :] = source[1].astype(jnp.float32)


def place_attention_kernel(own_ref, *refs):
    sources, (out_ref, proj_ref) = refs[:4], refs[4:]
    for flip, source in enumerate(sources):
        blocks, rows, width = source.shape
        place = pl.ds(pl.multiple_of((own_ref[0] ^ flip) * rows, rows), rows)
        for block in range(blocks):
            piece = source[block].astype(jnp.float32)
            if block < 2:
                out_ref[place, block * width : (block + 1) * width] = piece
            else:
                group, half = (block - 2) % 3, (block - 2) // 3
                start = (2 * group + half) * width
                proj_ref[place, start : start + width] = piece


def place_reps(kernel, rep_id, own, shapes, name):
    across = exchange(own, *MASKS["y"])
    parts = [own, exchange(own, *MASKS["core"]), across, exchange(across, *MASKS["core"])]
    return pl.pallas_call(
        kernel,
        grid_spec=pltpu.PrefetchScalarGridSpec(num_scalar_prefetch=1, grid=()),
        out_shape=[jax.ShapeDtypeStruct(shape, jnp.float32) for shape in shapes],
        compiler_params=kernel_params(32),
        cost_estimate=cost(2**20, 2**20),
        name=name,
    )(rep_id.astype(jnp.int32)[None], *parts)


def feed_forward_kernel(
    table,
    own_ref,
    norm_ref,
    grad_ref,
    expand_ref,
    bias_ref,
    shrink_ref,
    branch_ref,
    d_norm_ref,
    keep_e_ref,
    send_e_ref,
    keep_s_ref,
    send_s_ref,
    d_bias_ref,
    norm_t,
    hidden,
    d_pre,
):
    tokens, depth = norm_ref.shape
    units = hidden.shape[1]
    step = pl.program_id(0)
    expand = expand_ref[...].reshape(depth, units)
    shrink = shrink_ref[...].reshape(units, depth)

    @pl.when(step == 0)
    def _():
        norm_t[...] = norm_ref[...].T
        branch_ref[...] = jnp.zeros_like(branch_ref)
        d_norm_ref[...] = jnp.zeros_like(d_norm_ref)

    bias_sum = jnp.zeros((1, units), jnp.float32)
    starts = list(range(0, tokens, ROWS))

    def entering(start):
        rows = slice(start, start + ROWS)
        return dot_nn(norm_ref[rows, :], expand), dot_nt(grad_ref[rows, :], shrink)

    upcoming = entering(starts[0])
    for number, start in enumerate(starts):
        rows = slice(start, start + ROWS)
        pre, d_unit = upcoming
        if number + 1 < len(starts):
            upcoming = entering(starts[number + 1])
        pre = pre + bias_ref[...]
        square = pre * pre
        bend = jnp.tanh(GELU_ROOT * pre * (1.0 + GELU_CUBE * square))
        rise = 0.5 + 0.5 * bend
        unit = (pre * rise).astype(jnp.bfloat16)
        hidden[rows, :] = unit
        slope = rise + 0.5 * pre * (1.0 - bend * bend) * (
            GELU_ROOT + (3.0 * GELU_ROOT * GELU_CUBE) * square
        )
        d_low = (d_unit * slope).astype(jnp.bfloat16)
        d_pre[rows, :] = d_low
        bias_sum = bias_sum + jnp.sum(d_low.astype(jnp.float32), axis=0, keepdims=True)
        branch_ref[rows, :] += dot_nn(unit, shrink)
        d_norm_ref[rows, :] += dot_nt(d_low, expand)
    d_bias_ref[...] = bias_sum
    store_pieces(
        dot_tn(hidden[...], grad_ref[...]),
        own_ref[0],
        lambda slot: (0, own_ref[3] ^ slot, 0),
        keep_s_ref,
        send_s_ref,
    )
    store_pieces(
        dot_nn(norm_t[...], d_pre[...]),
        own_ref[0],
        lambda slot: (own_ref[1] ^ table[slot], 0),
        keep_e_ref,
        send_e_ref,
    )


def feed_forward(own, norm, grad, expand, bias, shrink, table):
    tokens, depth = norm.shape
    total = bias.shape[1]
    steps = total // FF_BLOCK
    slots = len(table)
    rows_e = depth // (2 * slots)
    per = depth // FF_BLOCK
    whole = pl.BlockSpec((tokens, depth), lambda i, own: (0, 0))
    half_e = pl.BlockSpec(
        (slots, 1, rows_e, FF_BLOCK), lambda i, own: (0, i // per, 0, i % per)
    )
    if slots > 1:
        spec_e = weight_spec(expand, 4, FF_BLOCK, lambda i, own: i)
        spec_s = pl.BlockSpec(
            (shrink.shape[0] // steps, 4) + shrink.shape[2:], lambda i, own: (i, 0, 0, 0)
        )
        shape_s = (2, 2, steps // 2, FF_BLOCK // 4, depth)
        half_s = pl.BlockSpec(
            (1, 2, 1, FF_BLOCK // 4, depth),
            lambda i, own: ((i & 1) ^ own[2], 0, ((i & 2) | (i >> 2)) ^ own[4], 0, 0),
        )
    else:
        spec_e = weight_spec(expand, 0, FF_BLOCK, lambda i, own: i)
        spec_s = pl.BlockSpec((FF_BLOCK, depth), lambda i, own: (i, 0))
        shape_s = (1, 1, steps, FF_BLOCK // 2, depth)
        half_s = pl.BlockSpec((1, 1, 1, FF_BLOCK // 2, depth), lambda i, own: (0, 0, i, 0, 0))
    line = pl.BlockSpec((1, FF_BLOCK), lambda i, own: (0, i))
    wide = jax.ShapeDtypeStruct((tokens, depth), jnp.float32)
    out_e = jax.ShapeDtypeStruct((slots, total // depth, rows_e, depth), jnp.bfloat16)
    out_s = jax.ShapeDtypeStruct(shape_s, jnp.bfloat16)
    return pl.pallas_call(
        partial(feed_forward_kernel, table),
        grid_spec=pltpu.PrefetchScalarGridSpec(
            num_scalar_prefetch=1,
            grid=(steps,),
            in_specs=[whole, whole, spec_e, line, spec_s],
            out_specs=[whole, whole, half_e, half_e, half_s, half_s, line],
            scratch_shapes=[
                pltpu.VMEM((depth, tokens), jnp.bfloat16),
                pltpu.VMEM((tokens, FF_BLOCK), jnp.bfloat16),
                pltpu.VMEM((tokens, FF_BLOCK), jnp.bfloat16),
            ],
        ),
        out_shape=[
            wide,
            wide,
            out_e,
            out_e,
            out_s,
            out_s,
            jax.ShapeDtypeStruct((1, total), jnp.float32),
        ],
        compiler_params=kernel_params(56),
        cost_estimate=cost(6 * tokens * depth * total, 16 * 2**20, tokens * total),
        name="feed_forward",
    )(own, norm, grad, expand, bias, shrink)


def attention_forward_kernel(q_ref, k_ref, v_ref, out_ref, out_t_ref, lse_ref):
    length = q_ref.shape[0]
    scaled = q_ref[...] * jnp.bfloat16(HEAD_DIM ** (-0.5))
    keys = k_ref[...]
    values_t = v_ref[...].T
    ones = jnp.ones((16, length), jnp.bfloat16)
    extended = [
        jnp.concatenate([values_t[head * HEAD_DIM : (head + 1) * HEAD_DIM], ones], axis=0)
        for head in range(2)
    ]
    tasks = [(start, head) for start in range(0, length, CHUNK) for head in range(2)]

    def scores_of(task):
        start, head = task
        cols = slice(head * HEAD_DIM, (head + 1) * HEAD_DIM)
        return dot_nt(keys[:, cols], scaled[start : start + CHUNK, cols])

    upcoming = scores_of(tasks[0])
    pieces = []
    for number, (start, head) in enumerate(tasks):
        scores = upcoming
        if number + 1 < len(tasks):
            upcoming = scores_of(tasks[number + 1])
        rows = slice(start, start + CHUNK)
        top = jnp.max(scores, axis=0, keepdims=True)
        terms = jnp.exp(scores - top).astype(jnp.bfloat16)
        part = dot_nn(extended[head], terms)
        total = part[HEAD_DIM : HEAD_DIM + 1]
        piece = part[:HEAD_DIM] / total
        lse_ref[0, head : head + 1, rows] = top + jnp.log(total)
        out_t_ref[head * HEAD_DIM : (head + 1) * HEAD_DIM, rows] = piece
        pieces.append(piece)
        if head == 1:
            out_ref[rows, :] = jnp.concatenate(pieces, axis=0).T.astype(jnp.bfloat16)
            pieces = []


def attention_forward(projected):
    length = projected.shape[0]
    pairs = HEADS // 2
    return pl.pallas_call(
        attention_forward_kernel,
        grid=(pairs,),
        in_specs=[
            pl.BlockSpec((length, PAIR), lambda i: (0, i)),
            pl.BlockSpec((length, PAIR), lambda i: (0, pairs + i)),
            pl.BlockSpec((length, PAIR), lambda i: (0, 2 * pairs + i)),
        ],
        out_specs=[
            pl.BlockSpec((length, PAIR), lambda i: (0, i)),
            pl.BlockSpec((PAIR, length), lambda i: (i, 0)),
            pl.BlockSpec((1, 2, length), lambda i: (i, 0, 0)),
        ],
        out_shape=[
            jax.ShapeDtypeStruct((length, HEADS * HEAD_DIM), jnp.bfloat16),
            jax.ShapeDtypeStruct((HEADS * HEAD_DIM, length), jnp.float32),
            jax.ShapeDtypeStruct((pairs, 2, length), jnp.float32),
        ],
        compiler_params=kernel_params(48),
        cost_estimate=cost(2**32, 8 * 2**20, 2**24),
        name="attention_forward",
    )(projected, projected, projected)


def attention_backward_kernel(q_ref, k_ref, v_ref, g_ref, o_ref, lse_ref, *refs):
    out_ref, qb_ref, vb_ref, probs, d_scores = refs[-5:]
    length = q_ref.shape[0]
    root = HEAD_DIM ** (-0.5)
    scaled = q_ref[...] * jnp.bfloat16(root)
    keys = k_ref[...]
    values = v_ref[...]
    grads = g_ref[...]
    keys_t = keys.T
    product = grads.T.astype(jnp.float32) * o_ref[...]
    sums_k = [None, None]
    sums_v = [None, None]
    sum_q = None
    pieces = []
    tasks = [(start, head) for start in range(0, length, CHUNK) for head in range(2)]
    for number, (start, head) in enumerate(tasks):
        rows = slice(start, start + CHUNK)
        slot = number % 2
        cols = slice(head * HEAD_DIM, (head + 1) * HEAD_DIM)
        query, grad = scaled[rows, cols], grads[rows, cols]
        lse = lse_ref[0, head : head + 1, rows]
        row_sum = jnp.sum(product[cols, rows], axis=0, keepdims=True)
        for block in range(0, length, KEY_BLOCK):
            some = slice(block, block + KEY_BLOCK)
            prob = jnp.exp(dot_nt(keys[some, cols], query) - lse)
            d_prob = dot_nt(values[some, cols], grad)
            probs[slot, some, :] = prob.astype(jnp.bfloat16)
            d_scores[slot, some, :] = (prob * (d_prob - row_sum)).astype(jnp.bfloat16)
        part_v = dot_nn(probs[slot], grad)
        part_k = dot_nn(d_scores[slot], query)
        sums_v[head] = part_v if start == 0 else sums_v[head] + part_v
        sums_k[head] = part_k if start == 0 else sums_k[head] + part_k
        pieces.append(dot_nn(keys_t[cols, :], d_scores[slot]) * root)
        if head == 1:
            d_query = jnp.concatenate(pieces, axis=0).T.astype(jnp.bfloat16)
            pieces = []
            out_ref[0, rows, :] = d_query
            part_q = jnp.sum(d_query.astype(jnp.float32), axis=0, keepdims=True)
            sum_q = part_q if start == 0 else sum_q + part_q
    out_ref[1] = jnp.concatenate(sums_k, axis=1).astype(jnp.bfloat16)
    d_value = jnp.concatenate(sums_v, axis=1).astype(jnp.bfloat16)
    out_ref[2] = d_value
    qb_ref[...] = sum_q
    vb_ref[...] = jnp.sum(d_value.astype(jnp.float32), axis=0, keepdims=True)


def attention_backward(operands, first, count, total, at, into, name):
    projected, d_attended, attended_t, lse = operands
    length = projected.shape[0]
    pairs = HEADS // 2
    row = pl.BlockSpec((1, PAIR), lambda i: (0, i))
    line = jax.ShapeDtypeStruct((1, count * PAIR), jnp.float32)
    in_specs = [
        pl.BlockSpec((length, PAIR), lambda i: (0, first + i)),
        pl.BlockSpec((length, PAIR), lambda i: (0, pairs + first + i)),
        pl.BlockSpec((length, PAIR), lambda i: (0, 2 * pairs + first + i)),
        pl.BlockSpec((length, PAIR), lambda i: (0, first + i)),
        pl.BlockSpec((PAIR, length), lambda i: (first + i, 0)),
        pl.BlockSpec((1, 2, length), lambda i: (first + i, 0, 0)),
    ]
    arrays = [projected, projected, projected, d_attended, attended_t, lse]
    aliases = {}
    if into is not None:
        in_specs.append(pl.BlockSpec(memory_space=pl.ANY))
        aliases = {len(arrays): 0}
        arrays.append(into)
    return pl.pallas_call(
        attention_backward_kernel,
        grid=(count,),
        in_specs=in_specs,
        out_specs=[pl.BlockSpec((3, length, PAIR), lambda i: (0, 0, at + i)), row, row],
        out_shape=[jax.ShapeDtypeStruct((3, length, total * PAIR), jnp.bfloat16), line, line],
        input_output_aliases=aliases,
        scratch_shapes=[
            pltpu.VMEM((2, length, CHUNK), jnp.bfloat16),
            pltpu.VMEM((2, length, CHUNK), jnp.bfloat16),
        ],
        compiler_params=kernel_params(48),
        cost_estimate=cost(count * 2**29, count * 2 * 2**20, count * 2**21),
        name=name,
    )(*arrays)


def normalize(values):
    average = jnp.mean(values, axis=-1, keepdims=True)
    centred = values - average
    variance = jnp.mean(centred * centred, axis=-1, keepdims=True)
    return centred * lax.rsqrt(variance + EPS_NORM)


def modulate(values, shifts, scales):
    return normalize(values) * (1.0 + scales[:, None, :]) + shifts[:, None, :]


MASKS = {"core": (1, 0), "y": (2, 0), "x": (0, 1), "z1": (0, 2), "z2": (0, 4)}
GATHER_ORDERS = (("z2", "z1", "x", "y"), ("z2", "z1", "y", "x"))


def exchange(value, rep_mask, fsdp_mask):
    reps, shards = lax.axis_size("rep"), lax.axis_size("fsdp")
    pairs = [
        (rep * shards + shard, (rep ^ rep_mask) * shards + (shard ^ fsdp_mask))
        for rep in range(reps)
        for shard in range(shards)
    ]
    return lax.ppermute(value, ("rep", "fsdp"), pairs)


def gather_relative(row, after_first):
    reps, shards = lax.axis_size("rep"), lax.axis_size("fsdp")
    masks = [(0, 1 << bit) for bit in reversed(range(shards.bit_length() - 1))]
    masks += [(1 << bit, 0) for bit in reversed(range(reps.bit_length() - 1))]
    rows = row[None]
    for number, pair in enumerate(masks):
        rows = jnp.concatenate([rows, exchange(rows, *pair)], axis=0)
        if number == 0:
            rows = after_first(rows)
    return rows


def gather_chain(quarter, order):
    rows = quarter[None]
    for name in order:
        rows = jnp.concatenate([rows, exchange(rows, *MASKS[name])], axis=0)
    return rows, exchange(rows, *MASKS["core"])


def chain_map(order):
    offsets = [0]
    for name in order:
        rep_mask, fsdp_mask = MASKS[name]
        offsets += [offset ^ (fsdp_mask * 4 + rep_mask) for offset in offsets]
    return tuple(offsets)


def to_absolute(parts, own):
    parts = list(parts)
    bit = 1
    while bit < len(parts):
        flipped = (own & bit) != 0
        parts = [jnp.where(flipped, parts[i ^ bit], parts[i]) for i in range(len(parts))]
        bit *= 2
    return parts


ORDERS = (("y", "x", "z1", "z2"), ("x", "y", "z1", "z2"))


def place_in(order, shard, y):
    bits = {"z2": (shard >> 2) & 1, "z1": (shard >> 1) & 1, "x": shard & 1, "y": y}
    place = 0
    for name in order:
        place = place * 2 + bits[name]
    return place


class HalvingSum:
    def __init__(self, halves, order):
        keep, send = halves
        self.masks = [MASKS[name] for name in order]
        self.stay = keep
        self.arrived = exchange(send, *MASKS["core"])

    def added(self, start, stop):
        stay, arrived = self.stay[start:stop], self.arrived[start:stop]
        return (stay.astype(jnp.float32) + arrived.astype(jnp.float32)).astype(jnp.bfloat16)

    def step(self):
        count = self.stay.shape[0]
        away = self.added(count // 2, count)
        self.stay = self.added(0, count // 2)
        self.arrived = exchange(away, *self.masks.pop(0))

    def finish(self):
        while self.masks:
            self.step()
        return self.added(0, 1)[0]


class PlainSum:
    def __init__(self, grad):
        self.arrived = grad

    def step(self):
        pass

    def finish(self):
        return scatter_rows(self.arrived)


def hold(value, *sums):
    held = lax.optimization_barrier((value, *[total.arrived for total in sums]))
    for total, arrived in zip(sums, held[1:]):
        total.arrived = arrived
    return held[0]


def scatter_rows(grad):
    own = lax.psum_scatter(grad, ("fsdp", "rep"), scatter_dimension=0, tiled=True)
    return lax.all_gather(own, "rep", axis=0, tiled=True).astype(jnp.float32)


def own_quarter(weight):
    part = weight.shape[0] // lax.axis_size("rep")
    return lax.dynamic_slice_in_dim(weight, lax.axis_index("rep") * part, part, 0)


def gather_rows(weight):
    return lax.all_gather(own_quarter(weight), ("fsdp", "rep"), axis=0, tiled=True)


def column_blocks(quarter, width):
    rows = quarter.shape[0]
    blocks = quarter.shape[1] // width
    return quarter.reshape(rows, blocks, width).transpose(1, 0, 2).reshape(blocks * rows, width)


def gather_packed(parts, rows):
    packed = jnp.concatenate(parts, axis=0)
    blocks, width = packed.shape[0] // rows, packed.shape[1]
    full = lax.all_gather(packed, ("fsdp", "rep"), axis=0, tiled=True)
    return full.reshape(full.shape[0] // packed.shape[0], blocks, rows, width)


def on_device(
    latents,
    conditions,
    modulator,
    modulbias,
    projector,
    querybias,
    valuebias,
    outweight,
    outbiases,
    expander,
    expandbias,
    shrinker,
    shrinkbias,
    upstream,
):
    seqs_dev, seq_len, feature = latents.shape
    token_count = seqs_dev * seq_len
    shard_id, rep_id = lax.axis_index("fsdp"), lax.axis_index("rep")
    shards, reps = lax.axis_size("fsdp"), lax.axis_size("rep")
    halving = shards == 8 and reps == 4
    own_rows = modulator.shape[0]
    own_bias = modulbias.shape[0]

    width = projector.shape[1]
    if halving:
        quarter = own_rows // reps
        proj_quarter = own_quarter(projector)
        chains = [
            gather_chain(proj_quarter[:, part * (width // 2) : (part + 1) * (width // 2)], order)
            for part, order in enumerate(GATHER_ORDERS)
        ]
        maps = [chain_map(order) for order in GATHER_ORDERS]
        packed = gather_packed(
            [
                own_quarter(shrinker),
                column_blocks(own_quarter(expander), feature),
                own_quarter(outweight),
            ],
            quarter,
        )
        out_at = (packed, 8)
        w_expand, w_shrink = packed, packed
        y_id = rep_id >> 1
        own = jnp.stack(
            [
                rep_id & 1,
                place_in(ORDERS[0], shard_id, y_id),
                shard_id & 1,
                y_id,
                (shard_id & 2) | (shard_id >> 2),
            ]
        ).astype(jnp.int32)
        table = tuple(place_in(ORDERS[0], slot >> 1, slot & 1) for slot in range(2 * shards))
        piece = quarter
    else:
        w_proj, out_at = gather_rows(projector), (gather_rows(outweight), 0)
        w_expand, w_shrink = gather_rows(expander), gather_rows(shrinker)
        own = jnp.zeros((5,), jnp.int32)
        table = (0,)
        piece = feature // 2

    def depth_sum(halves, order):
        if halving:
            return HalvingSum(halves, order)
        columns = [half[0].transpose(1, 0, 2).reshape(feature // 2, -1) for half in halves]
        return PlainSum(jnp.concatenate(columns, axis=0))

    def unit_sum(halves, order):
        if halving:
            return HalvingSum([half.reshape(16, -1, feature) for half in halves], order)
        blocks = [half.reshape(-1, 1, FF_BLOCK // 2, feature) for half in halves]
        return PlainSum(jnp.concatenate(blocks, axis=1).reshape(-1, feature))

    cond_full = conditions.astype(jnp.float32)
    cond_slice = lax.dynamic_slice_in_dim(cond_full, shard_id * own_rows, own_rows, 1)
    cond_act = jax.nn.silu(cond_slice).astype(jnp.bfloat16)
    cond_own = lax.dynamic_slice_in_dim(cond_full, shard_id * seqs_dev, seqs_dev, 0)
    cond_own = jax.nn.silu(cond_own).astype(jnp.bfloat16)
    mod_term = jnp.dot(cond_act, modulator, preferred_element_type=jnp.float32)
    bias_parts = (modulbias, querybias, valuebias, outbiases, expandbias, shrinkbias)
    own_biases = jnp.concatenate([part.astype(jnp.float32) for part in bias_parts])
    mod_width = seqs_dev * 6 * feature
    sent = jnp.concatenate(
        [
            mod_term.reshape(shards, mod_width),
            jnp.broadcast_to(own_biases[None, :], (shards, own_biases.shape[0])),
        ],
        axis=1,
    )
    got = lax.all_to_all(sent, "fsdp", split_axis=0, concat_axis=0, tiled=True)
    full_biases = []
    start = mod_width
    for part in bias_parts:
        full_biases.append(got[:, start : start + part.shape[0]].reshape(1, -1))
        start += part.shape[0]
    full_modbias, b_query, b_value, b_out, b_expand, b_shrink = full_biases
    modvals = jnp.sum(got[:, :mod_width], axis=0).reshape(seqs_dev, 6, feature)
    modvals = modvals + full_modbias.reshape(1, 6, feature)
    shift_a, scale_a, gate_a = (modvals[:, 0], modvals[:, 1], modvals[:, 2])
    shift_m, scale_m, gate_m = (modvals[:, 3], modvals[:, 4], modvals[:, 5])

    resid_in = latents.astype(jnp.float32)
    norm_a = modulate(resid_in, shift_a, scale_a).astype(jnp.bfloat16).reshape(token_count, feature)
    b_proj = jnp.concatenate([b_query, jnp.zeros_like(b_query), b_value], axis=1)
    if halving:
        flat = (shard_id * reps + rep_id).astype(jnp.int32)[None]
        projected, w_proj = project(flat, norm_a, b_proj, chains, maps)
    else:
        projected = forward_dot(norm_a, w_proj, 0, b_proj, jnp.bfloat16, "project")
    attended, attended_t, log_totals = attention_forward(projected)
    branch_a = forward_dot(attended, *out_at, b_out, jnp.float32, "attention_out")
    branch_a = branch_a.reshape(seqs_dev, seq_len, feature)
    middle = resid_in + gate_a[:, None, :] * branch_a
    norm_m = modulate(middle, shift_m, scale_m).astype(jnp.bfloat16).reshape(token_count, feature)

    grad_out = upstream.astype(jnp.float32)
    d_branch_m = (gate_m[:, None, :] * grad_out).astype(jnp.bfloat16).reshape(token_count, feature)
    g_shrinkbias = jnp.sum(d_branch_m, axis=0, dtype=jnp.float32)
    branch_m, d_norm_m, keep_e, send_e, keep_s, send_s, g_expandbias = feed_forward(
        own, norm_m, d_branch_m, w_expand, b_expand, w_shrink, table
    )
    sum_e = depth_sum((keep_e, send_e), ORDERS[0])
    sum_s = unit_sum((keep_s, send_s), ORDERS[1])
    flat_shape = (token_count, feature)
    lines = jnp.concatenate([b_shrink, gate_m, scale_m, gate_a, jnp.zeros((4, feature))], axis=0)
    layer_out, d_middle, d_branch_a, d_attended, row_sums = middle_back(
        branch_m,
        d_norm_m,
        middle.reshape(flat_shape),
        upstream.reshape(flat_shape),
        branch_a.reshape(flat_shape),
        lines,
        *out_at,
    )
    layer_out = layer_out.reshape(seqs_dev, seq_len, feature)
    d_gate_m, d_shift_m, d_scale_m, d_gate_a, g_outbiases = [row_sums[i] for i in range(5)]
    d_attended = hold(d_attended, sum_e, sum_s)
    sum_e.step()
    sum_s.step()
    half_pairs = HEADS // 4
    part_pairs = half_pairs // 2
    d_low, q_low, v_low = attention_backward(
        (projected, d_attended, attended_t, log_totals),
        0,
        half_pairs,
        half_pairs,
        0,
        None,
        "attention_backward_low",
    )
    halves_low = weight_grad(
        own, attended, d_branch_a, norm_a, d_low, table, piece, "weight_grad_low"
    )
    d_attended, halves_low = hold((d_attended, halves_low), sum_e, sum_s)
    sum_low = depth_sum(halves_low, ORDERS[0])
    for total in (sum_e, sum_s):
        total.step()
    d_high, *sums_mid = attention_backward(
        (projected, d_attended, attended_t, log_totals),
        half_pairs,
        part_pairs,
        half_pairs,
        0,
        None,
        "attention_backward_mid",
    )
    d_high = hold(d_high, sum_e, sum_s, sum_low)
    for total in (sum_e, sum_s, sum_low):
        total.step()
    d_high, *sums_high = attention_backward(
        (projected, d_attended, attended_t, log_totals),
        half_pairs + part_pairs,
        part_pairs,
        half_pairs,
        part_pairs,
        d_high,
        "attention_backward_high",
    )
    q_high, v_high = [jnp.concatenate(parts, axis=1) for parts in zip(sums_mid, sums_high)]
    halves_high = weight_grad(
        own, None, None, norm_a, d_high, table, piece, "weight_grad_high"
    )
    d_high, halves_high = hold((d_high, halves_high), sum_e, sum_s, sum_low)
    sum_high = depth_sum(halves_high, ORDERS[0])
    for total in (sum_e, sum_s, sum_low):
        total.step()
    d_high = hold(d_high, sum_high)
    sum_high.step()
    latents_grad, d_shift_a, d_scale_a = project_back(
        d_low,
        d_high,
        w_proj,
        latents.reshape(token_count, feature),
        scale_a,
        d_middle,
    )
    latents_grad = latents_grad.reshape(seqs_dev, seq_len, feature)
    g_querybias = jnp.concatenate([q_low, q_high], axis=1)
    g_valuebias = jnp.concatenate([v_low, v_high], axis=1)
    small = jnp.concatenate(
        [
            part.astype(jnp.float32).reshape(-1, 128)
            for part in (
                d_shift_a,
                d_scale_a,
                d_gate_a,
                d_shift_m,
                d_scale_m,
                d_gate_m,
                cond_own,
                g_querybias,
                g_valuebias,
                g_outbiases,
                g_expandbias,
                g_shrinkbias,
                jnp.zeros((feature,)),
            )
        ]
    ).astype(jnp.bfloat16)
    devices = reps * shards
    size = seqs_dev * feature

    def advance(rows):
        rows = hold(rows, sum_e, sum_s, sum_low, sum_high)
        for total in (sum_low, sum_high):
            total.step()
        return rows

    gathered = gather_relative(small, advance)
    if halving:
        done = jnp.stack([total.finish().reshape(-1, feature) for total in (sum_e, sum_s)])
        g_expander, g_shrinker = place_reps(
            place_units_kernel, rep_id, done, (expander.shape, shrinker.shape), "place_units"
        )
        done = jnp.concatenate([sum_low.finish(), sum_high.finish()], axis=0)
        g_outweight, g_projector = place_reps(
            place_attention_kernel, rep_id, done, (outweight.shape, projector.shape), "place_attention"
        )
    else:
        g_expander, g_shrinker = sum_e.finish(), sum_s.finish()
        low, high = sum_low.finish(), sum_high.finish()
        g_outweight = low[:, :feature]
        g_projector = jnp.stack(
            [low[:, feature:].reshape(own_rows, 3, -1), high.reshape(own_rows, 3, -1)], axis=2
        ).reshape(own_rows, 3 * feature)

    lines = size // 128
    cond_all = gathered[:, 6 * lines : 7 * lines].reshape(devices * seqs_dev, feature)
    cond_all = lax.dynamic_slice_in_dim(cond_all, shard_id * own_rows, own_rows, 1)
    d_mod = gathered[:, : 6 * lines].reshape(devices, 6, seqs_dev, feature).transpose(0, 2, 1, 3)
    d_mod = d_mod.reshape(devices * seqs_dev, 6 * feature)
    bias_sums = jnp.sum(gathered[:, 7 * lines :], axis=0, dtype=jnp.float32).reshape(-1)
    bias_grads = []
    start = 0
    for total in (feature, feature, feature, expandbias.shape[0] * shards, feature):
        part = total // shards
        bias_grads.append(lax.dynamic_slice_in_dim(bias_sums, start + shard_id * part, part, 0))
        start += total
    g_modbias = jnp.sum(
        lax.dynamic_slice_in_dim(d_mod, shard_id * own_bias, own_bias, 1), axis=0, dtype=jnp.float32
    )
    g_modulator = jnp.einsum("sr,sc->rc", cond_all, d_mod, preferred_element_type=jnp.float32)
    own_mod = d_mod[: shards * seqs_dev]
    d_cond_act = jnp.einsum("sc,rc->sr", own_mod, modulator, preferred_element_type=jnp.float32)
    d_cond_act = d_cond_act.reshape(shards, seqs_dev, own_rows)
    bits = shards.bit_length() - 1
    turned = [sum(((i >> bit) & 1) << (bits - 1 - bit) for bit in range(bits)) for i in range(shards)]
    d_cond_act = jnp.stack(to_absolute([d_cond_act[i] for i in turned], shard_id))
    d_cond_act = d_cond_act.reshape(shards * seqs_dev, own_rows)
    _, silu_pull = jax.vjp(jax.nn.silu, cond_slice)
    conditions_grad = silu_pull(d_cond_act)[0]
    return (
        layer_out,
        latents_grad,
        conditions_grad,
        g_modulator,
        g_modbias,
        g_projector,
        bias_grads[0],
        bias_grads[1],
        g_outweight,
        bias_grads[2],
        g_expander,
        bias_grads[3],
        g_shrinker,
        bias_grads[4],
    )


def solution(mesh):
    return jax.shard_map(
        on_device,
        mesh=mesh,
        in_specs=(
            P(("rep", "fsdp"), None, None),
            P("rep", None),
            P("fsdp", None),
            P("fsdp"),
            P("fsdp", None),
            P("fsdp"),
            P("fsdp"),
            P("fsdp", None),
            P("fsdp"),
            P("fsdp", None),
            P("fsdp"),
            P("fsdp", None),
            P("fsdp"),
            P(("rep", "fsdp"), None, None),
        ),
        out_specs=(
            P(("rep", "fsdp"), None, None),
            P(("rep", "fsdp"), None, None),
            P("rep", "fsdp"),
            P("fsdp", None),
            P("fsdp"),
            P("fsdp", None),
            P("fsdp"),
            P("fsdp"),
            P("fsdp", None),
            P("fsdp"),
            P("fsdp", None),
            P("fsdp"),
            P("fsdp", None),
            P("fsdp"),
        ),
        check_vma=False,
    )
```

```python
from functools import partial

import jax
import jax.numpy as jnp
from jax import lax
from jax.experimental import pallas as pl
from jax.experimental.pallas import tpu as pltpu
from jax.sharding import PartitionSpec as P

HEADS = 16
HEAD_DIM = 64
PAIR = 2 * HEAD_DIM
CHUNK = 256
KEY_BLOCK = 128
NORM_ROWS = 128
MIDDLE_ROWS = 256
EPS_NORM = 1e-06
ROWS = 512
FF_BLOCK = 512
COL_BLOCK = 512
GELU_ROOT = 0.7978845608028654
GELU_CUBE = 0.044715


def dot_nn(left, right):
    return jnp.dot(left, right, preferred_element_type=jnp.float32)


def dot_nt(left, right):
    return lax.dot_general(left, right, (((1,), (1,)), ((), ())), preferred_element_type=jnp.float32)


def dot_tn(left, right):
    return lax.dot_general(left, right, (((0,), (0,)), ((), ())), preferred_element_type=jnp.float32)


def kernel_params(mebibytes):
    return pltpu.CompilerParams(vmem_limit_bytes=mebibytes * 2**20)


def cost(flops, moved, special=0):
    return pl.CostEstimate(flops=flops, bytes_accessed=moved, transcendentals=special)


def weight_spec(weight, first, width, order):
    if weight.ndim == 2:
        offset = first * weight.shape[0] // width
        return pl.BlockSpec((weight.shape[0], width), lambda *at: (0, offset + order(*at)))
    devices, _, rows, columns = weight.shape
    per = columns // width
    return pl.BlockSpec(
        (devices, 1, rows, width),
        lambda *at: (0, first + order(*at) // per, 0, order(*at) % per),
    )


def forward_dot_kernel(x_ref, w_ref, b_ref, out_ref):
    weight = w_ref[...].reshape(x_ref.shape[1], out_ref.shape[1])
    out_ref[...] = (dot_nn(x_ref[...], weight) + b_ref[...]).astype(out_ref.dtype)


def forward_dot(x, weight, first, bias, dtype, name):
    tokens, depth = x.shape
    columns = bias.shape[1]
    return pl.pallas_call(
        forward_dot_kernel,
        grid=(columns // COL_BLOCK,),
        in_specs=[
            pl.BlockSpec((tokens, depth), lambda i: (0, 0)),
            weight_spec(weight, first, COL_BLOCK, lambda i: i),
            pl.BlockSpec((1, COL_BLOCK), lambda i: (0, i)),
        ],
        out_specs=pl.BlockSpec((tokens, COL_BLOCK), lambda i: (0, i)),
        out_shape=jax.ShapeDtypeStruct((tokens, columns), dtype),
        compiler_params=kernel_params(40),
        cost_estimate=cost(tokens * depth * columns, tokens * columns),
        name=name,
    )(x, weight, bias)


def project_kernel(maps, own_ref, x_ref, b_ref, *refs):
    sources, (out_ref, full_ref) = refs[:4], refs[4:]
    step = pl.program_id(0)
    rows = sources[0].shape[1]
    half = pl.num_programs(0) // 2
    for chain in range(2):

        @pl.when((step >= half) == (chain == 1))
        def _():
            for flip in range(2):
                source = sources[2 * chain + flip]
                for index, relative in enumerate(maps[chain]):
                    place = pl.multiple_of((own_ref[0] ^ (relative ^ flip)) * rows, rows)
                    full_ref[pl.ds(place, rows), :] = source[index]

    out_ref[...] = (dot_nn(x_ref[...], full_ref[...]) + b_ref[...]).astype(out_ref.dtype)


def project(flat, x, bias, chains, maps):
    tokens, depth = x.shape
    columns = bias.shape[1]
    steps = columns // COL_BLOCK
    half = steps // 2
    blocks, rows, _ = chains[0][0].shape
    first = pl.BlockSpec((blocks, rows, COL_BLOCK), lambda i, own: (0, 0, jnp.minimum(i, half - 1)))
    second = pl.BlockSpec((blocks, rows, COL_BLOCK), lambda i, own: (0, 0, jnp.maximum(i - half, 0)))
    return pl.pallas_call(
        partial(project_kernel, maps),
        grid_spec=pltpu.PrefetchScalarGridSpec(
            num_scalar_prefetch=1,
            grid=(steps,),
            in_specs=[
                pl.BlockSpec((tokens, depth), lambda i, own: (0, 0)),
                pl.BlockSpec((1, COL_BLOCK), lambda i, own: (0, i)),
                first,
                first,
                second,
                second,
            ],
            out_specs=[
                pl.BlockSpec((tokens, COL_BLOCK), lambda i, own: (0, i)),
                pl.BlockSpec((depth, COL_BLOCK), lambda i, own: (0, i)),
            ],
        ),
        out_shape=[
            jax.ShapeDtypeStruct((tokens, columns), jnp.bfloat16),
            jax.ShapeDtypeStruct((depth, columns), jnp.bfloat16),
        ],
        compiler_params=kernel_params(40),
        cost_estimate=cost(tokens * depth * columns, tokens * columns),
        name="project",
    )(flat, x, bias, *chains[0], *chains[1])


def middle_back_kernel(
    branch_ref,
    grad_ref,
    middle_ref,
    up_ref,
    branch_a_ref,
    lines_ref,
    w_ref,
    layer_ref,
    d_middle_ref,
    d_branch_ref,
    d_attended_ref,
    sums_ref,
):
    bias, gate_m, scale, gate_a = [lines_ref[i : i + 1, :] for i in range(4)]
    values = middle_ref[...]
    above = up_ref[...].astype(jnp.float32)
    branch = branch_ref[...] + bias
    layer_ref[...] = values + gate_m * branch
    centred = values - jnp.mean(values, axis=-1, keepdims=True)
    inverse = lax.rsqrt(jnp.mean(centred * centred, axis=-1, keepdims=True) + EPS_NORM)
    normal = centred * inverse
    grad = grad_ref[...]
    inner = grad * (1.0 + scale)
    average = jnp.mean(inner, axis=-1, keepdims=True)
    along = jnp.mean(inner * normal, axis=-1, keepdims=True)
    d_middle = above + inverse * (inner - average - normal * along)
    d_middle_ref[...] = d_middle
    d_branch = (gate_a * d_middle).astype(jnp.bfloat16)
    d_branch_ref[...] = d_branch
    weight = w_ref[...].reshape(d_attended_ref.shape[1], d_branch.shape[1])
    d_attended_ref[...] = dot_nt(d_branch, weight).astype(jnp.bfloat16)
    parts = (
        above * branch,
        grad,
        grad * normal,
        d_middle * branch_a_ref[...],
        d_branch.astype(jnp.float32),
    )
    sums = [jnp.sum(part, axis=0, keepdims=True) for part in parts]
    sums = jnp.concatenate(sums + [jnp.zeros((3, bias.shape[1]), jnp.float32)], axis=0)
    step = pl.program_id(0)

    @pl.when(step == 0)
    def _():
        sums_ref[...] = sums

    @pl.when(step > 0)
    def _():
        sums_ref[...] += sums


def middle_back(branch, grad, middle, above, branch_a, lines, weight, first):
    tokens, depth = middle.shape
    block = pl.BlockSpec((MIDDLE_ROWS, depth), lambda i: (i, 0))
    fixed = pl.BlockSpec((8, depth), lambda i: (0, 0))
    wide = jax.ShapeDtypeStruct((tokens, depth), jnp.float32)
    low = jax.ShapeDtypeStruct((tokens, depth), jnp.bfloat16)
    return pl.pallas_call(
        middle_back_kernel,
        grid=(tokens // MIDDLE_ROWS,),
        in_specs=[block] * 5 + [fixed, weight_spec(weight, first, depth, lambda i: 0)],
        out_specs=[block] * 4 + [fixed],
        out_shape=[wide, wide, low, low, jax.ShapeDtypeStruct((8, depth), jnp.float32)],
        compiler_params=kernel_params(48),
        cost_estimate=cost(tokens * depth * depth, 8 * tokens * depth),
        name="middle_back",
    )(branch, grad, middle, above, branch_a, lines, weight)


def project_back_kernel(
    low_ref, high_ref, w_ref, x_ref, scale_ref, carry_ref, out_ref, shift_sum_ref, scale_sum_ref, total
):
    step = pl.program_id(0)

    @pl.when(step == 0)
    def _():
        total[...] = dot_nt(low_ref[0], w_ref[...])

    @pl.when((step > 0) & (step % 2 == 0))
    def _():
        total[...] += dot_nt(low_ref[0], w_ref[...])

    @pl.when(step % 2 == 1)
    def _():
        total[...] += dot_nt(high_ref[0], w_ref[...])

    @pl.when(step == pl.num_programs(0) - 1)
    def _():
        gain = 1.0 + scale_ref[...]
        shift_sum = jnp.zeros(gain.shape, jnp.float32)
        scale_sum = jnp.zeros(gain.shape, jnp.float32)
        for start in range(0, x_ref.shape[0], NORM_ROWS):
            rows = slice(start, start + NORM_ROWS)
            values = x_ref[rows, :].astype(jnp.float32)
            centred = values - jnp.mean(values, axis=-1, keepdims=True)
            variance = jnp.mean(centred * centred, axis=-1, keepdims=True)
            inverse = lax.rsqrt(variance + EPS_NORM)
            normal = centred * inverse
            grad = total[rows, :]
            shift_sum += jnp.sum(grad, axis=0, keepdims=True)
            scale_sum += jnp.sum(grad * normal, axis=0, keepdims=True)
            inner = grad * gain
            average = jnp.mean(inner, axis=-1, keepdims=True)
            along = jnp.mean(inner * normal, axis=-1, keepdims=True)
            out_ref[rows, :] = carry_ref[rows, :] + inverse * (inner - average - normal * along)
        shift_sum_ref[...] = shift_sum
        scale_sum_ref[...] = scale_sum


def project_back(low, high, weight, x, scale, carry):
    groups, tokens, width = low.shape
    depth = weight.shape[0]
    block = pl.BlockSpec((1, tokens, width), lambda i: (i // 2, 0, 0))
    whole = pl.BlockSpec((tokens, depth), lambda i: (0, 0))
    line = pl.BlockSpec((1, depth), lambda i: (0, 0))
    row = jax.ShapeDtypeStruct((1, depth), jnp.float32)
    return pl.pallas_call(
        project_back_kernel,
        grid=(2 * groups,),
        in_specs=[
            block,
            block,
            pl.BlockSpec((depth, width), lambda i: (0, i)),
            whole,
            line,
            whole,
        ],
        out_specs=[whole, line, line],
        out_shape=[jax.ShapeDtypeStruct((tokens, depth), jnp.float32), row, row],
        scratch_shapes=[pltpu.VMEM((tokens, depth), jnp.float32)],
        compiler_params=kernel_params(48),
        cost_estimate=cost(groups * tokens * depth * width, tokens * width),
        name="project_back",
    )(low, high, weight, x, scale, carry)


def store_pieces(total, own_core, place_of, keep_ref, send_ref):
    rows = keep_ref.shape[-2]
    pieces = total.shape[0] // rows
    low = total.astype(jnp.bfloat16).reshape(pieces // 2, 2, rows, total.shape[1])
    here = own_core == 0
    for slot in range(pieces // 2):
        first, second = low[slot, 0], low[slot, 1]
        keep_ref[place_of(slot)] = jnp.where(here, first, second)
        send_ref[place_of(slot)] = jnp.where(here, second, first)


def weight_grad_kernel(table, first, own_ref, x_ref, dx_ref, y_ref, dy_ref, keep_ref, send_ref, left):
    step = pl.program_id(0)

    def place_of(slot):
        return own_ref[1] ^ table[slot], 0

    if first:

        @pl.when(step == 0)
        def _():
            left[...] = x_ref[...].T

    @pl.when(step == first)
    def _():
        left[...] = y_ref[...].T

    right = jnp.where(step < first, dx_ref[...], dy_ref[0]) if first else dy_ref[0]
    store_pieces(dot_nn(left[...], right), own_ref[0], place_of, keep_ref, send_ref)


def weight_grad(own, x, dx, y, dy, table, rows, name):
    tokens, depth = y.shape
    first = 0 if dx is None else dx.shape[1] // COL_BLOCK
    groups = dy.shape[0]
    blocks = first + groups
    whole = pl.BlockSpec((tokens, depth), lambda i, own: (0, 0))
    block = pl.BlockSpec((len(table), 1, rows, COL_BLOCK), lambda i, own: (0, i, 0, 0))
    half = jax.ShapeDtypeStruct((len(table), blocks, rows, COL_BLOCK), jnp.bfloat16)
    if dx is None:
        x, dx = y, y
    return pl.pallas_call(
        partial(weight_grad_kernel, table, first),
        grid_spec=pltpu.PrefetchScalarGridSpec(
            num_scalar_prefetch=1,
            grid=(blocks,),
            in_specs=[
                whole,
                pl.BlockSpec(
                    (tokens, COL_BLOCK), lambda i, own: (0, jnp.clip(i, 0, max(first - 1, 0)))
                ),
                whole,
                pl.BlockSpec(
                    (1, tokens, COL_BLOCK), lambda i, own: (jnp.maximum(i - first, 0), 0, 0)
                ),
            ],
            out_specs=[block, block],
            scratch_shapes=[pltpu.VMEM((depth, tokens), jnp.bfloat16)],
        ),
        out_shape=[half, half],
        compiler_params=kernel_params(40),
        cost_estimate=cost(tokens * depth * blocks * COL_BLOCK, tokens * blocks * COL_BLOCK),
        name=name,
    )(own, x, dx, y, dy)


def place_units_kernel(own_ref, *refs):
    sources, (expand_ref, shrink_ref) = refs[:4], refs[4:]
    for flip, source in enumerate(sources):
        at = own_ref[0] ^ flip
        rows = expand_ref.shape[0] // 4
        place = pl.ds(pl.multiple_of(at * rows, rows), rows)
        width = source.shape[2]
        for block in range(expand_ref.shape[1] // width):
            piece = source[0, block * rows : (block + 1) * rows, :]
            expand_ref[place, block * width : (block + 1) * width] = piece.astype(jnp.float32)
        rows = source.shape[1]
        place = pl.ds(pl.multiple_of(at * rows, rows), rows)
        shrink_ref[place, :] = source[1].astype(jnp.float32)


def place_attention_kernel(own_ref, *refs):
    sources, (out_ref, proj_ref) = refs[:4], refs[4:]
    for flip, source in enumerate(sources):
        blocks, rows, width = source.shape
        place = pl.ds(pl.multiple_of((own_ref[0] ^ flip) * rows, rows), rows)
        for block in range(blocks):
            piece = source[block].astype(jnp.float32)
            if block < 2:
                out_ref[place, block * width : (block + 1) * width] = piece
            else:
                group, half = (block - 2) % 3, (block - 2) // 3
                start = (2 * group + half) * width
                proj_ref[place, start : start + width] = piece


def place_reps(kernel, rep_id, own, shapes, name):
    across = exchange(own, *MASKS["y"])
    parts = [own, exchange(own, *MASKS["core"]), across, exchange(across, *MASKS["core"])]
    return pl.pallas_call(
        kernel,
        grid_spec=pltpu.PrefetchScalarGridSpec(num_scalar_prefetch=1, grid=()),
        out_shape=[jax.ShapeDtypeStruct(shape, jnp.float32) for shape in shapes],
        compiler_params=kernel_params(32),
        cost_estimate=cost(2**20, 2**20),
        name=name,
    )(rep_id.astype(jnp.int32)[None], *parts)


def feed_forward_kernel(
    table,
    own_ref,
    norm_ref,
    grad_ref,
    expand_ref,
    bias_ref,
    shrink_ref,
    branch_ref,
    d_norm_ref,
    keep_e_ref,
    send_e_ref,
    keep_s_ref,
    send_s_ref,
    d_bias_ref,
    norm_t,
    hidden,
    d_pre,
):
    tokens, depth = norm_ref.shape
    units = hidden.shape[1]
    step = pl.program_id(0)
    expand = expand_ref[...].reshape(depth, units)
    shrink = shrink_ref[...].reshape(units, depth)

    @pl.when(step == 0)
    def _():
        norm_t[...] = norm_ref[...].T
        branch_ref[...] = jnp.zeros_like(branch_ref)
        d_norm_ref[...] = jnp.zeros_like(d_norm_ref)

    bias_sum = jnp.zeros((1, units), jnp.float32)
    starts = list(range(0, tokens, ROWS))

    def entering(start):
        rows = slice(start, start + ROWS)
        return dot_nn(norm_ref[rows, :], expand), dot_nt(grad_ref[rows, :], shrink)

    upcoming = entering(starts[0])
    for number, start in enumerate(starts):
        rows = slice(start, start + ROWS)
        pre, d_unit = upcoming
        if number + 1 < len(starts):
            upcoming = entering(starts[number + 1])
        pre = pre + bias_ref[...]
        square = pre * pre
        bend = jnp.tanh(GELU_ROOT * pre * (1.0 + GELU_CUBE * square))
        rise = 0.5 + 0.5 * bend
        unit = (pre * rise).astype(jnp.bfloat16)
        hidden[rows, :] = unit
        slope = rise + 0.5 * pre * (1.0 - bend * bend) * (
            GELU_ROOT + (3.0 * GELU_ROOT * GELU_CUBE) * square
        )
        d_low = (d_unit * slope).astype(jnp.bfloat16)
        d_pre[rows, :] = d_low
        bias_sum = bias_sum + jnp.sum(d_low.astype(jnp.float32), axis=0, keepdims=True)
        branch_ref[rows, :] += dot_nn(unit, shrink)
        d_norm_ref[rows, :] += dot_nt(d_low, expand)
    d_bias_ref[...] = bias_sum
    store_pieces(
        dot_tn(hidden[...], grad_ref[...]),
        own_ref[0],
        lambda slot: (0, own_ref[3] ^ slot, 0),
        keep_s_ref,
        send_s_ref,
    )
    store_pieces(
        dot_nn(norm_t[...], d_pre[...]),
        own_ref[0],
        lambda slot: (own_ref[1] ^ table[slot], 0),
        keep_e_ref,
        send_e_ref,
    )


def feed_forward(own, norm, grad, expand, bias, shrink, table):
    tokens, depth = norm.shape
    total = bias.shape[1]
    steps = total // FF_BLOCK
    slots = len(table)
    rows_e = depth // (2 * slots)
    per = depth // FF_BLOCK
    whole = pl.BlockSpec((tokens, depth), lambda i, own: (0, 0))
    half_e = pl.BlockSpec(
        (slots, 1, rows_e, FF_BLOCK), lambda i, own: (0, i // per, 0, i % per)
    )
    if slots > 1:
        spec_e = weight_spec(expand, 4, FF_BLOCK, lambda i, own: i)
        spec_s = pl.BlockSpec(
            (shrink.shape[0] // steps, 4) + shrink.shape[2:], lambda i, own: (i, 0, 0, 0)
        )
        shape_s = (2, 2, steps // 2, FF_BLOCK // 4, depth)
        half_s = pl.BlockSpec(
            (1, 2, 1, FF_BLOCK // 4, depth),
            lambda i, own: ((i & 1) ^ own[2], 0, ((i & 2) | (i >> 2)) ^ own[4], 0, 0),
        )
    else:
        spec_e = weight_spec(expand, 0, FF_BLOCK, lambda i, own: i)
        spec_s = pl.BlockSpec((FF_BLOCK, depth), lambda i, own: (i, 0))
        shape_s = (1, 1, steps, FF_BLOCK // 2, depth)
        half_s = pl.BlockSpec((1, 1, 1, FF_BLOCK // 2, depth), lambda i, own: (0, 0, i, 0, 0))
    line = pl.BlockSpec((1, FF_BLOCK), lambda i, own: (0, i))
    wide = jax.ShapeDtypeStruct((tokens, depth), jnp.float32)
    out_e = jax.ShapeDtypeStruct((slots, total // depth, rows_e, depth), jnp.bfloat16)
    out_s = jax.ShapeDtypeStruct(shape_s, jnp.bfloat16)
    return pl.pallas_call(
        partial(feed_forward_kernel, table),
        grid_spec=pltpu.PrefetchScalarGridSpec(
            num_scalar_prefetch=1,
            grid=(steps,),
            in_specs=[whole, whole, spec_e, line, spec_s],
            out_specs=[whole, whole, half_e, half_e, half_s, half_s, line],
            scratch_shapes=[
                pltpu.VMEM((depth, tokens), jnp.bfloat16),
                pltpu.VMEM((tokens, FF_BLOCK), jnp.bfloat16),
                pltpu.VMEM((tokens, FF_BLOCK), jnp.bfloat16),
            ],
        ),
        out_shape=[
            wide,
            wide,
            out_e,
            out_e,
            out_s,
            out_s,
            jax.ShapeDtypeStruct((1, total), jnp.float32),
        ],
        compiler_params=kernel_params(56),
        cost_estimate=cost(6 * tokens * depth * total, 16 * 2**20, tokens * total),
        name="feed_forward",
    )(own, norm, grad, expand, bias, shrink)


def attention_forward_kernel(q_ref, k_ref, v_ref, out_ref, out_t_ref, lse_ref):
    length = q_ref.shape[0]
    scaled = q_ref[...] * jnp.bfloat16(HEAD_DIM ** (-0.5))
    keys = k_ref[...]
    values_t = v_ref[...].T
    ones = jnp.ones((16, length), jnp.bfloat16)
    extended = [
        jnp.concatenate([values_t[head * HEAD_DIM : (head + 1) * HEAD_DIM], ones], axis=0)
        for head in range(2)
    ]
    tasks = [(start, head) for start in range(0, length, CHUNK) for head in range(2)]

    def scores_of(task):
        start, head = task
        cols = slice(head * HEAD_DIM, (head + 1) * HEAD_DIM)
        return dot_nt(keys[:, cols], scaled[start : start + CHUNK, cols])

    upcoming = scores_of(tasks[0])
    pieces = []
    for number, (start, head) in enumerate(tasks):
        scores = upcoming
        if number + 1 < len(tasks):
            upcoming = scores_of(tasks[number + 1])
        rows = slice(start, start + CHUNK)
        top = jnp.max(scores, axis=0, keepdims=True)
        terms = jnp.exp(scores - top).astype(jnp.bfloat16)
        part = dot_nn(extended[head], terms)
        total = part[HEAD_DIM : HEAD_DIM + 1]
        piece = part[:HEAD_DIM] / total
        lse_ref[0, head : head + 1, rows] = top + jnp.log(total)
        out_t_ref[head * HEAD_DIM : (head + 1) * HEAD_DIM, rows] = piece
        pieces.append(piece)
        if head == 1:
            out_ref[rows, :] = jnp.concatenate(pieces, axis=0).T.astype(jnp.bfloat16)
            pieces = []


def attention_forward(projected):
    length = projected.shape[0]
    pairs = HEADS // 2
    return pl.pallas_call(
        attention_forward_kernel,
        grid=(pairs,),
        in_specs=[
            pl.BlockSpec((length, PAIR), lambda i: (0, i)),
            pl.BlockSpec((length, PAIR), lambda i: (0, pairs + i)),
            pl.BlockSpec((length, PAIR), lambda i: (0, 2 * pairs + i)),
        ],
        out_specs=[
            pl.BlockSpec((length, PAIR), lambda i: (0, i)),
            pl.BlockSpec((PAIR, length), lambda i: (i, 0)),
            pl.BlockSpec((1, 2, length), lambda i: (i, 0, 0)),
        ],
        out_shape=[
            jax.ShapeDtypeStruct((length, HEADS * HEAD_DIM), jnp.bfloat16),
            jax.ShapeDtypeStruct((HEADS * HEAD_DIM, length), jnp.float32),
            jax.ShapeDtypeStruct((pairs, 2, length), jnp.float32),
        ],
        compiler_params=kernel_params(48),
        cost_estimate=cost(2**32, 8 * 2**20, 2**24),
        name="attention_forward",
    )(projected, projected, projected)


def attention_backward_kernel(q_ref, k_ref, v_ref, g_ref, o_ref, lse_ref, *refs):
    out_ref, qb_ref, vb_ref, probs, d_scores = refs[-5:]
    length = q_ref.shape[0]
    root = HEAD_DIM ** (-0.5)
    scaled = q_ref[...] * jnp.bfloat16(root)
    keys = k_ref[...]
    values = v_ref[...]
    grads = g_ref[...]
    keys_t = keys.T
    product = grads.T.astype(jnp.float32) * o_ref[...]
    sums_k = [None, None]
    sums_v = [None, None]
    sum_q = None
    pieces = []
    tasks = [(start, head) for start in range(0, length, CHUNK) for head in range(2)]
    for number, (start, head) in enumerate(tasks):
        rows = slice(start, start + CHUNK)
        slot = number % 2
        cols = slice(head * HEAD_DIM, (head + 1) * HEAD_DIM)
        query, grad = scaled[rows, cols], grads[rows, cols]
        lse = lse_ref[0, head : head + 1, rows]
        row_sum = jnp.sum(product[cols, rows], axis=0, keepdims=True)
        for block in range(0, length, KEY_BLOCK):
            some = slice(block, block + KEY_BLOCK)
            prob = jnp.exp(dot_nt(keys[some, cols], query) - lse)
            d_prob = dot_nt(values[some, cols], grad)
            probs[slot, some, :] = prob.astype(jnp.bfloat16)
            d_scores[slot, some, :] = (prob * (d_prob - row_sum)).astype(jnp.bfloat16)
        part_v = dot_nn(probs[slot], grad)
        part_k = dot_nn(d_scores[slot], query)
        sums_v[head] = part_v if start == 0 else sums_v[head] + part_v
        sums_k[head] = part_k if start == 0 else sums_k[head] + part_k
        pieces.append(dot_nn(keys_t[cols, :], d_scores[slot]) * root)
        if head == 1:
            d_query = jnp.concatenate(pieces, axis=0).T.astype(jnp.bfloat16)
            pieces = []
            out_ref[0, rows, :] = d_query
            part_q = jnp.sum(d_query.astype(jnp.float32), axis=0, keepdims=True)
            sum_q = part_q if start == 0 else sum_q + part_q
    out_ref[1] = jnp.concatenate(sums_k, axis=1).astype(jnp.bfloat16)
    d_value = jnp.concatenate(sums_v, axis=1).astype(jnp.bfloat16)
    out_ref[2] = d_value
    qb_ref[...] = sum_q
    vb_ref[...] = jnp.sum(d_value.astype(jnp.float32), axis=0, keepdims=True)


def attention_backward(operands, first, count, total, at, into, name):
    projected, d_attended, attended_t, lse = operands
    length = projected.shape[0]
    pairs = HEADS // 2
    row = pl.BlockSpec((1, PAIR), lambda i: (0, i))
    line = jax.ShapeDtypeStruct((1, count * PAIR), jnp.float32)
    in_specs = [
        pl.BlockSpec((length, PAIR), lambda i: (0, first + i)),
        pl.BlockSpec((length, PAIR), lambda i: (0, pairs + first + i)),
        pl.BlockSpec((length, PAIR), lambda i: (0, 2 * pairs + first + i)),
        pl.BlockSpec((length, PAIR), lambda i: (0, first + i)),
        pl.BlockSpec((PAIR, length), lambda i: (first + i, 0)),
        pl.BlockSpec((1, 2, length), lambda i: (first + i, 0, 0)),
    ]
    arrays = [projected, projected, projected, d_attended, attended_t, lse]
    aliases = {}
    if into is not None:
        in_specs.append(pl.BlockSpec(memory_space=pl.ANY))
        aliases = {len(arrays): 0}
        arrays.append(into)
    return pl.pallas_call(
        attention_backward_kernel,
        grid=(count,),
        in_specs=in_specs,
        out_specs=[pl.BlockSpec((3, length, PAIR), lambda i: (0, 0, at + i)), row, row],
        out_shape=[jax.ShapeDtypeStruct((3, length, total * PAIR), jnp.bfloat16), line, line],
        input_output_aliases=aliases,
        scratch_shapes=[
            pltpu.VMEM((2, length, CHUNK), jnp.bfloat16),
            pltpu.VMEM((2, length, CHUNK), jnp.bfloat16),
        ],
        compiler_params=kernel_params(48),
        cost_estimate=cost(count * 2**29, count * 2 * 2**20, count * 2**21),
        name=name,
    )(*arrays)


def normalize(values):
    average = jnp.mean(values, axis=-1, keepdims=True)
    centred = values - average
    variance = jnp.mean(centred * centred, axis=-1, keepdims=True)
    return centred * lax.rsqrt(variance + EPS_NORM)


def modulate(values, shifts, scales):
    return normalize(values) * (1.0 + scales[:, None, :]) + shifts[:, None, :]


MASKS = {"core": (1, 0), "y": (2, 0), "x": (0, 1), "z1": (0, 2), "z2": (0, 4)}
GATHER_ORDERS = (("z2", "z1", "x", "y"), ("z2", "z1", "y", "x"))


def exchange(value, rep_mask, fsdp_mask):
    reps, shards = lax.axis_size("rep"), lax.axis_size("fsdp")
    pairs = [
        (rep * shards + shard, (rep ^ rep_mask) * shards + (shard ^ fsdp_mask))
        for rep in range(reps)
        for shard in range(shards)
    ]
    return lax.ppermute(value, ("rep", "fsdp"), pairs)


def gather_relative(row, after_first):
    reps, shards = lax.axis_size("rep"), lax.axis_size("fsdp")
    masks = [(0, 1 << bit) for bit in reversed(range(shards.bit_length() - 1))]
    masks += [(1 << bit, 0) for bit in reversed(range(reps.bit_length() - 1))]
    rows = row[None]
    for number, pair in enumerate(masks):
        rows = jnp.concatenate([rows, exchange(rows, *pair)], axis=0)
        if number == 0:
            rows = after_first(rows)
    return rows


def gather_chain(quarter, order):
    rows = quarter[None]
    for name in order:
        rows = jnp.concatenate([rows, exchange(rows, *MASKS[name])], axis=0)
    return rows, exchange(rows, *MASKS["core"])


def chain_map(order):
    offsets = [0]
    for name in order:
        rep_mask, fsdp_mask = MASKS[name]
        offsets += [offset ^ (fsdp_mask * 4 + rep_mask) for offset in offsets]
    return tuple(offsets)


def to_absolute(parts, own):
    parts = list(parts)
    bit = 1
    while bit < len(parts):
        flipped = (own & bit) != 0
        parts = [jnp.where(flipped, parts[i ^ bit], parts[i]) for i in range(len(parts))]
        bit *= 2
    return parts


ORDERS = (("y", "x", "z1", "z2"), ("x", "y", "z1", "z2"))


def place_in(order, shard, y):
    bits = {"z2": (shard >> 2) & 1, "z1": (shard >> 1) & 1, "x": shard & 1, "y": y}
    place = 0
    for name in order:
        place = place * 2 + bits[name]
    return place


class HalvingSum:
    def __init__(self, halves, order):
        keep, send = halves
        self.masks = [MASKS[name] for name in order]
        self.stay = keep
        self.arrived = exchange(send, *MASKS["core"])

    def added(self, start, stop):
        stay, arrived = self.stay[start:stop], self.arrived[start:stop]
        return (stay.astype(jnp.float32) + arrived.astype(jnp.float32)).astype(jnp.bfloat16)

    def step(self):
        count = self.stay.shape[0]
        away = self.added(count // 2, count)
        self.stay = self.added(0, count // 2)
        self.arrived = exchange(away, *self.masks.pop(0))

    def finish(self):
        while self.masks:
            self.step()
        return self.added(0, 1)[0]


class PlainSum:
    def __init__(self, grad):
        self.arrived = grad

    def step(self):
        pass

    def finish(self):
        return scatter_rows(self.arrived)


def hold(value, *sums):
    held = lax.optimization_barrier((value, *[total.arrived for total in sums]))
    for total, arrived in zip(sums, held[1:]):
        total.arrived = arrived
    return held[0]


def scatter_rows(grad):
    own = lax.psum_scatter(grad, ("fsdp", "rep"), scatter_dimension=0, tiled=True)
    return lax.all_gather(own, "rep", axis=0, tiled=True).astype(jnp.float32)


def own_quarter(weight):
    part = weight.shape[0] // lax.axis_size("rep")
    return lax.dynamic_slice_in_dim(weight, lax.axis_index("rep") * part, part, 0)


def gather_rows(weight):
    return lax.all_gather(own_quarter(weight), ("fsdp", "rep"), axis=0, tiled=True)


def column_blocks(quarter, width):
    rows = quarter.shape[0]
    blocks = quarter.shape[1] // width
    return quarter.reshape(rows, blocks, width).transpose(1, 0, 2).reshape(blocks * rows, width)


def gather_packed(parts, rows):
    packed = jnp.concatenate(parts, axis=0)
    blocks, width = packed.shape[0] // rows, packed.shape[1]
    full = lax.all_gather(packed, ("fsdp", "rep"), axis=0, tiled=True)
    return full.reshape(full.shape[0] // packed.shape[0], blocks, rows, width)


def on_device(
    latents,
    conditions,
    modulator,
    modulbias,
    projector,
    querybias,
    valuebias,
    outweight,
    outbiases,
    expander,
    expandbias,
    shrinker,
    shrinkbias,
    upstream,
):
    seqs_dev, seq_len, feature = latents.shape
    token_count = seqs_dev * seq_len
    shard_id, rep_id = lax.axis_index("fsdp"), lax.axis_index("rep")
    shards, reps = lax.axis_size("fsdp"), lax.axis_size("rep")
    halving = shards == 8 and reps == 4
    own_rows = modulator.shape[0]
    own_bias = modulbias.shape[0]

    width = projector.shape[1]
    if halving:
        quarter = own_rows // reps
        proj_quarter = own_quarter(projector)
        chains = [
            gather_chain(proj_quarter[:, part * (width // 2) : (part + 1) * (width // 2)], order)
            for part, order in enumerate(GATHER_ORDERS)
        ]
        maps = [chain_map(order) for order in GATHER_ORDERS]
        packed = gather_packed(
            [
                own_quarter(shrinker),
                column_blocks(own_quarter(expander), feature),
                own_quarter(outweight),
            ],
            quarter,
        )
        out_at = (packed, 8)
        w_expand, w_shrink = packed, packed
        y_id = rep_id >> 1
        own = jnp.stack(
            [
                rep_id & 1,
                place_in(ORDERS[0], shard_id, y_id),
                shard_id & 1,
                y_id,
                (shard_id & 2) | (shard_id >> 2),
            ]
        ).astype(jnp.int32)
        table = tuple(place_in(ORDERS[0], slot >> 1, slot & 1) for slot in range(2 * shards))
        piece = quarter
    else:
        w_proj, out_at = gather_rows(projector), (gather_rows(outweight), 0)
        w_expand, w_shrink = gather_rows(expander), gather_rows(shrinker)
        own = jnp.zeros((5,), jnp.int32)
        table = (0,)
        piece = feature // 2

    def depth_sum(halves, order):
        if halving:
            return HalvingSum(halves, order)
        columns = [half[0].transpose(1, 0, 2).reshape(feature // 2, -1) for half in halves]
        return PlainSum(jnp.concatenate(columns, axis=0))

    def unit_sum(halves, order):
        if halving:
            return HalvingSum([half.reshape(16, -1, feature) for half in halves], order)
        blocks = [half.reshape(-1, 1, FF_BLOCK // 2, feature) for half in halves]
        return PlainSum(jnp.concatenate(blocks, axis=1).reshape(-1, feature))

    cond_full = conditions.astype(jnp.float32)
    cond_slice = lax.dynamic_slice_in_dim(cond_full, shard_id * own_rows, own_rows, 1)
    cond_act = jax.nn.silu(cond_slice).astype(jnp.bfloat16)
    cond_own = lax.dynamic_slice_in_dim(cond_full, shard_id * seqs_dev, seqs_dev, 0)
    cond_own = jax.nn.silu(cond_own).astype(jnp.bfloat16)
    mod_term = jnp.dot(cond_act, modulator, preferred_element_type=jnp.float32)
    bias_parts = (modulbias, querybias, valuebias, outbiases, expandbias, shrinkbias)
    own_biases = jnp.concatenate([part.astype(jnp.float32) for part in bias_parts])
    mod_width = seqs_dev * 6 * feature
    sent = jnp.concatenate(
        [
            mod_term.reshape(shards, mod_width),
            jnp.broadcast_to(own_biases[None, :], (shards, own_biases.shape[0])),
        ],
        axis=1,
    )
    got = lax.all_to_all(sent, "fsdp", split_axis=0, concat_axis=0, tiled=True)
    full_biases = []
    start = mod_width
    for part in bias_parts:
        full_biases.append(got[:, start : start + part.shape[0]].reshape(1, -1))
        start += part.shape[0]
    full_modbias, b_query, b_value, b_out, b_expand, b_shrink = full_biases
    modvals = jnp.sum(got[:, :mod_width], axis=0).reshape(seqs_dev, 6, feature)
    modvals = modvals + full_modbias.reshape(1, 6, feature)
    shift_a, scale_a, gate_a = (modvals[:, 0], modvals[:, 1], modvals[:, 2])
    shift_m, scale_m, gate_m = (modvals[:, 3], modvals[:, 4], modvals[:, 5])

    resid_in = latents.astype(jnp.float32)
    norm_a = modulate(resid_in, shift_a, scale_a).astype(jnp.bfloat16).reshape(token_count, feature)
    b_proj = jnp.concatenate([b_query, jnp.zeros_like(b_query), b_value], axis=1)
    if halving:
        flat = (shard_id * reps + rep_id).astype(jnp.int32)[None]
        projected, w_proj = project(flat, norm_a, b_proj, chains, maps)
    else:
        projected = forward_dot(norm_a, w_proj, 0, b_proj, jnp.bfloat16, "project")
    attended, attended_t, log_totals = attention_forward(projected)
    branch_a = forward_dot(attended, *out_at, b_out, jnp.float32, "attention_out")
    branch_a = branch_a.reshape(seqs_dev, seq_len, feature)
    middle = resid_in + gate_a[:, None, :] * branch_a
    norm_m = modulate(middle, shift_m, scale_m).astype(jnp.bfloat16).reshape(token_count, feature)

    grad_out = upstream.astype(jnp.float32)
    d_branch_m = (gate_m[:, None, :] * grad_out).astype(jnp.bfloat16).reshape(token_count, feature)
    g_shrinkbias = jnp.sum(d_branch_m, axis=0, dtype=jnp.float32)
    branch_m, d_norm_m, keep_e, send_e, keep_s, send_s, g_expandbias = feed_forward(
        own, norm_m, d_branch_m, w_expand, b_expand, w_shrink, table
    )
    sum_e = depth_sum((keep_e, send_e), ORDERS[0])
    sum_s = unit_sum((keep_s, send_s), ORDERS[1])
    flat_shape = (token_count, feature)
    lines = jnp.concatenate([b_shrink, gate_m, scale_m, gate_a, jnp.zeros((4, feature))], axis=0)
    layer_out, d_middle, d_branch_a, d_attended, row_sums = middle_back(
        branch_m,
        d_norm_m,
        middle.reshape(flat_shape),
        upstream.reshape(flat_shape),
        branch_a.reshape(flat_shape),
        lines,
        *out_at,
    )
    layer_out = layer_out.reshape(seqs_dev, seq_len, feature)
    d_gate_m, d_shift_m, d_scale_m, d_gate_a, g_outbiases = [row_sums[i] for i in range(5)]
    d_attended = hold(d_attended, sum_e, sum_s)
    sum_e.step()
    sum_s.step()
    half_pairs = HEADS // 4
    part_pairs = half_pairs // 2
    d_low, q_low, v_low = attention_backward(
        (projected, d_attended, attended_t, log_totals),
        0,
        half_pairs,
        half_pairs,
        0,
        None,
        "attention_backward_low",
    )
    halves_low = weight_grad(
        own, attended, d_branch_a, norm_a, d_low, table, piece, "weight_grad_low"
    )
    d_high, *sums_mid = attention_backward(
        (projected, d_attended, attended_t, log_totals),
        half_pairs,
        part_pairs,
        half_pairs,
        0,
        None,
        "attention_backward_mid",
    )
    d_high, halves_low = hold((d_high, halves_low), sum_e, sum_s)
    sum_low = depth_sum(halves_low, ORDERS[0])
    for total in (sum_e, sum_s):
        total.step()
    d_high, *sums_high = attention_backward(
        (projected, d_attended, attended_t, log_totals),
        half_pairs + part_pairs,
        part_pairs,
        half_pairs,
        part_pairs,
        d_high,
        "attention_backward_high",
    )
    q_high, v_high = [jnp.concatenate(parts, axis=1) for parts in zip(sums_mid, sums_high)]
    halves_high = weight_grad(
        own, None, None, norm_a, d_high, table, piece, "weight_grad_high"
    )
    d_high, halves_high = hold((d_high, halves_high), sum_e, sum_s, sum_low)
    sum_high = depth_sum(halves_high, ORDERS[0])
    for total in (sum_e, sum_s, sum_low):
        total.step()
    d_high = hold(d_high, sum_high)
    sum_high.step()
    latents_grad, d_shift_a, d_scale_a = project_back(
        d_low,
        d_high,
        w_proj,
        latents.reshape(token_count, feature),
        scale_a,
        d_middle,
    )
    latents_grad = latents_grad.reshape(seqs_dev, seq_len, feature)
    g_querybias = jnp.concatenate([q_low, q_high], axis=1)
    g_valuebias = jnp.concatenate([v_low, v_high], axis=1)
    small = jnp.concatenate(
        [
            part.astype(jnp.float32).reshape(-1, 128)
            for part in (
                d_shift_a,
                d_scale_a,
                d_gate_a,
                d_shift_m,
                d_scale_m,
                d_gate_m,
                cond_own,
                g_querybias,
                g_valuebias,
                g_outbiases,
                g_expandbias,
                g_shrinkbias,
                jnp.zeros((feature,)),
            )
        ]
    ).astype(jnp.bfloat16)
    devices = reps * shards
    size = seqs_dev * feature

    def advance(rows):
        rows = hold(rows, sum_e, sum_s, sum_low, sum_high)
        for total in (sum_e, sum_s, sum_high, sum_low):
            total.step()
        return rows

    gathered = gather_relative(small, advance)
    if halving:
        done = jnp.stack([total.finish().reshape(-1, feature) for total in (sum_e, sum_s)])
        g_expander, g_shrinker = place_reps(
            place_units_kernel, rep_id, done, (expander.shape, shrinker.shape), "place_units"
        )
        done = jnp.concatenate([sum_low.finish(), sum_high.finish()], axis=0)
        g_outweight, g_projector = place_reps(
            place_attention_kernel, rep_id, done, (outweight.shape, projector.shape), "place_attention"
        )
    else:
        g_expander, g_shrinker = sum_e.finish(), sum_s.finish()
        low, high = sum_low.finish(), sum_high.finish()
        g_outweight = low[:, :feature]
        g_projector = jnp.stack(
            [low[:, feature:].reshape(own_rows, 3, -1), high.reshape(own_rows, 3, -1)], axis=2
        ).reshape(own_rows, 3 * feature)

    lines = size // 128
    cond_all = gathered[:, 6 * lines : 7 * lines].reshape(devices * seqs_dev, feature)
    cond_all = lax.dynamic_slice_in_dim(cond_all, shard_id * own_rows, own_rows, 1)
    d_mod = gathered[:, : 6 * lines].reshape(devices, 6, seqs_dev, feature).transpose(0, 2, 1, 3)
    d_mod = d_mod.reshape(devices * seqs_dev, 6 * feature)
    bias_sums = jnp.sum(gathered[:, 7 * lines :], axis=0, dtype=jnp.float32).reshape(-1)
    bias_grads = []
    start = 0
    for total in (feature, feature, feature, expandbias.shape[0] * shards, feature):
        part = total // shards
        bias_grads.append(lax.dynamic_slice_in_dim(bias_sums, start + shard_id * part, part, 0))
        start += total
    g_modbias = jnp.sum(
        lax.dynamic_slice_in_dim(d_mod, shard_id * own_bias, own_bias, 1), axis=0, dtype=jnp.float32
    )
    g_modulator = jnp.einsum("sr,sc->rc", cond_all, d_mod, preferred_element_type=jnp.float32)
    own_mod = d_mod[: shards * seqs_dev]
    d_cond_act = jnp.einsum("sc,rc->sr", own_mod, modulator, preferred_element_type=jnp.float32)
    d_cond_act = d_cond_act.reshape(shards, seqs_dev, own_rows)
    bits = shards.bit_length() - 1
    turned = [sum(((i >> bit) & 1) << (bits - 1 - bit) for bit in range(bits)) for i in range(shards)]
    d_cond_act = jnp.stack(to_absolute([d_cond_act[i] for i in turned], shard_id))
    d_cond_act = d_cond_act.reshape(shards * seqs_dev, own_rows)
    _, silu_pull = jax.vjp(jax.nn.silu, cond_slice)
    conditions_grad = silu_pull(d_cond_act)[0]
    return (
        layer_out,
        latents_grad,
        conditions_grad,
        g_modulator,
        g_modbias,
        g_projector,
        bias_grads[0],
        bias_grads[1],
        g_outweight,
        bias_grads[2],
        g_expander,
        bias_grads[3],
        g_shrinker,
        bias_grads[4],
    )


def solution(mesh):
    return jax.shard_map(
        on_device,
        mesh=mesh,
        in_specs=(
            P(("rep", "fsdp"), None, None),
            P("rep", None),
            P("fsdp", None),
            P("fsdp"),
            P("fsdp", None),
            P("fsdp"),
            P("fsdp"),
            P("fsdp", None),
            P("fsdp"),
            P("fsdp", None),
            P("fsdp"),
            P("fsdp", None),
            P("fsdp"),
            P(("rep", "fsdp"), None, None),
        ),
        out_specs=(
            P(("rep", "fsdp"), None, None),
            P(("rep", "fsdp"), None, None),
            P("rep", "fsdp"),
            P("fsdp", None),
            P("fsdp"),
            P("fsdp", None),
            P("fsdp"),
            P("fsdp"),
            P("fsdp", None),
            P("fsdp"),
            P("fsdp", None),
            P("fsdp"),
            P("fsdp", None),
            P("fsdp"),
        ),
        check_vma=False,
    )
```
